128 devices in a mesh: gz: 4 (over z), xy: 32 (over y, x, core).
Axes of the slice: x: 4, y: 4, z: 4, core: 2. Of those that a mesh axis runs over, the one named last changes fastest.
Arguments:
- features: bfloat16 [48, 16, 640, 256], P(None, 'gz', 'xy'), may hold values from -6 to 6
- first_weight: bfloat16 [3, 3, 3, 48, 48], replicated, may hold values from -0.15625 to 0.15625
- first_bias: float32 [48], replicated, may hold values from -0.5 to 0.5
- second_weight: bfloat16 [3, 3, 3, 64, 48], replicated, may hold values from -0.15625 to 0.15625
- second_bias: float32 [64], replicated, may hold values from -0.5 to 0.5
- labels: int32 [16, 640, 256], P('gz', 'xy'), may hold values from 0 to 16383, as said below
- blocks: int32 [4, 32, 256, 128], P('gz', 'xy'), may hold values from -1 to 20479, as said below
- owner_map: int32 [16384], replicated, may hold values from 0 to 16383, as said below
Outputs:
- mean_embedding: float32 [16384, 64], P(('gz', 'xy'))
- covariance: float32 [16384, 4096], P(('gz', 'xy'))
The draws below stay inside these ranges and needn't reach their ends.
Inputs may be any that keep to these rules, and one draw needn't show every extreme that they name: `labels`: all voxels listed in one block carry the same label. A tile's 256 blocks together list every voxel of the tile exactly once. A block lists a quarter of 128 to 128 voxels whose indices follow one another in ascending order, then -1 to its end. In each tile at most 6 blocks have rows owner_map[label] within one device's 128 output rows, and in every draw the rows of some devices receive exactly 6 blocks from every tile. `owner_map`: A permutation of the output rows.
All inputs are finite; a program needn't handle non-finite values.
Results may differ from the reference program's by a relative error of at most 0.0042.
Values may be sent and summed in bfloat16 or wider, within the bound.
A program may use at most 128 MiB of HBM per device.

```python
import jax
import jax.numpy as jnp
from jax import lax

IN_CH = 48
MID_CH = 48
EMB_CH = 64
X_LEN = 256
Z_DEV = 4
Y_DEV = 20
SV_DEV = 128
BLOCK_LEN = 128
Z_CELLS = 16
Y_CELLS = 640
OWNERS = 128
SEG_COUNT = 640
BLOCKS_DEV = 256
SLOT_CAP = 6
HEAVY_OWNERS = 16
SUPERVOXELS = 16384
N_GZ = 4
N_XY = 32


def layout(key):
    base = jax.random.fold_in(key, 4242)
    perm_key, heavy_key, offset_key, tiles_key = jax.random.split(base, 4)
    owner_map = jax.random.permutation(perm_key, SUPERVOXELS).astype(jnp.int32)
    inverse = jnp.zeros((SUPERVOXELS,), jnp.int32).at[owner_map].set(jnp.arange(SUPERVOXELS, dtype=jnp.int32))
    shuffled = jax.random.permutation(heavy_key, OWNERS).astype(jnp.int32)
    heavy_owners = shuffled[:HEAVY_OWNERS]
    light_owners = shuffled[HEAVY_OWNERS:]
    offsets = jax.random.randint(offset_key, (OWNERS,), 0, SV_DEV, dtype=jnp.int32)
    half_cap = SLOT_CAP // 2
    pool_size = (OWNERS - HEAVY_OWNERS) * half_cap
    seg_len = BLOCK_LEN // 4

    def one_tile(tile_key):
        pick_key, order_key, local_key, length_key = jax.random.split(tile_key, 4)
        heavy_part = jnp.repeat(heavy_owners, SLOT_CAP)
        picks = jax.random.permutation(pick_key, pool_size).astype(jnp.int32)[:BLOCKS_DEV - HEAVY_OWNERS * SLOT_CAP]
        light_part = light_owners[picks // half_cap]
        block_owner = jnp.concatenate([heavy_part, light_part])
        block_owner = block_owner[jax.random.permutation(order_key, BLOCKS_DEV).astype(jnp.int32)]
        local_draw = jax.random.randint(local_key, (BLOCKS_DEV,), 0, SV_DEV, dtype=jnp.int32)
        local_rows = (local_draw * local_draw // SV_DEV * local_draw // SV_DEV + offsets[block_owner]) % SV_DEV
        block_labels = inverse[block_owner * SV_DEV + local_rows]
        first_len = jax.random.randint(length_key, (BLOCKS_DEV // 2,), 1, 5, dtype=jnp.int32)
        lengths = jnp.stack([first_len, 5 - first_len], axis=1).reshape(BLOCKS_DEV)
        starts = jnp.cumsum(lengths) - lengths
        within = jnp.arange(BLOCK_LEN, dtype=jnp.int32)
        lists = jnp.where(within[None, :] < (lengths * seg_len)[:, None], starts[:, None] * seg_len + within[None, :], -1)
        run_marks = jnp.zeros((SEG_COUNT,), jnp.int32).at[starts].set(1)
        seg_block = jnp.cumsum(run_marks) - 1
        voxel_label = jnp.broadcast_to(block_labels[seg_block][:, None], (SEG_COUNT, seg_len)).reshape(Z_DEV, Y_DEV, X_LEN)
        return (voxel_label, lists.astype(jnp.int32))
    tile_keys = jax.random.split(tiles_key, OWNERS)
    tile_labels, tile_lists = jax.vmap(one_tile)(tile_keys)
    labels = tile_labels.reshape(N_GZ, N_XY, Z_DEV, Y_DEV, X_LEN).transpose(0, 2, 1, 3, 4).reshape(N_GZ * Z_DEV, N_XY * Y_DEV, X_LEN)
    lists = tile_lists.reshape(N_GZ, N_XY, BLOCKS_DEV, BLOCK_LEN)
    return (labels.astype(jnp.int32), lists, owner_map)


def draw_labels(key, part):
    return layout(key)[0]


def draw_blocks(key, part):
    return layout(key)[1]


def draw_owner_map(key, part):
    return layout(key)[2]


def steps_of(key, extent, cuts, least, top_value):
    factor_of, own = 1.0, jax.random.fold_in(key, 6)
    for position, blocks in cuts:
        heights = jnp.exp(jax.random.uniform(jax.random.fold_in(own, position), (blocks,), jnp.float32, least / len(cuts), top_value / len(cuts)))
        factor_of = factor_of * jnp.repeat(heights, extent[position] // blocks).reshape([-1 if axis == position else 1 for axis in range(len(extent))])
    return factor_of


def centred(stream_key, extent, deviation, most, shards=(), kind=jnp.bfloat16):
    array = jax.random.normal(stream_key, extent, jnp.float32) * deviation
    if len(shards) > 0:
        array = steps_of(stream_key, extent, shards, -0.22, 0.18) * array
    return jnp.clip(array, min=-most, max=most).astype(kind)


def setup_inputs(seed: int = 0) -> dict:
    streams_of = jax.random.split(jax.random.key(seed), 9)
    features = centred(streams_of[0], (IN_CH, Z_CELLS, Y_CELLS, X_LEN), 1.0, 6.0, ((1, 4), (2, 32)))
    first_weight = centred(streams_of[1], (3, 3, 3, MID_CH, IN_CH), (27 * IN_CH) ** -0.5, 0.15625)
    first_bias = jnp.clip(jax.random.uniform(streams_of[2], (MID_CH,), jnp.float32, -0.5, 0.5), -0.5, 0.5)
    second_weight = centred(streams_of[3], (3, 3, 3, EMB_CH, MID_CH), (27 * MID_CH) ** -0.5, 0.15625)
    second_bias = jnp.clip(jax.random.uniform(streams_of[4], (EMB_CH,), jnp.float32, -0.5, 0.5), -0.5, 0.5)
    labels = draw_labels(jax.random.fold_in(streams_of[8], 71), 0)
    blocks = draw_blocks(jax.random.fold_in(streams_of[8], 71), 0)
    owner_map = draw_owner_map(jax.random.fold_in(streams_of[8], 71), 0)
    return {"features": features, "first_weight": first_weight, "first_bias": first_bias, "second_weight": second_weight, "second_bias": second_bias, "labels": labels, "blocks": blocks, "owner_map": owner_map}


CONV_LAYOUT = ("NCDHW", "DHWOI", "NCDHW")


def convolve(volume, weight, bias):
    summed = lax.conv_general_dilated(volume[None], weight, (1, 1, 1), ((1, 1), (1, 1), (1, 1)), dimension_numbers=CONV_LAYOUT, preferred_element_type=jnp.float32)[0]
    return summed + bias[:, None, None, None]


def reference(features, first_weight, first_bias, second_weight, second_bias, labels, blocks, owner_map):
    hidden = jax.nn.relu(convolve(features, first_weight, first_bias)).astype(jnp.bfloat16)
    embedding = convolve(hidden, second_weight, second_bias).astype(jnp.bfloat16)
    tile_lists = blocks.reshape(N_GZ * N_XY, BLOCKS_DEV, BLOCK_LEN)

    def tile_step(totals, tile):
        depth = tile // N_XY
        plane = tile % N_XY
        anchor = jnp.zeros((), jnp.int32)
        piece = lax.dynamic_slice(embedding, (anchor, (depth * Z_DEV).astype(jnp.int32), (plane * Y_DEV).astype(jnp.int32), anchor), (EMB_CH, Z_DEV, Y_DEV, X_LEN)).reshape(EMB_CH, -1)
        tile_labels = lax.dynamic_slice(labels, ((depth * Z_DEV).astype(jnp.int32), (plane * Y_DEV).astype(jnp.int32), anchor), (Z_DEV, Y_DEV, X_LEN)).reshape(-1)
        voxel_lists = tile_lists[tile]
        in_block = voxel_lists >= 0
        picked = jnp.take(piece, jnp.where(in_block, voxel_lists, 0).reshape(-1), axis=1).reshape(EMB_CH, BLOCKS_DEV, BLOCK_LEN)
        picked = jnp.where(in_block[None], picked.astype(jnp.float32), jnp.zeros((), jnp.float32))
        block_sizes = jnp.sum(in_block.astype(jnp.float32), axis=1)
        block_sums = jnp.sum(picked, axis=2).T
        block_second = jnp.einsum("cnk,dnk->ncd", picked, picked).reshape(BLOCKS_DEV, EMB_CH * EMB_CH)
        owner_rows = owner_map[tile_labels[voxel_lists[:, 0]]]
        counts, sums, second = totals
        return (counts.at[owner_rows].add(block_sizes), sums.at[owner_rows].add(block_sums), second.at[owner_rows].add(block_second)), None

    start = (jnp.zeros((SUPERVOXELS,), jnp.float32), jnp.zeros((SUPERVOXELS, EMB_CH), jnp.float32), jnp.zeros((SUPERVOXELS, EMB_CH * EMB_CH), jnp.float32))
    totals = lax.scan(tile_step, start, jnp.arange(N_GZ * N_XY, dtype=jnp.int32))[0]
    counts, sums, second = totals
    denominator = jnp.maximum(counts, 1.0)
    mean_embedding = sums / denominator[:, None]
    covariance = second / denominator[:, None] - (mean_embedding[:, :, None] * mean_embedding[:, None, :]).reshape(SUPERVOXELS, EMB_CH * EMB_CH)
    return mean_embedding, covariance
```

```python
import functools

import jax
import jax.numpy as jnp
from jax import lax
from jax.experimental import pallas as pl
from jax.experimental.pallas import tpu as pltpu
from jax.sharding import PartitionSpec as P

SV_DEV = 128
EMB = 64
HALF = 32
SLOTS = 6
PAIRS = 3
BODY = PAIRS * HALF
ROWS = BODY + 16
DEVS = 128
GROUPS = 160
MESH = pl.DeviceIdType.MESH

CONV_LAYOUT = ("NCDHW", "DHWOI", "NCDHW")


def extended(array, sides, width):
    for axis, dim in sides:
        devices, length = (lax.axis_size(axis), array.shape[dim])
        up = [(i, (i + 1) % devices) for i in range(devices - 1)]
        down = [(j, i) for i, j in up]
        last = lax.slice_in_dim(array, length - width, length, axis=dim)
        leading = lax.slice_in_dim(array, 0, width, axis=dim)
        before = lax.ppermute(last, axis, up)
        after = lax.ppermute(leading, axis, down)
        array = jnp.concatenate([before, array, after], axis=dim)
    return array


def convolve(padded, weight, bias):
    summed = lax.conv_general_dilated(
        padded[None],
        weight,
        (1, 1, 1),
        ((0, 0), (0, 0), (1, 1)),
        dimension_numbers=CONV_LAYOUT,
        preferred_element_type=jnp.float32,
    )[0]
    return summed + bias[:, None, None, None]


def table_kernel(blocks_ref, labels_ref, owner_ref, table_ref, held, scalars, used, sem):
    lists = blocks_ref[...]
    sizes = jnp.sum(jnp.where(lists >= 0, 1, 0), axis=1, keepdims=True)
    lane = lax.broadcasted_iota(jnp.int32, lists.shape, 1)
    both = jnp.where(lane == 0, lists, sizes).astype(jnp.float32)
    held[...] = both.T[0:8, :].astype(jnp.int32)
    copy = pltpu.make_async_copy(held, scalars, sem)
    copy.start()

    def clear_used(d, carry):
        used[d] = 0
        return carry

    def clear_table(d, carry):
        table_ref[d] = 0
        return carry

    lax.fori_loop(0, DEVS, clear_used, 0, unroll=8)
    lax.fori_loop(0, DEVS * SLOTS, clear_table, 0, unroll=8)
    copy.wait()

    def step(b, carry):
        start = scalars[0, b]
        size = scalars[1, b]
        line = start >> 8
        z = line // 20
        row = owner_ref[labels_ref[z, line - z * 20, start & 255]]
        device = row >> 7
        rank = used[device]
        used[device] = rank + 1
        table_ref[device * SLOTS + rank] = (start << 15) + (size << 7) + (row & 127)
        return carry

    lax.fori_loop(0, lists.shape[0], step, 0, unroll=4)


def slot_table(blocks, labels, owner_map):
    count = blocks.shape[0]
    return pl.pallas_call(
        table_kernel,
        out_shape=jax.ShapeDtypeStruct((DEVS * SLOTS,), jnp.int32),
        in_specs=[
            pl.BlockSpec(memory_space=pltpu.VMEM),
            pl.BlockSpec(memory_space=pltpu.SMEM),
            pl.BlockSpec(memory_space=pltpu.SMEM),
        ],
        out_specs=pl.BlockSpec(memory_space=pltpu.SMEM),
        scratch_shapes=[
            pltpu.VMEM((8, count), jnp.int32),
            pltpu.SMEM((8, count), jnp.int32),
            pltpu.SMEM((DEVS,), jnp.int32),
            pltpu.SemaphoreType.DMA,
        ],
    )(blocks, labels, owner_map)


def place(device):
    return (device // 32, lax.rem(device, 32))


def partner(me, k):
    core, x, y, z = lax.rem(me, 2), lax.rem(me // 2, 4), lax.rem(me // 8, 4), me // 32
    kc, kx, ky, kz = lax.rem(k, 2), lax.rem(k // 2, 4), lax.rem(k // 8, 4), k // 32
    ky = lax.rem(ky + kx, 4)
    kz = lax.rem(kz + kx + ky, 4)
    there = (lax.rem(z + kz, 4) * 4 + lax.rem(y + ky, 4)) * 4 + lax.rem(x + kx, 4)
    return there * 2 + lax.rem(core + kc, 2)


def moments_of(emb_ref, table_ref, device, send_ref):
    lane = lax.broadcasted_iota(jnp.int32, (1, 128), 1)
    inner = lax.broadcasted_iota(jnp.int32, (HALF, 128), 1) & 63
    outer = lax.broadcasted_iota(jnp.int32, (HALF, 128), 0)
    upper = (inner >= HALF) | (inner >= outer)
    diagonal = inner == outer
    line = lax.broadcasted_iota(jnp.int32, (16, 128), 0)
    zero = jnp.zeros((EMB, 256), jnp.bfloat16)
    one = jnp.ones((EMB, 256), jnp.bfloat16)
    extras = jnp.zeros((16, 128), jnp.float32)
    for p in range(PAIRS):
        lefts, rights, masks, sizes, rows = [], [], [], [], []
        for h in range(2):
            code = table_ref[device * SLOTS + 2 * p + h]
            start = code >> 15
            size = (code >> 7) & 255
            rows.append((code & 127).astype(jnp.float32))
            sizes.append(size.astype(jnp.float32))
            group = start >> 7
            low = start & 127
            first = emb_ref[group]
            second = emb_ref[jnp.minimum(group + 1, GROUPS - 1)]
            in_first = jnp.where((lane >= low) & (lane < low + size), 1.0, 0.0).astype(jnp.bfloat16)
            in_second = jnp.where(lane + 128 < low + size, 1.0, 0.0).astype(jnp.bfloat16)
            lefts += [first * in_first, second * in_second]
            masks += [in_first, in_second]
            rights.append(jnp.concatenate([first, second], axis=1))
        mask_rows = jnp.broadcast_to(jnp.concatenate(masks, axis=1), (16, 512))
        left = jnp.concatenate([jnp.concatenate(lefts, axis=1), mask_rows], axis=0)
        right = jnp.concatenate(
            [
                jnp.concatenate([rights[0], zero], axis=1),
                jnp.concatenate([zero, rights[1]], axis=1),
                jnp.concatenate([one, zero], axis=1),
                jnp.concatenate([zero, one], axis=1),
            ],
            axis=0,
        )
        result = lax.dot_general(
            left, right, (((1,), (1,)), ((), ())), preferred_element_type=jnp.float32
        )
        size_row = jnp.where(lane < EMB, sizes[0], sizes[1])
        owner_row = jnp.where(lane < EMB, rows[0], rows[1])
        mean = result[EMB : EMB + 1, 0:128] / jnp.maximum(size_row, 1.0)
        centred = result[0:EMB, 0:128] - result[0:EMB, 128:256] * mean
        rolled = pltpu.roll(centred[HALF:EMB], 96, 1)
        packed = jnp.where(upper, centred[0:HALF], rolled)
        send_ref[device, p * HALF : (p + 1) * HALF, :] = packed.astype(jnp.bfloat16)
        diag = jnp.sum(jnp.where(diagonal, rolled, 0.0), axis=0, keepdims=True)
        high = mean.astype(jnp.bfloat16).astype(jnp.float32)
        for place_of, value in (
            (p, diag),
            (3 + p, high),
            (6 + p, mean - high),
            (9 + p, size_row),
            (12 + p, owner_row),
        ):
            extras = jnp.where(line == place_of, value, extras)
    send_ref[device, BODY:ROWS, :] = extras.astype(jnp.bfloat16)


def exchange_kernel(emb_ref, table_ref, got_ref, send_ref, send_sem, recv_sem, own_sem):
    me = lax.axis_index("gz") * 32 + lax.axis_index("xy")
    barrier = pltpu.get_barrier_semaphore()

    def greet(k, carry):
        pl.semaphore_signal(
            barrier, inc=1, device_id=place(partner(me, k)), device_id_type=MESH
        )
        return carry

    lax.fori_loop(1, DEVS, greet, 0)
    moments_of(emb_ref, table_ref, me, send_ref)
    own = pltpu.make_async_copy(send_ref.at[me], got_ref.at[me], own_sem)
    own.start()
    pl.semaphore_wait(barrier, DEVS - 1)

    def copy(k):
        device = partner(me, k)
        return pltpu.make_async_remote_copy(
            src_ref=send_ref.at[device],
            dst_ref=got_ref.at[me],
            send_sem=send_sem.at[k],
            recv_sem=recv_sem.at[k],
            device_id=place(device),
            device_id_type=MESH,
        )

    def send(k, carry):
        moments_of(emb_ref, table_ref, partner(me, k), send_ref)
        copy(k).start()
        return carry

    lax.fori_loop(1, DEVS, send, 0)

    def finish(k, carry):
        copy(k).wait()
        return carry

    lax.fori_loop(1, DEVS, finish, 0)
    own.wait()


def exchange(embedding, table):
    return pl.pallas_call(
        exchange_kernel,
        out_shape=jax.ShapeDtypeStruct((DEVS, ROWS, 128), jnp.bfloat16),
        in_specs=[
            pl.BlockSpec(memory_space=pltpu.VMEM),
            pl.BlockSpec(memory_space=pltpu.SMEM),
        ],
        out_specs=pl.BlockSpec(memory_space=pl.ANY),
        scratch_shapes=[
            pltpu.VMEM((DEVS, ROWS, 128), jnp.bfloat16),
            pltpu.SemaphoreType.DMA((DEVS,)),
            pltpu.SemaphoreType.DMA((DEVS,)),
            pltpu.SemaphoreType.DMA,
        ],
        compiler_params=pltpu.CompilerParams(
            collective_id=0, has_side_effects=True, vmem_limit_bytes=40 << 20
        ),
    )(embedding, table)


CHUNKS = 4
QUAD = 4


def total_kernel(
    got_ref, mean_ref, cov_ref, body, extra, lines, acc_a, acc_b, id_vec, ids, hits, spread,
    second, full, body_sem, extra_sem, id_sem,
):
    fast = lax.Precision.HIGHEST
    per = DEVS // CHUNKS
    extra_copy = pltpu.make_async_copy(got_ref.at[:, pl.ds(BODY, 16), :], extra, extra_sem)
    extra_copy.start()
    body_copies = [
        pltpu.make_async_copy(
            got_ref.at[pl.ds(c * per, per), pl.ds(0, BODY), :],
            body.at[pl.ds(c * per, per)],
            body_sem.at[c],
        )
        for c in range(CHUNKS)
    ]
    for one in body_copies:
        one.start()
    acc_a[...] = jnp.zeros_like(acc_a)
    acc_b[...] = jnp.zeros_like(acc_b)
    extra_copy.wait()
    lines[...] = extra[...].astype(jnp.float32).reshape(DEVS * 16, 128)

    def line(k):
        return lines[pl.ds(k, DEVS, stride=16), :]

    lane = lax.broadcasted_iota(jnp.int32, (DEVS, 128), 1)
    row = lax.broadcasted_iota(jnp.int32, (DEVS, 128), 0)
    inner = lane & 63
    owners = [line(12 + p) for p in range(PAIRS)]
    id_vec[...] = jnp.where(
        inner == 0, owners[0], jnp.where(inner == 1, owners[1], owners[2])
    ).astype(jnp.int32)
    id_copy = pltpu.make_async_copy(id_vec, ids, id_sem)
    id_copy.start()

    means, sizes = [], []
    sums = jnp.zeros((DEVS, 384), jnp.float32)
    for p in range(PAIRS):
        mean = line(3 + p) + line(6 + p)
        size = line(9 + p)
        means.append(mean)
        sizes.append(size)
        turned = owners[p].T
        for h in range(2):
            hit = jnp.where(row == turned[64 * h : 64 * h + 1, :].astype(jnp.int32), 1.0, 0.0)
            hits[:, (2 * p + h) * 128 : (2 * p + h + 1) * 128] = hit
            mine = (lane >= EMB) if h else (lane < EMB)
            values = jnp.concatenate(
                [
                    jnp.where(mine, size * mean, 0.0),
                    jnp.where(mine, size, 0.0),
                    jnp.where(mine, line(p), 0.0),
                ],
                axis=1,
            )
            sums = sums + jnp.dot(
                hit, values, preferred_element_type=jnp.float32, precision=fast
            )

    def folded(value):
        return value + pltpu.roll(value, EMB, 1)

    count = jnp.maximum(folded(sums[:, 128:256]), 1.0)
    total_mean = folded(sums[:, 0:128]) / count
    mean_ref[...] = total_mean[:, 0:EMB]
    diag_sum = folded(sums[:, 256:384])
    inverse = 1.0 / count
    lines[0:DEVS, :] = diag_sum
    lines[DEVS : 2 * DEVS, :] = inverse

    for p in range(PAIRS):
        for h in range(2):
            owner = owners[p]
            other = pltpu.roll(owner, EMB, 1)
            owner_all = (
                jnp.where(lane < EMB, other, owner) if h else jnp.where(lane < EMB, owner, other)
            )
            hit_t = jnp.where(owner_all.astype(jnp.int32) == lane, 1.0, 0.0)
            theirs = jnp.dot(
                hit_t, total_mean, preferred_element_type=jnp.float32, precision=fast
            )
            off = jnp.sqrt(sizes[p]) * (means[p] - theirs)
            if h:
                off = pltpu.roll(off, EMB, 1)
            off = jnp.where(lane < EMB, off, 0.0)
            k = 2 * p + h
            second[k * 128 : (k + 1) * 128, :] = off.astype(jnp.bfloat16)
            spread[:, k * 128 : (k + 1) * 128] = off.T[0:EMB, :].astype(jnp.bfloat16)

    id_copy.wait()
    for c in range(CHUNKS):
        body_copies[c].wait()

        def add(s, carry):
            for p in range(PAIRS):
                value = body[s, p * HALF : (p + 1) * HALF, :].astype(jnp.float32)
                a = ids[s, p]
                b = ids[s, 64 + p]
                acc_a[a] = acc_a[a] + value
                acc_b[b] = acc_b[b] + value
            return carry

        lax.fori_loop(c * per, (c + 1) * per, add, 0, unroll=2)

    lane32 = lax.broadcasted_iota(jnp.int32, (HALF, 128), 1)
    row32 = lax.broadcasted_iota(jnp.int32, (HALF, 128), 0)

    def quad(q, carry):
        base = q * QUAD
        left = []
        for t in range(QUAD):
            mask = hits[pl.ds(base + t, 1), :].astype(jnp.bfloat16)
            left.append(spread[...] * mask)
        between = jnp.dot(
            jnp.concatenate(left, axis=0), second[...], preferred_element_type=jnp.float32
        )
        packed = [
            acc_a[base + t] + pltpu.roll(acc_b[base + t], EMB, 1) for t in range(QUAD)
        ]
        turned = jnp.concatenate(packed, axis=0).T
        for t in range(QUAD):
            diag = lines[pl.ds(base + t, 1), :]
            inv = lines[pl.ds(DEVS + base + t, 1), :]
            flip = pltpu.roll(turned, (128 - HALF * t) % 128, 1) if t else turned
            flip_up, flip_down = flip[0:HALF], flip[HALF:EMB]
            here = packed[t]
            top = jnp.where((lane32 >= HALF) | (lane32 >= row32), here, flip_up)
            low = jnp.where(
                lane32 < row32, here, jnp.where(lane32 == row32, diag, flip_up)
            )
            bottom = jnp.where(lane32 < HALF, flip_down, pltpu.roll(low, HALF, 1))
            both = jnp.concatenate([top, bottom], axis=0)
            both = (both + between[t * EMB : (t + 1) * EMB]) * inv
            full[pl.ds((base + t) * EMB, EMB), :] = both
        return carry

    lax.fori_loop(0, SV_DEV // QUAD, quad, 0)

    for t in range(EMB // 2):
        even = full[pl.ds(2 * t, SV_DEV, stride=EMB), :]
        odd = full[pl.ds(2 * t + 1, SV_DEV, stride=EMB), :]
        cov_ref[:, t * 128 : (t + 1) * 128] = jnp.where(
            lane < EMB, even, pltpu.roll(odd, EMB, 1)
        )


def totals(got):
    return pl.pallas_call(
        total_kernel,
        out_shape=(
            jax.ShapeDtypeStruct((SV_DEV, EMB), jnp.float32),
            jax.ShapeDtypeStruct((SV_DEV, EMB * EMB), jnp.float32),
        ),
        in_specs=[pl.BlockSpec(memory_space=pl.ANY)],
        out_specs=(
            pl.BlockSpec(memory_space=pltpu.VMEM),
            pl.BlockSpec(memory_space=pltpu.VMEM),
        ),
        scratch_shapes=[
            pltpu.VMEM((DEVS, BODY, 128), jnp.bfloat16),
            pltpu.VMEM((DEVS, 16, 128), jnp.bfloat16),
            pltpu.VMEM((DEVS * 16, 128), jnp.float32),
            pltpu.VMEM((SV_DEV, HALF, 128), jnp.float32),
            pltpu.VMEM((SV_DEV, HALF, 128), jnp.float32),
            pltpu.VMEM((DEVS, 128), jnp.int32),
            pltpu.SMEM((DEVS, 128), jnp.int32),
            pltpu.VMEM((SV_DEV, DEVS * SLOTS), jnp.float32),
            pltpu.VMEM((EMB, DEVS * SLOTS), jnp.bfloat16),
            pltpu.VMEM((DEVS * SLOTS, 128), jnp.bfloat16),
            pltpu.VMEM((SV_DEV * EMB, 128), jnp.float32),
            pltpu.SemaphoreType.DMA((CHUNKS,)),
            pltpu.SemaphoreType.DMA,
            pltpu.SemaphoreType.DMA,
        ],
        compiler_params=pltpu.CompilerParams(vmem_limit_bytes=48 << 20),
    )(got)


def local(
    features, first_weight, first_bias, second_weight, second_bias, labels, blocks, owner_map
):
    table = slot_table(blocks.reshape(blocks.shape[2], blocks.shape[3]), labels, owner_map)
    padded = extended(features, (("gz", 1), ("xy", 2)), 1)
    hidden = jax.nn.relu(convolve(padded, first_weight, first_bias)).astype(jnp.bfloat16)
    hidden_pad = extended(hidden, (("gz", 1), ("xy", 2)), 1)
    embedding = convolve(hidden_pad, second_weight, second_bias).astype(jnp.bfloat16)
    grouped = embedding.reshape(EMB, GROUPS, 128).transpose(1, 0, 2)
    return totals(exchange(grouped, table))


def solution(mesh):
    return jax.shard_map(
        local,
        mesh=mesh,
        in_specs=(
            P(None, "gz", "xy", None),
            P(),
            P(),
            P(),
            P(),
            P("gz", "xy", None),
            P("gz", "xy", None, None),
            P(),
        ),
        out_specs=(P(("gz", "xy"), None), P(("gz", "xy"), None)),
        check_vma=False,
    )
```

```python
import functools

import jax
import jax.numpy as jnp
from jax import lax
from jax.experimental import pallas as pl
from jax.experimental.pallas import tpu as pltpu
from jax.sharding import PartitionSpec as P

SV_DEV = 128
EMB = 64
HALF = 32
SLOTS = 6
PAIRS = 3
BODY = PAIRS * HALF
ROWS = BODY + 16
DEVS = 128
GROUPS = 160
AHEAD = 4
MESH = pl.DeviceIdType.MESH


def table_kernel(blocks_ref, labels_ref, owner_ref, table_ref, held, scalars, used, sem):
    lists = blocks_ref[...]
    sizes = jnp.sum(jnp.where(lists >= 0, 1, 0), axis=1, keepdims=True)
    lane = lax.broadcasted_iota(jnp.int32, lists.shape, 1)
    both = jnp.where(lane == 0, lists, sizes).astype(jnp.float32)
    held[...] = both.T[0:8, :].astype(jnp.int32)
    copy = pltpu.make_async_copy(held, scalars, sem)
    copy.start()

    def clear_used(d, carry):
        used[d] = 0
        return carry

    def clear_table(d, carry):
        table_ref[d] = 0
        return carry

    lax.fori_loop(0, DEVS, clear_used, 0, unroll=8)
    lax.fori_loop(0, DEVS * SLOTS, clear_table, 0, unroll=8)
    copy.wait()

    def step(b, carry):
        start = scalars[0, b]
        size = scalars[1, b]
        line = start >> 8
        z = line // 20
        row = owner_ref[labels_ref[z, line - z * 20, start & 255]]
        device = row >> 7
        rank = used[device]
        used[device] = rank + 1
        table_ref[device * SLOTS + rank] = (start << 15) + (size << 7) + (row & 127)
        return carry

    lax.fori_loop(0, lists.shape[0], step, 0, unroll=4)


def slot_table(blocks, labels, owner_map):
    count = blocks.shape[0]
    return pl.pallas_call(
        table_kernel,
        out_shape=jax.ShapeDtypeStruct((DEVS * SLOTS,), jnp.int32),
        in_specs=[
            pl.BlockSpec(memory_space=pltpu.VMEM),
            pl.BlockSpec(memory_space=pltpu.SMEM),
            pl.BlockSpec(memory_space=pltpu.SMEM),
        ],
        out_specs=pl.BlockSpec(memory_space=pltpu.SMEM),
        scratch_shapes=[
            pltpu.VMEM((8, count), jnp.int32),
            pltpu.SMEM((8, count), jnp.int32),
            pltpu.SMEM((DEVS,), jnp.int32),
            pltpu.SemaphoreType.DMA,
        ],
    )(blocks, labels, owner_map)


FEATURE_CHUNKS = ((0, 5), (5, 5), (10, 5), (15, 5))
HIDDEN_CHUNKS = ((0, 4), (4, 5), (9, 5), (14, 6))
LAST_CHUNKS = ((0, 3), (3, 5), (8, 5), (13, 7))
PER_EXCHANGE = 14


def halo_copies(own, side_z, side_y, chunks, base, send_sem, recv_sem):
    gz, xy = lax.axis_index("gz"), lax.axis_index("xy")
    depth, height = lax.axis_size("gz"), lax.axis_size("xy")
    plan = []
    for c, (first, length) in enumerate(chunks):
        rows = pl.ds(first, length)
        plan.append(((1, 0), own.at[3, rows], side_z.at[0, rows]))
        plan.append(((-1, 0), own.at[0, rows], side_z.at[1, rows]))
    plan.append(((0, 1), own.at[:, 19], side_y.at[0, pl.ds(1, 4)]))
    plan.append(((0, -1), own.at[:, 0], side_y.at[1, pl.ds(1, 4)]))
    plan.append(((1, 1), own.at[3, 19], side_y.at[0, 0]))
    plan.append(((1, -1), own.at[3, 0], side_y.at[1, 0]))
    plan.append(((-1, 1), own.at[0, 19], side_y.at[0, 5]))
    plan.append(((-1, -1), own.at[0, 0], side_y.at[1, 5]))
    copies = []
    for i, ((dz, dy), src, dst) in enumerate(plan):
        def inside(a, b):
            return (a >= 0) & (a < depth) & (b >= 0) & (b < height)

        copy = pltpu.make_async_remote_copy(
            src_ref=src,
            dst_ref=dst,
            send_sem=send_sem.at[base + i],
            recv_sem=recv_sem.at[base + i],
            device_id=(gz + dz, xy + dy),
            device_id_type=MESH,
        )
        copies.append((copy, inside(gz + dz, xy + dy), inside(gz - dz, xy - dy)))
    return copies


def start(entry):
    @pl.when(entry[1])
    def _():
        entry[0].start()


def arrive(entry):
    @pl.when(entry[2])
    def _():
        entry[0].wait_recv()


def leave(entry):
    @pl.when(entry[1])
    def _():
        entry[0].wait_send()


def conv_kernel(
    own, w1, b1, w2, b2, emb_ref, wide, hwide, hidden, fz, fy, hz, hy, part1, part2,
    send_sem, recv_sem,
):
    gz, xy = lax.axis_index("gz"), lax.axis_index("xy")
    depth, height = lax.axis_size("gz"), lax.axis_size("xy")
    barrier = pltpu.get_barrier_semaphore()
    near = [(a, b) for a in (-1, 0, 1) for b in (-1, 0, 1) if (a, b) != (0, 0)]

    def exists(a, b):
        return (gz + a >= 0) & (gz + a < depth) & (xy + b >= 0) & (xy + b < height)

    for a, b in near:
        @pl.when(exists(a, b))
        def _():
            pl.semaphore_signal(
                barrier, inc=1, device_id=(gz + a, xy + b), device_id_type=MESH
            )

    for side, has in ((0, gz == 0), (1, gz == depth - 1)):
        @pl.when(has)
        def _():
            zeros = jnp.zeros(fz.shape[1:], fz.dtype)
            fz[side] = zeros
            hz[side] = zeros
            for s in range(2):
                fy[s, 5 * side] = jnp.zeros(fy.shape[2:], fy.dtype)
                hy[s, 5 * side] = jnp.zeros(fy.shape[2:], fy.dtype)

    for side, has in ((0, xy == 0), (1, xy == height - 1)):
        @pl.when(has)
        def _():
            fy[side] = jnp.zeros(fy.shape[1:], fy.dtype)
            hy[side] = jnp.zeros(fy.shape[1:], fy.dtype)

    beside_z = jnp.where(gz > 0, 1, 0) + jnp.where(gz < depth - 1, 1, 0)
    beside_y = jnp.where(xy > 0, 1, 0) + jnp.where(xy < height - 1, 1, 0)
    pl.semaphore_wait(barrier, (1 + beside_z) * (1 + beside_y) - 1)

    first = halo_copies(own, fz, fy, FEATURE_CHUNKS, 0, send_sem, recv_sem)
    then = halo_copies(hidden, hz, hy, HIDDEN_CHUNKS, PER_EXCHANGE, send_sem, recv_sem)
    for entry in first[8:] + first[:8]:
        start(entry)

    lane = lax.broadcasted_iota(jnp.int32, (48, 256), 1)

    def put(ref, e, y, value):
        turned = value.astype(jnp.float32)
        left = jnp.where(lane == 0, 0.0, pltpu.roll(turned, 1, 1))
        right = jnp.where(lane == 255, 0.0, pltpu.roll(turned, 255, 1))
        ref[e, y, 0:48, :] = left.astype(jnp.bfloat16)
        ref[e, y, 48:96, :] = value
        ref[e, y, 96:144, :] = right.astype(jnp.bfloat16)

    def slab(ref, e, y):
        return ref[e, pl.ds(y, 3)].reshape(432, 256)

    def product(w, ref, e, y, low, high, channels):
        r = jnp.dot(
            w[low * channels : (high + 1) * channels, :],
            slab(ref, e, y),
            preferred_element_type=jnp.float32,
        )
        return {
            e - dz: r[(dz - low) * channels : (dz - low + 1) * channels]
            for dz in range(low, high + 1)
        }

    def inner(w, ref, y, channels):
        total = {}
        for e, low, high in ((1, 0, 1), (2, 0, 2), (3, 0, 2), (4, 1, 2)):
            for z, v in product(w, ref, e, y, low, high, channels).items():
                total[z] = total[z] + v if z in total else v
        return total

    def fill(y, carry):
        for z in range(4):
            put(wide, z + 1, y + 1, own[z, y])
        return carry

    lax.fori_loop(0, 20, fill, 0)
    for entry in first[8:]:
        arrive(entry)

    def fill_side(e, carry):
        put(wide, e, 0, fy[0, e])
        put(wide, e, 21, fy[1, e])
        return carry

    lax.fori_loop(0, 6, fill_side, 0)

    bias1 = jnp.broadcast_to(b1[...], (48, 256))
    bias2 = jnp.broadcast_to(b2[...], (64, 256))

    def keep_hidden(z, y, total):
        value = jnp.maximum(total + bias1, 0.0).astype(jnp.bfloat16)
        hidden[z, y] = value
        put(hwide, z + 1, y + 1, value)

    def first_inner(y, carry):
        total = inner(w1, wide, y, 48)
        part1[0, y] = total[0]
        part1[1, y] = total[3]
        keep_hidden(1, y, total[1])
        keep_hidden(2, y, total[2])
        return carry

    lax.fori_loop(0, 20, first_inner, 0, unroll=2)

    def fill_z(y, carry):
        put(wide, 0, y + 1, fz[0, y])
        put(wide, 5, y + 1, fz[1, y])
        return carry

    def first_outer(y, carry):
        keep_hidden(0, y, part1[0, y] + product(w1, wide, 0, y, 0, 0, 48)[0])
        keep_hidden(3, y, part1[1, y] + product(w1, wide, 5, y, 2, 2, 48)[3])
        return carry

    for c in range(4):
        arrive(first[2 * c])
        arrive(first[2 * c + 1])
        low, length = FEATURE_CHUNKS[c]
        lax.fori_loop(low, low + length, fill_z, 0)
        low, length = HIDDEN_CHUNKS[c]
        lax.fori_loop(low, low + length, first_outer, 0)
        start(then[2 * c])
        start(then[2 * c + 1])
        if c == 0:
            for i in (9, 11, 13):
                start(then[i])
    for i in (8, 10, 12):
        start(then[i])

    for entry in then[8:]:
        arrive(entry)

    def hidden_side(e, carry):
        put(hwide, e, 0, hy[0, e])
        put(hwide, e, 21, hy[1, e])
        return carry

    lax.fori_loop(0, 6, hidden_side, 0)

    def keep(z, y, total):
        value = (total + bias2).astype(jnp.bfloat16)
        group = (z * 20 + y) * 2
        emb_ref[group] = value[:, 0:128]
        emb_ref[group + 1] = value[:, 128:256]

    def second_inner(y, carry):
        total = inner(w2, hwide, y, 64)
        part2[0, y] = total[0]
        part2[1, y] = total[3]
        keep(1, y, total[1])
        keep(2, y, total[2])
        return carry

    lax.fori_loop(0, 20, second_inner, 0, unroll=2)

    def hidden_z(y, carry):
        put(hwide, 0, y + 1, hz[0, y])
        put(hwide, 5, y + 1, hz[1, y])
        return carry

    def second_outer(y, carry):
        keep(0, y, part2[0, y] + product(w2, hwide, 0, y, 0, 0, 64)[0])
        keep(3, y, part2[1, y] + product(w2, hwide, 5, y, 2, 2, 64)[3])
        return carry

    for c in range(4):
        arrive(then[2 * c])
        arrive(then[2 * c + 1])
        low, length = HIDDEN_CHUNKS[c]
        lax.fori_loop(low, low + length, hidden_z, 0)
        low, length = LAST_CHUNKS[c]
        lax.fori_loop(low, low + length, second_outer, 0)

    for entry in first + then:
        leave(entry)


def embed(features, first_weight, first_bias, second_weight, second_bias):
    own = features.transpose(1, 2, 0, 3)
    w1 = first_weight.transpose(0, 3, 1, 2, 4).reshape(144, 432)
    w2 = second_weight.transpose(0, 3, 1, 2, 4).reshape(192, 432)
    bf, f32 = jnp.bfloat16, jnp.float32
    return pl.pallas_call(
        conv_kernel,
        out_shape=jax.ShapeDtypeStruct((GROUPS, EMB, 128), bf),
        in_specs=[pl.BlockSpec(memory_space=pltpu.VMEM)] * 5,
        out_specs=pl.BlockSpec(memory_space=pltpu.VMEM),
        scratch_shapes=[
            pltpu.VMEM((6, 22, 144, 256), bf),
            pltpu.VMEM((6, 22, 144, 256), bf),
            pltpu.VMEM((4, 20, 48, 256), bf),
            pltpu.VMEM((2, 20, 48, 256), bf),
            pltpu.VMEM((2, 6, 48, 256), bf),
            pltpu.VMEM((2, 20, 48, 256), bf),
            pltpu.VMEM((2, 6, 48, 256), bf),
            pltpu.VMEM((2, 20, 48, 256), f32),
            pltpu.VMEM((2, 20, 64, 256), f32),
            pltpu.SemaphoreType.DMA((2 * PER_EXCHANGE,)),
            pltpu.SemaphoreType.DMA((2 * PER_EXCHANGE,)),
        ],
        compiler_params=pltpu.CompilerParams(
            collective_id=1, has_side_effects=True, vmem_limit_bytes=52 << 20
        ),
    )(own, w1, first_bias[:, None], w2, second_bias[:, None])


def place(device):
    return (device // 32, lax.rem(device, 32))


def partner(me, k):
    core, x, y, z = lax.rem(me, 2), lax.rem(me // 2, 4), lax.rem(me // 8, 4), me // 32
    kc, kx, ky, kz = lax.rem(k, 2), lax.rem(k // 2, 4), lax.rem(k // 8, 4), k // 32
    ky = lax.rem(ky + kx, 4)
    kz = lax.rem(kz + kx + ky, 4)
    there = (lax.rem(z + kz, 4) * 4 + lax.rem(y + ky, 4)) * 4 + lax.rem(x + kx, 4)
    return there * 2 + lax.rem(core + kc, 2)


def moments_of(emb_ref, table_ref, device, send_ref):
    lane = lax.broadcasted_iota(jnp.int32, (1, 128), 1)
    inner = lax.broadcasted_iota(jnp.int32, (HALF, 128), 1) & 63
    outer = lax.broadcasted_iota(jnp.int32, (HALF, 128), 0)
    upper = (inner >= HALF) | (inner >= outer)
    diagonal = inner == outer
    line = lax.broadcasted_iota(jnp.int32, (16, 128), 0)
    one = jnp.ones((EMB, 256), jnp.bfloat16)
    near = lax.broadcasted_iota(jnp.int32, (EMB, 128), 1) < EMB
    extras = jnp.zeros((16, 128), jnp.float32)
    for p in range(PAIRS):
        parts, sizes, rows = [], [], []
        for h in range(2):
            code = table_ref[device * SLOTS + 2 * p + h]
            start = code >> 15
            size = (code >> 7) & 255
            rows.append((code & 127).astype(jnp.float32))
            sizes.append(size.astype(jnp.float32))
            group = start >> 7
            low = start & 127
            first = emb_ref[group]
            second = emb_ref[jnp.minimum(group + 1, GROUPS - 1)]
            in_first = jnp.where((lane >= low) & (lane < low + size), 1.0, 0.0).astype(jnp.bfloat16)
            in_second = jnp.where(lane + 128 < low + size, 1.0, 0.0).astype(jnp.bfloat16)
            mask_rows = jnp.broadcast_to(jnp.concatenate([in_first, in_second], axis=1), (16, 256))
            whole = jnp.concatenate([first, second], axis=1)
            left = jnp.concatenate([jnp.concatenate([first * in_first, second * in_second], axis=1), mask_rows], axis=0)
            right = jnp.concatenate([whole, one] if h == 0 else [one, whole], axis=0)
            parts.append(lax.dot_general(left, right, (((1,), (1,)), ((), ())), preferred_element_type=jnp.float32))
        size_row = jnp.where(lane < EMB, sizes[0], sizes[1])
        owner_row = jnp.where(lane < EMB, rows[0], rows[1])
        second_row = jnp.where(near[0:1], parts[0][EMB : EMB + 1], parts[1][EMB : EMB + 1])
        mean = second_row / jnp.maximum(size_row, 1.0)
        square = jnp.where(near, parts[0][0:EMB], parts[1][0:EMB])
        column = pltpu.roll(jnp.where(near, parts[1][0:EMB], parts[0][0:EMB]), EMB, 1)
        centred = square - column * mean
        rolled = pltpu.roll(centred[HALF:EMB], 96, 1)
        packed = jnp.where(upper, centred[0:HALF], rolled)
        send_ref[device, p * HALF : (p + 1) * HALF, :] = packed.astype(jnp.bfloat16)
        diag = jnp.sum(jnp.where(diagonal, rolled, 0.0), axis=0, keepdims=True)
        high = mean.astype(jnp.bfloat16).astype(jnp.float32)
        for place_of, value in (
            (p, diag),
            (3 + p, high),
            (6 + p, mean - high),
            (9 + p, size_row),
            (12 + p, owner_row),
        ):
            extras = jnp.where(line == place_of, value, extras)
    send_ref[device, BODY:ROWS, :] = extras.astype(jnp.bfloat16)


def exchange_kernel(emb_ref, table_ref, got_ref, send_ref, send_sem, recv_sem, own_sem):
    me = lax.axis_index("gz") * 32 + lax.axis_index("xy")
    barrier = pltpu.get_barrier_semaphore()

    def greet(k, carry):
        pl.semaphore_signal(
            barrier, inc=1, device_id=place(partner(me, k)), device_id_type=MESH
        )
        return carry

    lax.fori_loop(1, DEVS, greet, 0)
    for k in range(AHEAD):
        moments_of(emb_ref, table_ref, partner(me, k), send_ref)
    own = pltpu.make_async_copy(send_ref.at[me], got_ref.at[me], own_sem)
    own.start()
    pl.semaphore_wait(barrier, DEVS - 1)

    def copy(k):
        device = partner(me, k)
        return pltpu.make_async_remote_copy(
            src_ref=send_ref.at[device],
            dst_ref=got_ref.at[me],
            send_sem=send_sem.at[k],
            recv_sem=recv_sem.at[k],
            device_id=place(device),
            device_id_type=MESH,
        )

    for k in range(1, AHEAD):
        copy(k).start()

    def send(i, carry):
        for t in range(AHEAD):
            moments_of(emb_ref, table_ref, partner(me, i * AHEAD + t), send_ref)
        for t in range(AHEAD):
            copy(i * AHEAD + t).start()
        return carry

    lax.fori_loop(1, DEVS // AHEAD, send, 0)

    def finish(k, carry):
        copy(k).wait()
        return carry

    lax.fori_loop(1, DEVS, finish, 0)
    own.wait()


def exchange(embedding, table):
    return pl.pallas_call(
        exchange_kernel,
        out_shape=jax.ShapeDtypeStruct((DEVS, ROWS, 128), jnp.bfloat16),
        in_specs=[
            pl.BlockSpec(memory_space=pltpu.VMEM),
            pl.BlockSpec(memory_space=pltpu.SMEM),
        ],
        out_specs=pl.BlockSpec(memory_space=pl.ANY),
        scratch_shapes=[
            pltpu.VMEM((DEVS, ROWS, 128), jnp.bfloat16),
            pltpu.SemaphoreType.DMA((DEVS,)),
            pltpu.SemaphoreType.DMA((DEVS,)),
            pltpu.SemaphoreType.DMA,
        ],
        compiler_params=pltpu.CompilerParams(
            collective_id=0, has_side_effects=True, vmem_limit_bytes=40 << 20
        ),
    )(embedding, table)


CHUNKS = 4
QUAD = 4


def total_kernel(
    got_ref, mean_ref, cov_ref, body, extra, lines, acc_a, acc_b, id_vec, ids, hits, spread,
    second, full, body_sem, extra_sem, id_sem,
):
    fast = lax.Precision.HIGHEST
    per = DEVS // CHUNKS
    extra_copy = pltpu.make_async_copy(got_ref.at[:, pl.ds(BODY, 16), :], extra, extra_sem)
    extra_copy.start()
    body_copies = [
        pltpu.make_async_copy(
            got_ref.at[pl.ds(c * per, per), pl.ds(0, BODY), :],
            body.at[pl.ds(c * per, per)],
            body_sem.at[c],
        )
        for c in range(CHUNKS)
    ]
    for one in body_copies:
        one.start()
    acc_a[...] = jnp.zeros_like(acc_a)
    acc_b[...] = jnp.zeros_like(acc_b)
    extra_copy.wait()
    lines[...] = extra[...].astype(jnp.float32).reshape(DEVS * 16, 128)

    def line(k):
        return lines[pl.ds(k, DEVS, stride=16), :]

    lane = lax.broadcasted_iota(jnp.int32, (DEVS, 128), 1)
    row = lax.broadcasted_iota(jnp.int32, (DEVS, 128), 0)
    inner = lane & 63
    owners = [line(12 + p) for p in range(PAIRS)]
    id_vec[...] = jnp.where(
        inner == 0, owners[0], jnp.where(inner == 1, owners[1], owners[2])
    ).astype(jnp.int32)
    id_copy = pltpu.make_async_copy(id_vec, ids, id_sem)
    id_copy.start()

    means, sizes = [], []
    sums = jnp.zeros((DEVS, 384), jnp.float32)
    for p in range(PAIRS):
        mean = line(3 + p) + line(6 + p)
        size = line(9 + p)
        means.append(mean)
        sizes.append(size)
        turned = owners[p].T
        for h in range(2):
            hit = jnp.where(row == turned[64 * h : 64 * h + 1, :].astype(jnp.int32), 1.0, 0.0)
            hits[:, (2 * p + h) * 128 : (2 * p + h + 1) * 128] = hit
            mine = (lane >= EMB) if h else (lane < EMB)
            values = jnp.concatenate(
                [
                    jnp.where(mine, size * mean, 0.0),
                    jnp.where(mine, size, 0.0),
                    jnp.where(mine, line(p), 0.0),
                ],
                axis=1,
            )
            sums = sums + jnp.dot(
                hit, values, preferred_element_type=jnp.float32, precision=fast
            )

    def folded(value):
        return value + pltpu.roll(value, EMB, 1)

    count = jnp.maximum(folded(sums[:, 128:256]), 1.0)
    total_mean = folded(sums[:, 0:128]) / count
    mean_ref[...] = total_mean[:, 0:EMB]
    diag_sum = folded(sums[:, 256:384])
    inverse = 1.0 / count
    lines[0:DEVS, :] = diag_sum
    lines[DEVS : 2 * DEVS, :] = inverse

    for p in range(PAIRS):
        for h in range(2):
            owner = owners[p]
            other = pltpu.roll(owner, EMB, 1)
            owner_all = (
                jnp.where(lane < EMB, other, owner) if h else jnp.where(lane < EMB, owner, other)
            )
            hit_t = jnp.where(owner_all.astype(jnp.int32) == lane, 1.0, 0.0)
            theirs = jnp.dot(
                hit_t, total_mean, preferred_element_type=jnp.float32, precision=fast
            )
            off = jnp.sqrt(sizes[p]) * (means[p] - theirs)
            if h:
                off = pltpu.roll(off, EMB, 1)
            off = jnp.where(lane < EMB, off, 0.0)
            k = 2 * p + h
            second[k * 128 : (k + 1) * 128, :] = off.astype(jnp.bfloat16)
            spread[:, k * 128 : (k + 1) * 128] = off.T[0:EMB, :].astype(jnp.bfloat16)

    id_copy.wait()
    for c in range(CHUNKS):
        body_copies[c].wait()

        def add(s, carry):
            for p in range(PAIRS):
                value = body[s, p * HALF : (p + 1) * HALF, :].astype(jnp.float32)
                a = ids[s, p]
                b = ids[s, 64 + p]
                acc_a[a] = acc_a[a] + value
                acc_b[b] = acc_b[b] + value
            return carry

        lax.fori_loop(c * per, (c + 1) * per, add, 0, unroll=2)

    lane32 = lax.broadcasted_iota(jnp.int32, (HALF, 128), 1)
    row32 = lax.broadcasted_iota(jnp.int32, (HALF, 128), 0)

    def quad(q, carry):
        base = q * QUAD
        left = []
        for t in range(QUAD):
            mask = hits[pl.ds(base + t, 1), :].astype(jnp.bfloat16)
            left.append(spread[...] * mask)
        between = jnp.dot(
            jnp.concatenate(left, axis=0), second[...], preferred_element_type=jnp.float32
        )
        packed = [
            acc_a[base + t] + pltpu.roll(acc_b[base + t], EMB, 1) for t in range(QUAD)
        ]
        turned = jnp.concatenate(packed, axis=0).T
        for t in range(QUAD):
            diag = lines[pl.ds(base + t, 1), :]
            inv = lines[pl.ds(DEVS + base + t, 1), :]
            flip = pltpu.roll(turned, (128 - HALF * t) % 128, 1) if t else turned
            flip_up, flip_down = flip[0:HALF], flip[HALF:EMB]
            here = packed[t]
            top = jnp.where((lane32 >= HALF) | (lane32 >= row32), here, flip_up)
            low = jnp.where(
                lane32 < row32, here, jnp.where(lane32 == row32, diag, flip_up)
            )
            bottom = jnp.where(lane32 < HALF, flip_down, pltpu.roll(low, HALF, 1))
            both = jnp.concatenate([top, bottom], axis=0)
            both = (both + between[t * EMB : (t + 1) * EMB]) * inv
            full[pl.ds((base + t) * EMB, EMB), :] = both
        return carry

    lax.fori_loop(0, SV_DEV // QUAD, quad, 0)

    for t in range(EMB // 2):
        even = full[pl.ds(2 * t, SV_DEV, stride=EMB), :]
        odd = full[pl.ds(2 * t + 1, SV_DEV, stride=EMB), :]
        cov_ref[:, t * 128 : (t + 1) * 128] = jnp.where(
            lane < EMB, even, pltpu.roll(odd, EMB, 1)
        )


def totals(got):
    return pl.pallas_call(
        total_kernel,
        out_shape=(
            jax.ShapeDtypeStruct((SV_DEV, EMB), jnp.float32),
            jax.ShapeDtypeStruct((SV_DEV, EMB * EMB), jnp.float32),
        ),
        in_specs=[pl.BlockSpec(memory_space=pl.ANY)],
        out_specs=(
            pl.BlockSpec(memory_space=pltpu.VMEM),
            pl.BlockSpec(memory_space=pltpu.VMEM),
        ),
        scratch_shapes=[
            pltpu.VMEM((DEVS, BODY, 128), jnp.bfloat16),
            pltpu.VMEM((DEVS, 16, 128), jnp.bfloat16),
            pltpu.VMEM((DEVS * 16, 128), jnp.float32),
            pltpu.VMEM((SV_DEV, HALF, 128), jnp.float32),
            pltpu.VMEM((SV_DEV, HALF, 128), jnp.float32),
            pltpu.VMEM((DEVS, 128), jnp.int32),
            pltpu.SMEM((DEVS, 128), jnp.int32),
            pltpu.VMEM((SV_DEV, DEVS * SLOTS), jnp.float32),
            pltpu.VMEM((EMB, DEVS * SLOTS), jnp.bfloat16),
            pltpu.VMEM((DEVS * SLOTS, 128), jnp.bfloat16),
            pltpu.VMEM((SV_DEV * EMB, 128), jnp.float32),
            pltpu.SemaphoreType.DMA((CHUNKS,)),
            pltpu.SemaphoreType.DMA,
            pltpu.SemaphoreType.DMA,
        ],
        compiler_params=pltpu.CompilerParams(vmem_limit_bytes=48 << 20),
    )(got)


def local(
    features, first_weight, first_bias, second_weight, second_bias, labels, blocks, owner_map
):
    table = slot_table(blocks.reshape(blocks.shape[2], blocks.shape[3]), labels, owner_map)
    grouped = embed(features, first_weight, first_bias, second_weight, second_bias)
    return totals(exchange(grouped, table))


def solution(mesh):
    return jax.shard_map(
        local,
        mesh=mesh,
        in_specs=(
            P(None, "gz", "xy", None),
            P(),
            P(),
            P(),
            P(),
            P("gz", "xy", None),
            P("gz", "xy", None, None),
            P(),
        ),
        out_specs=(P(("gz", "xy"), None), P(("gz", "xy"), None)),
        check_vma=False,
    )
```

```python
import functools

import jax
import jax.numpy as jnp
from jax import lax
from jax.experimental import pallas as pl
from jax.experimental.pallas import tpu as pltpu
from jax.sharding import PartitionSpec as P

SV_DEV = 128
EMB = 64
HALF = 32
SLOTS = 6
PAIRS = 3
BODY = PAIRS * HALF
ROWS = BODY + 16
DEVS = 128
GROUPS = 160
AHEAD = 4
MESH = pl.DeviceIdType.MESH


FEATURE_CHUNKS = ((0, 5), (5, 5), (10, 5), (15, 5))
HIDDEN_CHUNKS = ((0, 4), (4, 5), (9, 5), (14, 6))
LAST_CHUNKS = ((0, 3), (3, 5), (8, 5), (13, 7))
PER_EXCHANGE = 14


def halo_copies(own, side_z, side_y, chunks, base, send_sem, recv_sem):
    gz, xy = lax.axis_index("gz"), lax.axis_index("xy")
    depth, height = lax.axis_size("gz"), lax.axis_size("xy")
    plan = []
    for c, (first, length) in enumerate(chunks):
        rows = pl.ds(first, length)
        plan.append(((1, 0), own.at[3, rows], side_z.at[0, rows]))
        plan.append(((-1, 0), own.at[0, rows], side_z.at[1, rows]))
    plan.append(((0, 1), own.at[:, 19], side_y.at[0, pl.ds(1, 4)]))
    plan.append(((0, -1), own.at[:, 0], side_y.at[1, pl.ds(1, 4)]))
    plan.append(((1, 1), own.at[3, 19], side_y.at[0, 0]))
    plan.append(((1, -1), own.at[3, 0], side_y.at[1, 0]))
    plan.append(((-1, 1), own.at[0, 19], side_y.at[0, 5]))
    plan.append(((-1, -1), own.at[0, 0], side_y.at[1, 5]))
    copies = []
    for i, ((dz, dy), src, dst) in enumerate(plan):
        def inside(a, b):
            return (a >= 0) & (a < depth) & (b >= 0) & (b < height)

        copy = pltpu.make_async_remote_copy(
            src_ref=src,
            dst_ref=dst,
            send_sem=send_sem.at[base + i],
            recv_sem=recv_sem.at[base + i],
            device_id=(gz + dz, xy + dy),
            device_id_type=MESH,
        )
        copies.append((copy, inside(gz + dz, xy + dy), inside(gz - dz, xy - dy)))
    return copies


def start(entry):
    @pl.when(entry[1])
    def _():
        entry[0].start()


def arrive(entry):
    @pl.when(entry[2])
    def _():
        entry[0].wait_recv()


def leave(entry):
    @pl.when(entry[1])
    def _():
        entry[0].wait_send()


def main_kernel(
    own, w1, b1, w2, b2, lists_ref, labels_hbm, owner_hbm, got_ref, wide, hwide, hidden,
    fz, fy, hz, hy, part1, part2, emb_ref, send_ref, labels_ref, owner_ref, facts, scalars,
    rows_s, rows_v, table_v, table_ref, send_sem, recv_sem, far_send, far_recv, own_sem, here_sem,
):
    gz, xy = lax.axis_index("gz"), lax.axis_index("xy")
    depth, height = lax.axis_size("gz"), lax.axis_size("xy")
    me = gz * 32 + xy
    barrier = pltpu.get_barrier_semaphore()
    labels_copy = pltpu.make_async_copy(labels_hbm, labels_ref, here_sem.at[0])
    owner_copy = pltpu.make_async_copy(owner_hbm, owner_ref, here_sem.at[1])
    labels_copy.start()
    owner_copy.start()

    for side, has in ((0, gz == 0), (1, gz == depth - 1)):
        @pl.when(has)
        def _():
            zeros = jnp.zeros(fz.shape[1:], fz.dtype)
            fz[side] = zeros
            hz[side] = zeros
            for s in range(2):
                fy[s, 5 * side] = jnp.zeros(fy.shape[2:], fy.dtype)
                hy[s, 5 * side] = jnp.zeros(fy.shape[2:], fy.dtype)

    for side, has in ((0, xy == 0), (1, xy == height - 1)):
        @pl.when(has)
        def _():
            fy[side] = jnp.zeros(fy.shape[1:], fy.dtype)
            hy[side] = jnp.zeros(fy.shape[1:], fy.dtype)

    lane = lax.broadcasted_iota(jnp.int32, (48, 256), 1)

    def put(ref, e, y, value):
        turned = value.astype(jnp.float32)
        left = jnp.where(lane == 0, 0.0, pltpu.roll(turned, 1, 1))
        right = jnp.where(lane == 255, 0.0, pltpu.roll(turned, 255, 1))
        ref[e, y, 0:48, :] = left.astype(jnp.bfloat16)
        ref[e, y, 48:96, :] = value
        ref[e, y, 96:144, :] = right.astype(jnp.bfloat16)

    def greet(k):
        pl.semaphore_signal(
            barrier, inc=1, device_id=place(partner(me, k)), device_id_type=MESH
        )

    def fill(y, carry):
        for k in range(6):
            greet(1 + y * 6 + k)
        for z in range(4):
            put(wide, z + 1, y + 1, own[z, y])
        return carry

    lax.fori_loop(0, 20, fill, 0)
    for k in range(121, DEVS):
        greet(k)
    count = lists_ref.shape[0]
    lists = lists_ref[...]
    sizes = jnp.sum(jnp.where(lists >= 0, 1, 0), axis=1, keepdims=True)
    column = lax.broadcasted_iota(jnp.int32, lists.shape, 1)
    facts[...] = jnp.where(column == 0, lists, sizes).astype(jnp.float32).T[0:8, :].astype(jnp.int32)
    facts_copy = pltpu.make_async_copy(facts, scalars, here_sem.at[2])
    facts_copy.start()
    pl.semaphore_wait(barrier, DEVS - 1)

    first = halo_copies(own, fz, fy, FEATURE_CHUNKS, 0, send_sem, recv_sem)
    then = halo_copies(hidden, hz, hy, HIDDEN_CHUNKS, PER_EXCHANGE, send_sem, recv_sem)
    for entry in first[8:] + first[:8]:
        start(entry)

    def slab(ref, e, y):
        return ref[e, pl.ds(y, 3)].reshape(432, 256)

    def product(w, ref, e, y, low, high, channels):
        r = jnp.dot(
            w[low * channels : (high + 1) * channels, :],
            slab(ref, e, y),
            preferred_element_type=jnp.float32,
        )
        return {
            e - dz: r[(dz - low) * channels : (dz - low + 1) * channels]
            for dz in range(low, high + 1)
        }

    def inner(w, ref, y, channels):
        total = {}
        for e, low, high in ((1, 0, 1), (2, 0, 2), (3, 0, 2), (4, 1, 2)):
            for z, v in product(w, ref, e, y, low, high, channels).items():
                total[z] = total[z] + v if z in total else v
        return total

    for entry in first[8:]:
        arrive(entry)

    def fill_side(e, carry):
        put(wide, e, 0, fy[0, e])
        put(wide, e, 21, fy[1, e])
        return carry

    lax.fori_loop(0, 6, fill_side, 0)

    bias1 = jnp.broadcast_to(b1[...], (48, 256))
    bias2 = jnp.broadcast_to(b2[...], (64, 256))

    def keep_hidden(z, y, total):
        value = jnp.maximum(total + bias1, 0.0).astype(jnp.bfloat16)
        hidden[z, y] = value
        put(hwide, z + 1, y + 1, value)

    def first_inner(y, carry):
        total = inner(w1, wide, y, 48)
        part1[0, y] = total[0]
        part1[1, y] = total[3]
        keep_hidden(1, y, total[1])
        keep_hidden(2, y, total[2])
        return carry

    lax.fori_loop(0, 20, first_inner, 0, unroll=2)

    labels_copy.wait()
    owner_copy.wait()
    facts_copy.wait()

    def look(b, carry):
        at = scalars[0, b]
        run = at >> 8
        z = jnp.clip((run * 3277) >> 16, 0, 3)
        label = labels_ref[z, jnp.clip(run - z * 20, 0, 19), at & 255]
        rows_s[0, b] = owner_ref[label & (owner_ref.shape[0] - 1)]
        return carry

    lax.fori_loop(0, count, look, 0, unroll=8)
    rows_copy = pltpu.make_async_copy(rows_s, rows_v, here_sem.at[3])
    rows_copy.start()
    rows_copy.wait()
    line8 = lax.broadcasted_iota(jnp.int32, (8, count), 0)
    three = jnp.where(line8 == 2, jnp.broadcast_to(rows_v[0:1, :], (8, count)), facts[...])
    turned3 = jnp.concatenate(
        [three.astype(jnp.float32), jnp.zeros((120, count), jnp.float32)], axis=0
    ).T.astype(jnp.int32)
    row_of = turned3[:, 2:3]
    code = (turned3[:, 0:1] << 15) + (turned3[:, 1:2] << 7) + (row_of & 127)
    hit = (row_of >> 7) == lax.broadcasted_iota(jnp.int32, (count, DEVS), 1)
    before = lax.broadcasted_iota(jnp.int32, (count, count), 0) > lax.broadcasted_iota(
        jnp.int32, (count, count), 1
    )
    rank = jnp.dot(
        jnp.where(before, 1.0, 0.0).astype(jnp.bfloat16),
        jnp.where(hit, 1.0, 0.0).astype(jnp.bfloat16),
        preferred_element_type=jnp.float32,
    )
    rank = jnp.where(hit, rank, -1.0)
    slots = [
        jnp.sum(jnp.where(rank == float(k), code, 0), axis=0, keepdims=True)
        for k in range(SLOTS)
    ]
    table_v[...] = jnp.concatenate(slots + [slots[0], slots[0]], axis=0)
    table_copy = pltpu.make_async_copy(table_v, table_ref, here_sem.at[4])
    table_copy.start()

    def fill_z(y, carry):
        put(wide, 0, y + 1, fz[0, y])
        put(wide, 5, y + 1, fz[1, y])
        return carry

    def first_outer(y, carry):
        keep_hidden(0, y, part1[0, y] + product(w1, wide, 0, y, 0, 0, 48)[0])
        keep_hidden(3, y, part1[1, y] + product(w1, wide, 5, y, 2, 2, 48)[3])
        return carry

    for c in range(4):
        arrive(first[2 * c])
        arrive(first[2 * c + 1])
        low, length = FEATURE_CHUNKS[c]
        lax.fori_loop(low, low + length, fill_z, 0)
        low, length = HIDDEN_CHUNKS[c]
        lax.fori_loop(low, low + length, first_outer, 0)
        start(then[2 * c])
        start(then[2 * c + 1])
        if c == 0:
            for i in (9, 11, 13):
                start(then[i])
    for i in (8, 10, 12):
        start(then[i])

    for entry in then[8:]:
        arrive(entry)

    def hidden_side(e, carry):
        put(hwide, e, 0, hy[0, e])
        put(hwide, e, 21, hy[1, e])
        return carry

    lax.fori_loop(0, 6, hidden_side, 0)

    def keep(z, y, total):
        value = (total + bias2).astype(jnp.bfloat16)
        group = (z * 20 + y) * 2
        emb_ref[group] = value[:, 0:128]
        emb_ref[group + 1] = value[:, 128:256]

    def second_inner(y, carry):
        total = inner(w2, hwide, y, 64)
        part2[0, y] = total[0]
        part2[1, y] = total[3]
        keep(1, y, total[1])
        keep(2, y, total[2])
        return carry

    lax.fori_loop(0, 20, second_inner, 0, unroll=2)

    def hidden_z(y, carry):
        put(hwide, 0, y + 1, hz[0, y])
        put(hwide, 5, y + 1, hz[1, y])
        return carry

    def second_outer(y, carry):
        keep(0, y, part2[0, y] + product(w2, hwide, 0, y, 0, 0, 64)[0])
        keep(3, y, part2[1, y] + product(w2, hwide, 5, y, 2, 2, 64)[3])
        return carry

    for c in range(4):
        arrive(then[2 * c])
        arrive(then[2 * c + 1])
        low, length = HIDDEN_CHUNKS[c]
        lax.fori_loop(low, low + length, hidden_z, 0)
        low, length = LAST_CHUNKS[c]
        lax.fori_loop(low, low + length, second_outer, 0)

    table_copy.wait()

    def copy(k):
        device = partner(me, k)
        return pltpu.make_async_remote_copy(
            src_ref=send_ref.at[device],
            dst_ref=got_ref.at[me],
            send_sem=far_send.at[k],
            recv_sem=far_recv.at[k],
            device_id=place(device),
            device_id_type=MESH,
        )

    for k in range(AHEAD):
        moments_of(emb_ref, table_ref, partner(me, k), send_ref)
    own_copy = pltpu.make_async_copy(send_ref.at[me], got_ref.at[me], own_sem)
    own_copy.start()
    for k in range(1, AHEAD):
        copy(k).start()

    def send(i, carry):
        for t in range(AHEAD):
            moments_of(emb_ref, table_ref, partner(me, i * AHEAD + t), send_ref)
        for t in range(AHEAD):
            copy(i * AHEAD + t).start()
        return carry

    lax.fori_loop(1, DEVS // AHEAD, send, 0)
    for entry in first + then:
        leave(entry)

    def finish(k, carry):
        copy(k).wait()
        return carry

    lax.fori_loop(1, DEVS, finish, 0)
    own_copy.wait()


def main(features, first_weight, first_bias, second_weight, second_bias, labels, blocks, owner_map):
    own = features.transpose(1, 2, 0, 3)
    w1 = first_weight.transpose(0, 3, 1, 2, 4).reshape(144, 432)
    w2 = second_weight.transpose(0, 3, 1, 2, 4).reshape(192, 432)
    bf, f32, i32 = jnp.bfloat16, jnp.float32, jnp.int32
    count = blocks.shape[0]
    return pl.pallas_call(
        main_kernel,
        out_shape=jax.ShapeDtypeStruct((DEVS, ROWS, 128), bf),
        in_specs=[pl.BlockSpec(memory_space=pltpu.VMEM)] * 6
        + [pl.BlockSpec(memory_space=pl.ANY)] * 2,
        out_specs=pl.BlockSpec(memory_space=pl.ANY),
        scratch_shapes=[
            pltpu.VMEM((6, 22, 144, 256), bf),
            pltpu.VMEM((6, 22, 144, 256), bf),
            pltpu.VMEM((4, 20, 48, 256), bf),
            pltpu.VMEM((2, 20, 48, 256), bf),
            pltpu.VMEM((2, 6, 48, 256), bf),
            pltpu.VMEM((2, 20, 48, 256), bf),
            pltpu.VMEM((2, 6, 48, 256), bf),
            pltpu.VMEM((2, 20, 48, 256), f32),
            pltpu.VMEM((2, 20, 64, 256), f32),
            pltpu.VMEM((GROUPS, EMB, 128), bf),
            pltpu.VMEM((DEVS, ROWS, 128), bf),
            pltpu.SMEM(labels.shape, i32),
            pltpu.SMEM(owner_map.shape, i32),
            pltpu.VMEM((8, count), i32),
            pltpu.SMEM((8, count), i32),
            pltpu.SMEM((8, count), i32),
            pltpu.VMEM((8, count), i32),
            pltpu.VMEM((8, DEVS), i32),
            pltpu.SMEM((8, DEVS), i32),
            pltpu.SemaphoreType.DMA((2 * PER_EXCHANGE,)),
            pltpu.SemaphoreType.DMA((2 * PER_EXCHANGE,)),
            pltpu.SemaphoreType.DMA((DEVS,)),
            pltpu.SemaphoreType.DMA((DEVS,)),
            pltpu.SemaphoreType.DMA,
            pltpu.SemaphoreType.DMA((5,)),
        ],
        compiler_params=pltpu.CompilerParams(
            collective_id=0, has_side_effects=True, vmem_limit_bytes=52 << 20
        ),
    )(own, w1, first_bias[:, None], w2, second_bias[:, None], blocks, labels, owner_map)


def place(device):
    return (device // 32, lax.rem(device, 32))


def partner(me, k):
    core, x, y, z = lax.rem(me, 2), lax.rem(me // 2, 4), lax.rem(me // 8, 4), me // 32
    kc, kx, ky, kz = lax.rem(k, 2), lax.rem(k // 2, 4), lax.rem(k // 8, 4), k // 32
    ky = lax.rem(ky + kx, 4)
    kz = lax.rem(kz + kx + ky, 4)
    there = (lax.rem(z + kz, 4) * 4 + lax.rem(y + ky, 4)) * 4 + lax.rem(x + kx, 4)
    return there * 2 + lax.rem(core + kc, 2)


def moments_of(emb_ref, table_ref, device, send_ref):
    lane = lax.broadcasted_iota(jnp.int32, (1, 128), 1)
    inner = lax.broadcasted_iota(jnp.int32, (HALF, 128), 1) & 63
    outer = lax.broadcasted_iota(jnp.int32, (HALF, 128), 0)
    upper = (inner >= HALF) | (inner >= outer)
    diagonal = inner == outer
    line = lax.broadcasted_iota(jnp.int32, (16, 128), 0)
    one = jnp.ones((EMB, 256), jnp.bfloat16)
    near = lax.broadcasted_iota(jnp.int32, (EMB, 128), 1) < EMB
    extras = jnp.zeros((16, 128), jnp.float32)
    for p in range(PAIRS):
        parts, sizes, rows = [], [], []
        for h in range(2):
            code = table_ref[2 * p + h, device]
            start = code >> 15
            size = (code >> 7) & 255
            rows.append((code & 127).astype(jnp.float32))
            sizes.append(size.astype(jnp.float32))
            group = jnp.clip(start >> 7, 0, GROUPS - 1)
            low = start & 127
            first = emb_ref[group]
            second = emb_ref[jnp.minimum(group + 1, GROUPS - 1)]
            in_first = jnp.where((lane >= low) & (lane < low + size), 1.0, 0.0).astype(jnp.bfloat16)
            in_second = jnp.where(lane + 128 < low + size, 1.0, 0.0).astype(jnp.bfloat16)
            mask_rows = jnp.broadcast_to(jnp.concatenate([in_first, in_second], axis=1), (16, 256))
            whole = jnp.concatenate([first, second], axis=1)
            left = jnp.concatenate([jnp.concatenate([first * in_first, second * in_second], axis=1), mask_rows], axis=0)
            right = jnp.concatenate([whole, one] if h == 0 else [one, whole], axis=0)
            parts.append(lax.dot_general(left, right, (((1,), (1,)), ((), ())), preferred_element_type=jnp.float32))
        size_row = jnp.where(lane < EMB, sizes[0], sizes[1])
        owner_row = jnp.where(lane < EMB, rows[0], rows[1])
        second_row = jnp.where(near[0:1], parts[0][EMB : EMB + 1], parts[1][EMB : EMB + 1])
        mean = second_row / jnp.maximum(size_row, 1.0)
        square = jnp.where(near, parts[0][0:EMB], parts[1][0:EMB])
        column = pltpu.roll(jnp.where(near, parts[1][0:EMB], parts[0][0:EMB]), EMB, 1)
        centred = square - column * mean
        rolled = pltpu.roll(centred[HALF:EMB], 96, 1)
        packed = jnp.where(upper, centred[0:HALF], rolled)
        send_ref[device, p * HALF : (p + 1) * HALF, :] = packed.astype(jnp.bfloat16)
        diag = jnp.sum(jnp.where(diagonal, rolled, 0.0), axis=0, keepdims=True)
        high = mean.astype(jnp.bfloat16).astype(jnp.float32)
        for place_of, value in (
            (p, diag),
            (3 + p, high),
            (6 + p, mean - high),
            (9 + p, size_row),
            (12 + p, owner_row),
        ):
            extras = jnp.where(line == place_of, value, extras)
    send_ref[device, BODY:ROWS, :] = extras.astype(jnp.bfloat16)


CHUNKS = 4
QUAD = 4


def total_kernel(
    got_ref, mean_ref, cov_ref, body, extra, lines, acc_a, acc_b, id_vec, ids, hits, spread,
    second, full, body_sem, extra_sem, id_sem,
):
    fast = lax.Precision.HIGHEST
    per = DEVS // CHUNKS
    extra_copy = pltpu.make_async_copy(got_ref.at[:, pl.ds(BODY, 16), :], extra, extra_sem)
    extra_copy.start()
    body_copies = [
        pltpu.make_async_copy(
            got_ref.at[pl.ds(c * per, per), pl.ds(0, BODY), :],
            body.at[pl.ds(c * per, per)],
            body_sem.at[c],
        )
        for c in range(CHUNKS)
    ]
    for one in body_copies:
        one.start()
    acc_a[...] = jnp.zeros_like(acc_a)
    acc_b[...] = jnp.zeros_like(acc_b)
    extra_copy.wait()
    lines[...] = extra[...].astype(jnp.float32).reshape(DEVS * 16, 128)

    def line(k):
        return lines[pl.ds(k, DEVS, stride=16), :]

    lane = lax.broadcasted_iota(jnp.int32, (DEVS, 128), 1)
    row = lax.broadcasted_iota(jnp.int32, (DEVS, 128), 0)
    inner = lane & 63
    owners = [line(12 + p) for p in range(PAIRS)]
    id_vec[...] = jnp.where(
        inner == 0, owners[0], jnp.where(inner == 1, owners[1], owners[2])
    ).astype(jnp.int32)
    id_copy = pltpu.make_async_copy(id_vec, ids, id_sem)
    id_copy.start()

    means, sizes = [], []
    sums = jnp.zeros((DEVS, 384), jnp.float32)
    for p in range(PAIRS):
        mean = line(3 + p) + line(6 + p)
        size = line(9 + p)
        means.append(mean)
        sizes.append(size)
        turned = owners[p].T
        for h in range(2):
            hit = jnp.where(row == turned[64 * h : 64 * h + 1, :].astype(jnp.int32), 1.0, 0.0)
            hits[:, (2 * p + h) * 128 : (2 * p + h + 1) * 128] = hit
            mine = (lane >= EMB) if h else (lane < EMB)
            values = jnp.concatenate(
                [
                    jnp.where(mine, size * mean, 0.0),
                    jnp.where(mine, size, 0.0),
                    jnp.where(mine, line(p), 0.0),
                ],
                axis=1,
            )
            sums = sums + jnp.dot(
                hit, values, preferred_element_type=jnp.float32, precision=fast
            )

    def folded(value):
        return value + pltpu.roll(value, EMB, 1)

    count = jnp.maximum(folded(sums[:, 128:256]), 1.0)
    total_mean = folded(sums[:, 0:128]) / count
    mean_ref[...] = total_mean[:, 0:EMB]
    diag_sum = folded(sums[:, 256:384])
    inverse = 1.0 / count
    lines[0:DEVS, :] = diag_sum
    lines[DEVS : 2 * DEVS, :] = inverse

    for p in range(PAIRS):
        for h in range(2):
            owner = owners[p]
            other = pltpu.roll(owner, EMB, 1)
            owner_all = (
                jnp.where(lane < EMB, other, owner) if h else jnp.where(lane < EMB, owner, other)
            )
            hit_t = jnp.where(owner_all.astype(jnp.int32) == lane, 1.0, 0.0)
            theirs = jnp.dot(
                hit_t, total_mean, preferred_element_type=jnp.float32, precision=fast
            )
            off = jnp.sqrt(sizes[p]) * (means[p] - theirs)
            if h:
                off = pltpu.roll(off, EMB, 1)
            off = jnp.where(lane < EMB, off, 0.0)
            k = 2 * p + h
            second[k * 128 : (k + 1) * 128, :] = off.astype(jnp.bfloat16)
            spread[:, k * 128 : (k + 1) * 128] = off.T[0:EMB, :].astype(jnp.bfloat16)

    id_copy.wait()
    for c in range(CHUNKS):
        body_copies[c].wait()

        def add(s, carry):
            for p in range(PAIRS):
                value = body[s, p * HALF : (p + 1) * HALF, :].astype(jnp.float32)
                a = ids[s, p]
                b = ids[s, 64 + p]
                acc_a[a] = acc_a[a] + value
                acc_b[b] = acc_b[b] + value
            return carry

        lax.fori_loop(c * per, (c + 1) * per, add, 0, unroll=2)

    lane32 = lax.broadcasted_iota(jnp.int32, (HALF, 128), 1)
    row32 = lax.broadcasted_iota(jnp.int32, (HALF, 128), 0)

    def quad(q, carry):
        base = q * QUAD
        left = []
        for t in range(QUAD):
            mask = hits[pl.ds(base + t, 1), :].astype(jnp.bfloat16)
            left.append(spread[...] * mask)
        between = jnp.dot(
            jnp.concatenate(left, axis=0), second[...], preferred_element_type=jnp.float32
        )
        packed = [
            acc_a[base + t] + pltpu.roll(acc_b[base + t], EMB, 1) for t in range(QUAD)
        ]
        turned = jnp.concatenate(packed, axis=0).T
        for t in range(QUAD):
            diag = lines[pl.ds(base + t, 1), :]
            inv = lines[pl.ds(DEVS + base + t, 1), :]
            flip = pltpu.roll(turned, (128 - HALF * t) % 128, 1) if t else turned
            flip_up, flip_down = flip[0:HALF], flip[HALF:EMB]
            here = packed[t]
            top = jnp.where((lane32 >= HALF) | (lane32 >= row32), here, flip_up)
            low = jnp.where(
                lane32 < row32, here, jnp.where(lane32 == row32, diag, flip_up)
            )
            bottom = jnp.where(lane32 < HALF, flip_down, pltpu.roll(low, HALF, 1))
            both = jnp.concatenate([top, bottom], axis=0)
            both = (both + between[t * EMB : (t + 1) * EMB]) * inv
            full[pl.ds((base + t) * EMB, EMB), :] = both
        return carry

    lax.fori_loop(0, SV_DEV // QUAD, quad, 0)

    for t in range(EMB // 2):
        even = full[pl.ds(2 * t, SV_DEV, stride=EMB), :]
        odd = full[pl.ds(2 * t + 1, SV_DEV, stride=EMB), :]
        cov_ref[:, t * 128 : (t + 1) * 128] = jnp.where(
            lane < EMB, even, pltpu.roll(odd, EMB, 1)
        )


def totals(got):
    return pl.pallas_call(
        total_kernel,
        out_shape=(
            jax.ShapeDtypeStruct((SV_DEV, EMB), jnp.float32),
            jax.ShapeDtypeStruct((SV_DEV, EMB * EMB), jnp.float32),
        ),
        in_specs=[pl.BlockSpec(memory_space=pl.ANY)],
        out_specs=(
            pl.BlockSpec(memory_space=pltpu.VMEM),
            pl.BlockSpec(memory_space=pltpu.VMEM),
        ),
        scratch_shapes=[
            pltpu.VMEM((DEVS, BODY, 128), jnp.bfloat16),
            pltpu.VMEM((DEVS, 16, 128), jnp.bfloat16),
            pltpu.VMEM((DEVS * 16, 128), jnp.float32),
            pltpu.VMEM((SV_DEV, HALF, 128), jnp.float32),
            pltpu.VMEM((SV_DEV, HALF, 128), jnp.float32),
            pltpu.VMEM((DEVS, 128), jnp.int32),
            pltpu.SMEM((DEVS, 128), jnp.int32),
            pltpu.VMEM((SV_DEV, DEVS * SLOTS), jnp.float32),
            pltpu.VMEM((EMB, DEVS * SLOTS), jnp.bfloat16),
            pltpu.VMEM((DEVS * SLOTS, 128), jnp.bfloat16),
            pltpu.VMEM((SV_DEV * EMB, 128), jnp.float32),
            pltpu.SemaphoreType.DMA((CHUNKS,)),
            pltpu.SemaphoreType.DMA,
            pltpu.SemaphoreType.DMA,
        ],
        compiler_params=pltpu.CompilerParams(vmem_limit_bytes=48 << 20),
    )(got)


def local(
    features, first_weight, first_bias, second_weight, second_bias, labels, blocks, owner_map
):
    got = main(
        features,
        first_weight,
        first_bias,
        second_weight,
        second_bias,
        labels,
        blocks.reshape(blocks.shape[2], blocks.shape[3]),
        owner_map,
    )
    return totals(got)


def solution(mesh):
    return jax.shard_map(
        local,
        mesh=mesh,
        in_specs=(
            P(None, "gz", "xy", None),
            P(),
            P(),
            P(),
            P(),
            P("gz", "xy", None),
            P("gz", "xy", None, None),
            P(),
        ),
        out_specs=(P(("gz", "xy"), None), P(("gz", "xy"), None)),
        check_vma=False,
    )
```

```python
import functools

import jax
import jax.numpy as jnp
from jax import lax
from jax.experimental import pallas as pl
from jax.experimental.pallas import tpu as pltpu
from jax.sharding import PartitionSpec as P

SV_DEV = 128
EMB = 64
HALF = 32
SLOTS = 6
PAIRS = 3
BODY = PAIRS * HALF
ROWS = BODY + 16
DEVS = 128
GROUPS = 160
AHEAD = 4
ROUNDS = 7
MESH = pl.DeviceIdType.MESH


FEATURE_CHUNKS = ((0, 5), (5, 5), (10, 5), (15, 5))
HIDDEN_CHUNKS = ((0, 4), (4, 5), (9, 5), (14, 6))
LAST_CHUNKS = ((0, 3), (3, 5), (8, 5), (13, 7))
PER_EXCHANGE = 14


def halo_copies(own, side_z, side_y, chunks, base, send_sem, recv_sem):
    gz, xy = lax.axis_index("gz"), lax.axis_index("xy")
    depth, height = lax.axis_size("gz"), lax.axis_size("xy")
    plan = []
    for c, (first, length) in enumerate(chunks):
        rows = pl.ds(first, length)
        plan.append(((1, 0), own.at[3, rows], side_z.at[0, rows]))
        plan.append(((-1, 0), own.at[0, rows], side_z.at[1, rows]))
    plan.append(((0, 1), own.at[:, 19], side_y.at[0, pl.ds(1, 4)]))
    plan.append(((0, -1), own.at[:, 0], side_y.at[1, pl.ds(1, 4)]))
    plan.append(((1, 1), own.at[3, 19], side_y.at[0, 0]))
    plan.append(((1, -1), own.at[3, 0], side_y.at[1, 0]))
    plan.append(((-1, 1), own.at[0, 19], side_y.at[0, 5]))
    plan.append(((-1, -1), own.at[0, 0], side_y.at[1, 5]))
    copies = []
    for i, ((dz, dy), src, dst) in enumerate(plan):
        def inside(a, b):
            return (a >= 0) & (a < depth) & (b >= 0) & (b < height)

        copy = pltpu.make_async_remote_copy(
            src_ref=src,
            dst_ref=dst,
            send_sem=send_sem.at[base + i],
            recv_sem=recv_sem.at[base + i],
            device_id=(gz + dz, xy + dy),
            device_id_type=MESH,
        )
        copies.append((copy, inside(gz + dz, xy + dy), inside(gz - dz, xy - dy)))
    return copies


def start(entry):
    @pl.when(entry[1])
    def _():
        entry[0].start()


def arrive(entry):
    @pl.when(entry[2])
    def _():
        entry[0].wait_recv()


def leave(entry):
    @pl.when(entry[1])
    def _():
        entry[0].wait_send()


def main_kernel(
    own, raw1, b1, raw2, b2, lists_ref, labels_hbm, owner_hbm, got_ref, wide, hwide, hidden,
    fz, fy, hz, hy, part1, part2, emb_ref, send_ref, labels_ref, owner_ref, facts, scalars,
    rows_s, rows_v, table_v, table_ref, send_sem, recv_sem, far_send, far_recv, own_sem, here_sem,
    round_sem, w1, w2,
):
    gz, xy = lax.axis_index("gz"), lax.axis_index("xy")
    depth, height = lax.axis_size("gz"), lax.axis_size("xy")
    me = gz * 32 + xy
    barrier = pltpu.get_barrier_semaphore()
    labels_copy = pltpu.make_async_copy(labels_hbm, labels_ref, here_sem.at[0])
    owner_copy = pltpu.make_async_copy(owner_hbm, owner_ref, here_sem.at[1])
    labels_copy.start()
    owner_copy.start()

    for side, has in ((0, gz == 0), (1, gz == depth - 1)):
        @pl.when(has)
        def _():
            zeros = jnp.zeros(fz.shape[1:], fz.dtype)
            fz[side] = zeros
            hz[side] = zeros
            for s in range(2):
                fy[s, 5 * side] = jnp.zeros(fy.shape[2:], fy.dtype)
                hy[s, 5 * side] = jnp.zeros(fy.shape[2:], fy.dtype)

    for side, has in ((0, xy == 0), (1, xy == height - 1)):
        @pl.when(has)
        def _():
            fy[side] = jnp.zeros(fy.shape[1:], fy.dtype)
            hy[side] = jnp.zeros(fy.shape[1:], fy.dtype)

    lane = lax.broadcasted_iota(jnp.int32, (48, 256), 1)

    def put(ref, e, y, value):
        turned = value.astype(jnp.float32)
        left = jnp.where(lane == 0, 0.0, pltpu.roll(turned, 1, 1))
        right = jnp.where(lane == 255, 0.0, pltpu.roll(turned, 255, 1))
        ref[e, y, 0:48, :] = left.astype(jnp.bfloat16)
        ref[e, y, 48:96, :] = value
        ref[e, y, 96:144, :] = right.astype(jnp.bfloat16)

    near = [(a, b) for a in (-1, 0, 1) for b in (-1, 0, 1) if (a, b) != (0, 0)]
    for a, b in near:
        there = (gz + a >= 0) & (gz + a < depth) & (xy + b >= 0) & (xy + b < height)

        @pl.when(there)
        def _():
            pl.semaphore_signal(
                barrier, inc=1, device_id=(gz + a, xy + b), device_id_type=MESH
            )

    def across(r):
        bit = lax.rem(me // (1 << r), 2)
        return place(me + (1 - 2 * bit) * (1 << r))

    for r in range(ROUNDS):
        pl.semaphore_signal(barrier, inc=1, device_id=across(r), device_id_type=MESH)

    def tell(r):
        pl.semaphore_signal(
            round_sem.at[r], inc=1, device_id=across(r), device_id_type=MESH
        )

    def hear(r):
        pl.semaphore_wait(round_sem.at[r], 1)

    def fill(y, carry):
        for z in range(4):
            put(wide, z + 1, y + 1, own[z, y])
        return carry

    count = lists_ref.shape[0]
    lists = lists_ref[...]
    sizes = jnp.sum(jnp.where(lists >= 0, 1, 0), axis=1, keepdims=True)
    column = lax.broadcasted_iota(jnp.int32, lists.shape, 1)
    facts[...] = jnp.where(column == 0, lists, sizes).astype(jnp.float32).T[0:8, :].astype(jnp.int32)
    facts_copy = pltpu.make_async_copy(facts, scalars, here_sem.at[2])
    facts_copy.start()
    beside_z = jnp.where(gz > 0, 1, 0) + jnp.where(gz < depth - 1, 1, 0)
    beside_y = jnp.where(xy > 0, 1, 0) + jnp.where(xy < height - 1, 1, 0)
    pl.semaphore_wait(barrier, (1 + beside_z) * (1 + beside_y) - 1 + ROUNDS)

    first = halo_copies(own, fz, fy, FEATURE_CHUNKS, 0, send_sem, recv_sem)
    then = halo_copies(hidden, hz, hy, HIDDEN_CHUNKS, PER_EXCHANGE, send_sem, recv_sem)
    for entry in first[8:] + first[:8]:
        start(entry)
    tell(0)
    for raw, w, channels in ((raw1, w1, 48), (raw2, w2, 64)):
        for dz in range(3):
            w[dz * channels : (dz + 1) * channels, :] = jnp.concatenate(
                [raw[dz * 9 + t] for t in range(9)], axis=1
            )
    lax.fori_loop(0, 20, fill, 0)
    hear(0)
    tell(1)

    def slab(ref, e, y):
        return ref[e, pl.ds(y, 3)].reshape(432, 256)

    def product(w, ref, e, y, low, high, channels):
        r = jnp.dot(
            w[low * channels : (high + 1) * channels, :],
            slab(ref, e, y),
            preferred_element_type=jnp.float32,
        )
        return {
            e - dz: r[(dz - low) * channels : (dz - low + 1) * channels]
            for dz in range(low, high + 1)
        }

    def inner(w, ref, y, channels):
        total = {}
        for e, low, high in ((1, 0, 1), (2, 0, 2), (3, 0, 2), (4, 1, 2)):
            for z, v in product(w, ref, e, y, low, high, channels).items():
                total[z] = total[z] + v if z in total else v
        return total

    for entry in first[8:]:
        arrive(entry)
    hear(1)
    tell(2)

    def fill_side(e, carry):
        put(wide, e, 0, fy[0, e])
        put(wide, e, 21, fy[1, e])
        return carry

    lax.fori_loop(0, 6, fill_side, 0)

    def bias_of(ref, channels):
        line = jnp.concatenate([ref[...], jnp.zeros((1, 128 - channels), jnp.float32)], axis=1)
        tall = jnp.broadcast_to(line, (128, 128)).T[0:channels]
        return jnp.concatenate([tall, tall], axis=1)

    bias1 = bias_of(b1, 48)
    bias2 = bias_of(b2, 64)

    def keep_hidden(z, y, total):
        value = jnp.maximum(total + bias1, 0.0).astype(jnp.bfloat16)
        hidden[z, y] = value
        put(hwide, z + 1, y + 1, value)

    def first_inner(y, carry):
        total = inner(w1, wide, y, 48)
        part1[0, y] = total[0]
        part1[1, y] = total[3]
        keep_hidden(1, y, total[1])
        keep_hidden(2, y, total[2])
        return carry

    lax.fori_loop(0, 20, first_inner, 0, unroll=2)

    labels_copy.wait()
    owner_copy.wait()
    facts_copy.wait()

    def look(b, carry):
        at = scalars[0, b]
        run = at >> 8
        z = jnp.clip((run * 3277) >> 16, 0, 3)
        label = labels_ref[z, jnp.clip(run - z * 20, 0, 19), at & 255]
        rows_s[0, b] = owner_ref[label & (owner_ref.shape[0] - 1)]
        return carry

    lax.fori_loop(0, count, look, 0, unroll=8)
    rows_copy = pltpu.make_async_copy(rows_s, rows_v, here_sem.at[3])
    rows_copy.start()
    rows_copy.wait()
    line8 = lax.broadcasted_iota(jnp.int32, (8, count), 0)
    three = jnp.where(line8 == 2, jnp.broadcast_to(rows_v[0:1, :], (8, count)), facts[...])
    turned3 = jnp.concatenate(
        [three.astype(jnp.float32), jnp.zeros((120, count), jnp.float32)], axis=0
    ).T.astype(jnp.int32)
    row_of = turned3[:, 2:3]
    code = (turned3[:, 0:1] << 15) + (turned3[:, 1:2] << 7) + (row_of & 127)
    hit = (row_of >> 7) == lax.broadcasted_iota(jnp.int32, (count, DEVS), 1)
    before = lax.broadcasted_iota(jnp.int32, (count, count), 0) > lax.broadcasted_iota(
        jnp.int32, (count, count), 1
    )
    rank = jnp.dot(
        jnp.where(before, 1.0, 0.0).astype(jnp.bfloat16),
        jnp.where(hit, 1.0, 0.0).astype(jnp.bfloat16),
        preferred_element_type=jnp.float32,
    )
    rank = jnp.where(hit, rank, -1.0)
    slots = [
        jnp.sum(jnp.where(rank == float(k), code, 0), axis=0, keepdims=True)
        for k in range(SLOTS)
    ]
    table_v[...] = jnp.concatenate(slots + [slots[0], slots[0]], axis=0)
    table_copy = pltpu.make_async_copy(table_v, table_ref, here_sem.at[4])
    table_copy.start()

    def fill_z(y, carry):
        put(wide, 0, y + 1, fz[0, y])
        put(wide, 5, y + 1, fz[1, y])
        return carry

    def first_outer(y, carry):
        keep_hidden(0, y, part1[0, y] + product(w1, wide, 0, y, 0, 0, 48)[0])
        keep_hidden(3, y, part1[1, y] + product(w1, wide, 5, y, 2, 2, 48)[3])
        return carry

    for c in range(4):
        arrive(first[2 * c])
        arrive(first[2 * c + 1])
        low, length = FEATURE_CHUNKS[c]
        lax.fori_loop(low, low + length, fill_z, 0)
        low, length = HIDDEN_CHUNKS[c]
        lax.fori_loop(low, low + length, first_outer, 0)
        if c == 0:
            for i in (9, 11, 13):
                start(then[i])
        if c == 3:
            for i in (8, 10, 12):
                start(then[i])
        start(then[2 * c])
        start(then[2 * c + 1])
        hear(2 + c)
        tell(3 + c)

    arrive(then[8])
    arrive(then[9])
    hear(6)

    def hidden_side(e, carry):
        put(hwide, e, 0, hy[0, e])
        put(hwide, e, 21, hy[1, e])
        return carry

    lax.fori_loop(1, 5, hidden_side, 0)

    def keep(z, y, total):
        value = (total + bias2).astype(jnp.bfloat16)
        group = (z * 20 + y) * 2
        emb_ref[group] = value[:, 0:128]
        emb_ref[group + 1] = value[:, 128:256]

    def second_inner(y, carry):
        total = inner(w2, hwide, y, 64)
        part2[0, y] = total[0]
        part2[1, y] = total[3]
        keep(1, y, total[1])
        keep(2, y, total[2])
        return carry

    lax.fori_loop(0, 20, second_inner, 0, unroll=2)

    def hidden_z(y, carry):
        put(hwide, 0, y + 1, hz[0, y])
        put(hwide, 5, y + 1, hz[1, y])
        return carry

    def second_outer(y, carry):
        keep(0, y, part2[0, y] + product(w2, hwide, 0, y, 0, 0, 64)[0])
        keep(3, y, part2[1, y] + product(w2, hwide, 5, y, 2, 2, 64)[3])
        return carry

    for entry in then[10:]:
        arrive(entry)
    hidden_side(0, 0)
    hidden_side(5, 0)
    for c in range(4):
        arrive(then[2 * c])
        arrive(then[2 * c + 1])
        low, length = HIDDEN_CHUNKS[c]
        lax.fori_loop(low, low + length, hidden_z, 0)
        low, length = LAST_CHUNKS[c]
        lax.fori_loop(low, low + length, second_outer, 0)

    table_copy.wait()

    def copy(k):
        device = partner(me, k)
        return pltpu.make_async_remote_copy(
            src_ref=send_ref.at[device],
            dst_ref=got_ref.at[me],
            send_sem=far_send.at[k],
            recv_sem=far_recv.at[k],
            device_id=place(device),
            device_id_type=MESH,
        )

    for k in range(AHEAD):
        moments_of(emb_ref, table_ref, partner(me, k), send_ref)
    own_copy = pltpu.make_async_copy(send_ref.at[me], got_ref.at[me], own_sem)
    own_copy.start()
    for k in range(1, AHEAD):
        copy(k).start()

    def send(i, carry):
        for t in range(AHEAD):
            moments_of(emb_ref, table_ref, partner(me, i * AHEAD + t), send_ref)
        for t in range(AHEAD):
            copy(i * AHEAD + t).start()
        return carry

    lax.fori_loop(1, DEVS // AHEAD, send, 0)
    for entry in first + then:
        leave(entry)

    def finish(k, carry):
        copy(k).wait()
        return carry

    lax.fori_loop(1, DEVS, finish, 0)
    own_copy.wait()


def main(features, first_weight, first_bias, second_weight, second_bias, labels, blocks, owner_map):
    own = features.transpose(1, 2, 0, 3)
    w1 = first_weight.reshape(27, 48, 48)
    w2 = second_weight.reshape(27, 64, 48)
    bf, f32, i32 = jnp.bfloat16, jnp.float32, jnp.int32
    count = blocks.shape[0]
    return pl.pallas_call(
        main_kernel,
        out_shape=jax.ShapeDtypeStruct((DEVS, ROWS, 128), bf),
        in_specs=[pl.BlockSpec(memory_space=pltpu.VMEM)] * 6
        + [pl.BlockSpec(memory_space=pl.ANY)] * 2,
        out_specs=pl.BlockSpec(memory_space=pl.ANY),
        scratch_shapes=[
            pltpu.VMEM((6, 22, 144, 256), bf),
            pltpu.VMEM((6, 22, 144, 256), bf),
            pltpu.VMEM((4, 20, 48, 256), bf),
            pltpu.VMEM((2, 20, 48, 256), bf),
            pltpu.VMEM((2, 6, 48, 256), bf),
            pltpu.VMEM((2, 20, 48, 256), bf),
            pltpu.VMEM((2, 6, 48, 256), bf),
            pltpu.VMEM((2, 20, 48, 256), f32),
            pltpu.VMEM((2, 20, 64, 256), f32),
            pltpu.VMEM((GROUPS, EMB, 128), bf),
            pltpu.VMEM((DEVS, ROWS, 128), bf),
            pltpu.SMEM(labels.shape, i32),
            pltpu.SMEM(owner_map.shape, i32),
            pltpu.VMEM((8, count), i32),
            pltpu.SMEM((8, count), i32),
            pltpu.SMEM((8, count), i32),
            pltpu.VMEM((8, count), i32),
            pltpu.VMEM((8, DEVS), i32),
            pltpu.SMEM((8, DEVS), i32),
            pltpu.SemaphoreType.DMA((2 * PER_EXCHANGE,)),
            pltpu.SemaphoreType.DMA((2 * PER_EXCHANGE,)),
            pltpu.SemaphoreType.DMA((DEVS,)),
            pltpu.SemaphoreType.DMA((DEVS,)),
            pltpu.SemaphoreType.DMA,
            pltpu.SemaphoreType.DMA((5,)),
            pltpu.SemaphoreType.REGULAR((ROUNDS,)),
            pltpu.VMEM((144, 432), bf),
            pltpu.VMEM((192, 432), bf),
        ],
        compiler_params=pltpu.CompilerParams(
            collective_id=0, has_side_effects=True, vmem_limit_bytes=52 << 20
        ),
    )(own, w1, first_bias[None], w2, second_bias[None], blocks, labels, owner_map)


def place(device):
    return (device // 32, lax.rem(device, 32))


def partner(me, k):
    core, x, y, z = lax.rem(me, 2), lax.rem(me // 2, 4), lax.rem(me // 8, 4), me // 32
    kc, kx, ky, kz = lax.rem(k, 2), lax.rem(k // 2, 4), lax.rem(k // 8, 4), k // 32
    ky = lax.rem(ky + kx, 4)
    kz = lax.rem(kz + kx + ky, 4)
    there = (lax.rem(z + kz, 4) * 4 + lax.rem(y + ky, 4)) * 4 + lax.rem(x + kx, 4)
    return there * 2 + lax.rem(core + kc, 2)


def moments_of(emb_ref, table_ref, device, send_ref):
    lane = lax.broadcasted_iota(jnp.int32, (1, 128), 1)
    inner = lax.broadcasted_iota(jnp.int32, (HALF, 128), 1) & 63
    outer = lax.broadcasted_iota(jnp.int32, (HALF, 128), 0)
    upper = (inner >= HALF) | (inner >= outer)
    diagonal = inner == outer
    line = lax.broadcasted_iota(jnp.int32, (16, 128), 0)
    one = jnp.ones((EMB, 256), jnp.bfloat16)
    near = lax.broadcasted_iota(jnp.int32, (EMB, 128), 1) < EMB
    extras = jnp.zeros((16, 128), jnp.float32)
    for p in range(PAIRS):
        parts, sizes, rows = [], [], []
        for h in range(2):
            code = table_ref[2 * p + h, device]
            start = code >> 15
            size = (code >> 7) & 255
            rows.append((code & 127).astype(jnp.float32))
            sizes.append(size.astype(jnp.float32))
            group = jnp.clip(start >> 7, 0, GROUPS - 1)
            low = start & 127
            first = emb_ref[group]
            second = emb_ref[jnp.minimum(group + 1, GROUPS - 1)]
            in_first = jnp.where((lane >= low) & (lane < low + size), 1.0, 0.0).astype(jnp.bfloat16)
            in_second = jnp.where(lane + 128 < low + size, 1.0, 0.0).astype(jnp.bfloat16)
            mask_rows = jnp.broadcast_to(jnp.concatenate([in_first, in_second], axis=1), (16, 256))
            whole = jnp.concatenate([first, second], axis=1)
            left = jnp.concatenate([jnp.concatenate([first * in_first, second * in_second], axis=1), mask_rows], axis=0)
            right = jnp.concatenate([whole, one] if h == 0 else [one, whole], axis=0)
            parts.append(lax.dot_general(left, right, (((1,), (1,)), ((), ())), preferred_element_type=jnp.float32))
        size_row = jnp.where(lane < EMB, sizes[0], sizes[1])
        owner_row = jnp.where(lane < EMB, rows[0], rows[1])
        second_row = jnp.where(near[0:1], parts[0][EMB : EMB + 1], parts[1][EMB : EMB + 1])
        mean = second_row / jnp.maximum(size_row, 1.0)
        square = jnp.where(near, parts[0][0:EMB], parts[1][0:EMB])
        column = pltpu.roll(jnp.where(near, parts[1][0:EMB], parts[0][0:EMB]), EMB, 1)
        centred = square - column * mean
        rolled = pltpu.roll(centred[HALF:EMB], 96, 1)
        packed = jnp.where(upper, centred[0:HALF], rolled)
        send_ref[device, p * HALF : (p + 1) * HALF, :] = packed.astype(jnp.bfloat16)
        diag = jnp.sum(jnp.where(diagonal, rolled, 0.0), axis=0, keepdims=True)
        high = mean.astype(jnp.bfloat16).astype(jnp.float32)
        for place_of, value in (
            (p, diag),
            (3 + p, high),
            (6 + p, mean - high),
            (9 + p, size_row),
            (12 + p, owner_row),
        ):
            extras = jnp.where(line == place_of, value, extras)
    send_ref[device, BODY:ROWS, :] = extras.astype(jnp.bfloat16)


CHUNKS = 4
QUAD = 4


def total_kernel(
    got_ref, mean_ref, cov_ref, body, extra, lines, acc_a, acc_b, id_vec, ids, hits, spread,
    second, full, body_sem, extra_sem, id_sem,
):
    fast = lax.Precision.HIGHEST
    per = DEVS // CHUNKS
    extra_copy = pltpu.make_async_copy(got_ref.at[:, pl.ds(BODY, 16), :], extra, extra_sem)
    extra_copy.start()
    body_copies = [
        pltpu.make_async_copy(
            got_ref.at[pl.ds(c * per, per), pl.ds(0, BODY), :],
            body.at[pl.ds(c * per, per)],
            body_sem.at[c],
        )
        for c in range(CHUNKS)
    ]
    for one in body_copies:
        one.start()
    acc_a[...] = jnp.zeros_like(acc_a)
    acc_b[...] = jnp.zeros_like(acc_b)
    extra_copy.wait()
    lines[...] = extra[...].astype(jnp.float32).reshape(DEVS * 16, 128)

    def line(k):
        return lines[pl.ds(k, DEVS, stride=16), :]

    lane = lax.broadcasted_iota(jnp.int32, (DEVS, 128), 1)
    row = lax.broadcasted_iota(jnp.int32, (DEVS, 128), 0)
    inner = lane & 63
    owners = [line(12 + p) for p in range(PAIRS)]
    id_vec[...] = jnp.where(
        inner == 0, owners[0], jnp.where(inner == 1, owners[1], owners[2])
    ).astype(jnp.int32)
    id_copy = pltpu.make_async_copy(id_vec, ids, id_sem)
    id_copy.start()

    means, sizes = [], []
    sums = jnp.zeros((DEVS, 384), jnp.float32)
    for p in range(PAIRS):
        mean = line(3 + p) + line(6 + p)
        size = line(9 + p)
        means.append(mean)
        sizes.append(size)
        turned = owners[p].T
        for h in range(2):
            hit = jnp.where(row == turned[64 * h : 64 * h + 1, :].astype(jnp.int32), 1.0, 0.0)
            hits[:, (2 * p + h) * 128 : (2 * p + h + 1) * 128] = hit
            mine = (lane >= EMB) if h else (lane < EMB)
            values = jnp.concatenate(
                [
                    jnp.where(mine, size * mean, 0.0),
                    jnp.where(mine, size, 0.0),
                    jnp.where(mine, line(p), 0.0),
                ],
                axis=1,
            )
            sums = sums + jnp.dot(
                hit, values, preferred_element_type=jnp.float32, precision=fast
            )

    def folded(value):
        return value + pltpu.roll(value, EMB, 1)

    count = jnp.maximum(folded(sums[:, 128:256]), 1.0)
    total_mean = folded(sums[:, 0:128]) / count
    mean_ref[...] = total_mean[:, 0:EMB]
    diag_sum = folded(sums[:, 256:384])
    inverse = 1.0 / count
    lines[0:DEVS, :] = diag_sum
    lines[DEVS : 2 * DEVS, :] = inverse

    for p in range(PAIRS):
        for h in range(2):
            owner = owners[p]
            other = pltpu.roll(owner, EMB, 1)
            owner_all = (
                jnp.where(lane < EMB, other, owner) if h else jnp.where(lane < EMB, owner, other)
            )
            hit_t = jnp.where(owner_all.astype(jnp.int32) == lane, 1.0, 0.0)
            theirs = jnp.dot(
                hit_t, total_mean, preferred_element_type=jnp.float32, precision=fast
            )
            off = jnp.sqrt(sizes[p]) * (means[p] - theirs)
            if h:
                off = pltpu.roll(off, EMB, 1)
            off = jnp.where(lane < EMB, off, 0.0)
            k = 2 * p + h
            second[k * 128 : (k + 1) * 128, :] = off.astype(jnp.bfloat16)
            spread[:, k * 128 : (k + 1) * 128] = off.T[0:EMB, :].astype(jnp.bfloat16)

    id_copy.wait()
    for c in range(CHUNKS):
        body_copies[c].wait()

        def add(s, carry):
            for p in range(PAIRS):
                value = body[s, p * HALF : (p + 1) * HALF, :].astype(jnp.float32)
                a = ids[s, p]
                b = ids[s, 64 + p]
                acc_a[a] = acc_a[a] + value
                acc_b[b] = acc_b[b] + value
            return carry

        lax.fori_loop(c * per, (c + 1) * per, add, 0, unroll=2)

    lane32 = lax.broadcasted_iota(jnp.int32, (HALF, 128), 1)
    row32 = lax.broadcasted_iota(jnp.int32, (HALF, 128), 0)

    def quad(q, carry):
        base = q * QUAD
        left = []
        for t in range(QUAD):
            mask = hits[pl.ds(base + t, 1), :].astype(jnp.bfloat16)
            left.append(spread[...] * mask)
        between = jnp.dot(
            jnp.concatenate(left, axis=0), second[...], preferred_element_type=jnp.float32
        )
        packed = [
            acc_a[base + t] + pltpu.roll(acc_b[base + t], EMB, 1) for t in range(QUAD)
        ]
        turned = jnp.concatenate(packed, axis=0).T
        for t in range(QUAD):
            diag = lines[pl.ds(base + t, 1), :]
            inv = lines[pl.ds(DEVS + base + t, 1), :]
            flip = pltpu.roll(turned, (128 - HALF * t) % 128, 1) if t else turned
            flip_up, flip_down = flip[0:HALF], flip[HALF:EMB]
            here = packed[t]
            top = jnp.where((lane32 >= HALF) | (lane32 >= row32), here, flip_up)
            low = jnp.where(
                lane32 < row32, here, jnp.where(lane32 == row32, diag, flip_up)
            )
            bottom = jnp.where(lane32 < HALF, flip_down, pltpu.roll(low, HALF, 1))
            both = jnp.concatenate([top, bottom], axis=0)
            both = (both + between[t * EMB : (t + 1) * EMB]) * inv
            full[pl.ds((base + t) * EMB, EMB), :] = both
        return carry

    lax.fori_loop(0, SV_DEV // QUAD, quad, 0)

    for t in range(EMB // 2):
        even = full[pl.ds(2 * t, SV_DEV, stride=EMB), :]
        odd = full[pl.ds(2 * t + 1, SV_DEV, stride=EMB), :]
        cov_ref[:, t * 128 : (t + 1) * 128] = jnp.where(
            lane < EMB, even, pltpu.roll(odd, EMB, 1)
        )


def totals(got):
    return pl.pallas_call(
        total_kernel,
        out_shape=(
            jax.ShapeDtypeStruct((SV_DEV, EMB), jnp.float32),
            jax.ShapeDtypeStruct((SV_DEV, EMB * EMB), jnp.float32),
        ),
        in_specs=[pl.BlockSpec(memory_space=pl.ANY)],
        out_specs=(
            pl.BlockSpec(memory_space=pltpu.VMEM),
            pl.BlockSpec(memory_space=pltpu.VMEM),
        ),
        scratch_shapes=[
            pltpu.VMEM((DEVS, BODY, 128), jnp.bfloat16),
            pltpu.VMEM((DEVS, 16, 128), jnp.bfloat16),
            pltpu.VMEM((DEVS * 16, 128), jnp.float32),
            pltpu.VMEM((SV_DEV, HALF, 128), jnp.float32),
            pltpu.VMEM((SV_DEV, HALF, 128), jnp.float32),
            pltpu.VMEM((DEVS, 128), jnp.int32),
            pltpu.SMEM((DEVS, 128), jnp.int32),
            pltpu.VMEM((SV_DEV, DEVS * SLOTS), jnp.float32),
            pltpu.VMEM((EMB, DEVS * SLOTS), jnp.bfloat16),
            pltpu.VMEM((DEVS * SLOTS, 128), jnp.bfloat16),
            pltpu.VMEM((SV_DEV * EMB, 128), jnp.float32),
            pltpu.SemaphoreType.DMA((CHUNKS,)),
            pltpu.SemaphoreType.DMA,
            pltpu.SemaphoreType.DMA,
        ],
        compiler_params=pltpu.CompilerParams(vmem_limit_bytes=60 << 20),
    )(got)


def local(
    features, first_weight, first_bias, second_weight, second_bias, labels, blocks, owner_map
):
    got = main(
        features,
        first_weight,
        first_bias,
        second_weight,
        second_bias,
        labels,
        blocks.reshape(blocks.shape[2], blocks.shape[3]),
        owner_map,
    )
    return totals(got)


def solution(mesh):
    return jax.shard_map(
        local,
        mesh=mesh,
        in_specs=(
            P(None, "gz", "xy", None),
            P(),
            P(),
            P(),
            P(),
            P("gz", "xy", None),
            P("gz", "xy", None, None),
            P(),
        ),
        out_specs=(P(("gz", "xy"), None), P(("gz", "xy"), None)),
        check_vma=False,
    )
```

```python
import functools

import jax
import jax.numpy as jnp
from jax import lax
from jax.experimental import pallas as pl
from jax.experimental.pallas import tpu as pltpu
from jax.sharding import PartitionSpec as P

SV_DEV = 128
EMB = 64
HALF = 32
SLOTS = 6
PAIRS = 3
BODY = PAIRS * HALF
ROWS = BODY + 16
DEVS = 128
GROUPS = 160
AHEAD = 4
ROUNDS = 7
MESH = pl.DeviceIdType.MESH


FEATURE_CHUNKS = ((0, 5), (5, 5), (10, 5), (15, 5))
HIDDEN_CHUNKS = ((0, 4), (4, 5), (9, 5), (14, 6))
LAST_CHUNKS = ((0, 3), (3, 5), (8, 5), (13, 7))
PER_EXCHANGE = 14


def halo_copies(own, side_z, side_y, chunks, base, send_sem, recv_sem):
    gz, xy = lax.axis_index("gz"), lax.axis_index("xy")
    depth, height = lax.axis_size("gz"), lax.axis_size("xy")
    plan = []
    for c, (first, length) in enumerate(chunks):
        rows = pl.ds(first, length)
        plan.append(((1, 0), own.at[3, rows], side_z.at[0, rows]))
        plan.append(((-1, 0), own.at[0, rows], side_z.at[1, rows]))
    plan.append(((0, 1), own.at[:, 19], side_y.at[0, pl.ds(1, 4)]))
    plan.append(((0, -1), own.at[:, 0], side_y.at[1, pl.ds(1, 4)]))
    plan.append(((1, 1), own.at[3, 19], side_y.at[0, 0]))
    plan.append(((1, -1), own.at[3, 0], side_y.at[1, 0]))
    plan.append(((-1, 1), own.at[0, 19], side_y.at[0, 5]))
    plan.append(((-1, -1), own.at[0, 0], side_y.at[1, 5]))
    copies = []
    for i, ((dz, dy), src, dst) in enumerate(plan):
        def inside(a, b):
            return (a >= 0) & (a < depth) & (b >= 0) & (b < height)

        copy = pltpu.make_async_remote_copy(
            src_ref=src,
            dst_ref=dst,
            send_sem=send_sem.at[base + i],
            recv_sem=recv_sem.at[base + i],
            device_id=(gz + dz, xy + dy),
            device_id_type=MESH,
        )
        copies.append((copy, inside(gz + dz, xy + dy), inside(gz - dz, xy - dy)))
    return copies


def start(entry):
    @pl.when(entry[1])
    def _():
        entry[0].start()


def arrive(entry):
    @pl.when(entry[2])
    def _():
        entry[0].wait_recv()


def leave(entry):
    @pl.when(entry[1])
    def _():
        entry[0].wait_send()


def main_kernel(
    own, raw1, b1, raw2, b2, lists_ref, labels_hbm, owner_hbm, got_ref, wide, hwide, hidden,
    fz, fy, hz, hy, part1, part2, emb_ref, send_ref, labels_ref, owner_ref, facts, scalars,
    rows_s, rows_v, table_v, table_ref, send_sem, recv_sem, far_send, far_recv, own_sem, here_sem,
    round_sem, w1, w2,
):
    gz, xy = lax.axis_index("gz"), lax.axis_index("xy")
    depth, height = lax.axis_size("gz"), lax.axis_size("xy")
    me = gz * 32 + xy
    barrier = pltpu.get_barrier_semaphore()
    labels_copy = pltpu.make_async_copy(labels_hbm, labels_ref, here_sem.at[0])
    owner_copy = pltpu.make_async_copy(owner_hbm, owner_ref, here_sem.at[1])
    labels_copy.start()
    owner_copy.start()

    for side, has in ((0, gz == 0), (1, gz == depth - 1)):
        @pl.when(has)
        def _():
            zeros = jnp.zeros(fz.shape[1:], fz.dtype)
            fz[side] = zeros
            hz[side] = zeros
            for s in range(2):
                fy[s, 5 * side] = jnp.zeros(fy.shape[2:], fy.dtype)
                hy[s, 5 * side] = jnp.zeros(fy.shape[2:], fy.dtype)

    for side, has in ((0, xy == 0), (1, xy == height - 1)):
        @pl.when(has)
        def _():
            fy[side] = jnp.zeros(fy.shape[1:], fy.dtype)
            hy[side] = jnp.zeros(fy.shape[1:], fy.dtype)

    lane = lax.broadcasted_iota(jnp.int32, (48, 256), 1)

    def put(ref, e, y, value):
        turned = value.astype(jnp.float32)
        left = jnp.where(lane == 0, 0.0, pltpu.roll(turned, 1, 1))
        right = jnp.where(lane == 255, 0.0, pltpu.roll(turned, 255, 1))
        ref[e, y, 0:48, :] = left.astype(jnp.bfloat16)
        ref[e, y, 48:96, :] = value
        ref[e, y, 96:144, :] = right.astype(jnp.bfloat16)

    near = [(a, b) for a in (-1, 0, 1) for b in (-1, 0, 1) if (a, b) != (0, 0)]
    for a, b in near:
        there = (gz + a >= 0) & (gz + a < depth) & (xy + b >= 0) & (xy + b < height)

        @pl.when(there)
        def _():
            pl.semaphore_signal(
                barrier, inc=1, device_id=(gz + a, xy + b), device_id_type=MESH
            )

    def across(r):
        bit = lax.rem(me // (1 << r), 2)
        return place(me + (1 - 2 * bit) * (1 << r))

    for r in range(ROUNDS):
        pl.semaphore_signal(barrier, inc=1, device_id=across(r), device_id_type=MESH)

    def tell(r):
        pl.semaphore_signal(
            round_sem.at[r], inc=1, device_id=across(r), device_id_type=MESH
        )

    def hear(r):
        pl.semaphore_wait(round_sem.at[r], 1)

    def fill(y, carry):
        for z in range(4):
            put(wide, z + 1, y + 1, own[z, y])
        return carry

    count = lists_ref.shape[0]
    lists = lists_ref[...]
    sizes = jnp.sum(jnp.where(lists >= 0, 1, 0), axis=1, keepdims=True)
    column = lax.broadcasted_iota(jnp.int32, lists.shape, 1)
    facts[...] = jnp.where(column == 0, lists, sizes).astype(jnp.float32).T[0:8, :].astype(jnp.int32)
    facts_copy = pltpu.make_async_copy(facts, scalars, here_sem.at[2])
    facts_copy.start()
    beside_z = jnp.where(gz > 0, 1, 0) + jnp.where(gz < depth - 1, 1, 0)
    beside_y = jnp.where(xy > 0, 1, 0) + jnp.where(xy < height - 1, 1, 0)
    pl.semaphore_wait(barrier, (1 + beside_z) * (1 + beside_y) - 1 + ROUNDS)

    first = halo_copies(own, fz, fy, FEATURE_CHUNKS, 0, send_sem, recv_sem)
    then = halo_copies(hidden, hz, hy, HIDDEN_CHUNKS, PER_EXCHANGE, send_sem, recv_sem)
    for entry in first[8:] + first[:8]:
        start(entry)
    tell(0)
    for raw, w, channels in ((raw1, w1, 48), (raw2, w2, 64)):
        for dz in range(3):
            w[dz * channels : (dz + 1) * channels, :] = jnp.concatenate(
                [raw[dz * 9 + t] for t in range(9)], axis=1
            )
    lax.fori_loop(0, 20, fill, 0)
    hear(0)
    tell(1)

    def slab(ref, e, y):
        return ref[e, pl.ds(y, 3)].reshape(432, 256)

    def product(w, ref, e, y, low, high, channels):
        r = jnp.dot(
            w[low * channels : (high + 1) * channels, :],
            slab(ref, e, y),
            preferred_element_type=jnp.float32,
        )
        return {
            e - dz: r[(dz - low) * channels : (dz - low + 1) * channels]
            for dz in range(low, high + 1)
        }

    def inner(w, ref, y, channels):
        total = {}
        for e, low, high in ((1, 0, 1), (2, 0, 2), (3, 0, 2), (4, 1, 2)):
            for z, v in product(w, ref, e, y, low, high, channels).items():
                total[z] = total[z] + v if z in total else v
        return total

    for entry in first[8:]:
        arrive(entry)
    hear(1)
    tell(2)

    def fill_side(e, carry):
        put(wide, e, 0, fy[0, e])
        put(wide, e, 21, fy[1, e])
        return carry

    lax.fori_loop(0, 6, fill_side, 0)

    def bias_of(ref, channels):
        line = jnp.concatenate([ref[...], jnp.zeros((1, 128 - channels), jnp.float32)], axis=1)
        tall = jnp.broadcast_to(line, (128, 128)).T[0:channels]
        return jnp.concatenate([tall, tall], axis=1)

    bias1 = bias_of(b1, 48)
    bias2 = bias_of(b2, 64)

    def keep_hidden(z, y, total):
        value = jnp.maximum(total + bias1, 0.0).astype(jnp.bfloat16)
        hidden[z, y] = value
        put(hwide, z + 1, y + 1, value)

    labels_copy.wait()
    owner_copy.wait()
    facts_copy.wait()

    def look(b):
        at = scalars[0, b]
        run = at >> 8
        z = jnp.clip((run * 3277) >> 16, 0, 3)
        label = labels_ref[z, jnp.clip(run - z * 20, 0, 19), at & 255]
        rows_s[0, b] = owner_ref[label & (owner_ref.shape[0] - 1)]

    each = -(-count // 20)

    def first_inner(y, carry):
        for t in range(each):
            look(jnp.minimum(y * each + t, count - 1))
        total = inner(w1, wide, y, 48)
        part1[0, y] = total[0]
        part1[1, y] = total[3]
        keep_hidden(1, y, total[1])
        keep_hidden(2, y, total[2])
        return carry

    lax.fori_loop(0, 20, first_inner, 0, unroll=4)

    def fill_z(y, carry):
        put(wide, 0, y + 1, fz[0, y])
        put(wide, 5, y + 1, fz[1, y])
        return carry

    def first_outer(y, carry):
        keep_hidden(0, y, part1[0, y] + product(w1, wide, 0, y, 0, 0, 48)[0])
        keep_hidden(3, y, part1[1, y] + product(w1, wide, 5, y, 2, 2, 48)[3])
        return carry

    for c in range(4):
        arrive(first[2 * c])
        arrive(first[2 * c + 1])
        low, length = FEATURE_CHUNKS[c]
        lax.fori_loop(low, low + length, fill_z, 0, unroll=length)
        low, length = HIDDEN_CHUNKS[c]
        lax.fori_loop(low, low + length, first_outer, 0, unroll=length)
        if c == 0:
            for i in (9, 11, 13):
                start(then[i])
        if c == 3:
            for i in (8, 10, 12):
                start(then[i])
        start(then[2 * c])
        start(then[2 * c + 1])
        hear(2 + c)
        tell(3 + c)

    rows_copy = pltpu.make_async_copy(rows_s, rows_v, here_sem.at[3])
    rows_copy.start()
    rows_copy.wait()
    line8 = lax.broadcasted_iota(jnp.int32, (8, count), 0)
    three = jnp.where(line8 == 2, jnp.broadcast_to(rows_v[0:1, :], (8, count)), facts[...])
    turned3 = jnp.concatenate(
        [three.astype(jnp.float32), jnp.zeros((120, count), jnp.float32)], axis=0
    ).T.astype(jnp.int32)
    row_of = turned3[:, 2:3]
    code = (turned3[:, 0:1] << 15) + (turned3[:, 1:2] << 7) + (row_of & 127)
    hit = (row_of >> 7) == lax.broadcasted_iota(jnp.int32, (count, DEVS), 1)
    before = lax.broadcasted_iota(jnp.int32, (count, count), 0) > lax.broadcasted_iota(
        jnp.int32, (count, count), 1
    )
    rank = jnp.dot(
        jnp.where(before, 1.0, 0.0).astype(jnp.bfloat16),
        jnp.where(hit, 1.0, 0.0).astype(jnp.bfloat16),
        preferred_element_type=jnp.float32,
    )
    rank = jnp.where(hit, rank, -1.0)
    slots = [
        jnp.sum(jnp.where(rank == float(k), code, 0), axis=0, keepdims=True)
        for k in range(SLOTS)
    ]
    table_v[...] = jnp.concatenate(slots + [slots[0], slots[0]], axis=0)
    table_copy = pltpu.make_async_copy(table_v, table_ref, here_sem.at[4])
    table_copy.start()

    arrive(then[8])
    arrive(then[9])
    hear(6)

    def hidden_side(e, carry):
        put(hwide, e, 0, hy[0, e])
        put(hwide, e, 21, hy[1, e])
        return carry

    lax.fori_loop(1, 5, hidden_side, 0)

    def keep(z, y, total):
        value = (total + bias2).astype(jnp.bfloat16)
        group = (z * 20 + y) * 2
        emb_ref[group] = value[:, 0:128]
        emb_ref[group + 1] = value[:, 128:256]

    def second_inner(y, carry):
        total = inner(w2, hwide, y, 64)
        part2[0, y] = total[0]
        part2[1, y] = total[3]
        keep(1, y, total[1])
        keep(2, y, total[2])
        return carry

    lax.fori_loop(0, 20, second_inner, 0, unroll=4)

    def hidden_z(y, carry):
        put(hwide, 0, y + 1, hz[0, y])
        put(hwide, 5, y + 1, hz[1, y])
        return carry

    def second_outer(y, carry):
        keep(0, y, part2[0, y] + product(w2, hwide, 0, y, 0, 0, 64)[0])
        keep(3, y, part2[1, y] + product(w2, hwide, 5, y, 2, 2, 64)[3])
        return carry

    for entry in then[10:]:
        arrive(entry)
    hidden_side(0, 0)
    hidden_side(5, 0)
    for c in range(4):
        arrive(then[2 * c])
        arrive(then[2 * c + 1])
        low, length = HIDDEN_CHUNKS[c]
        lax.fori_loop(low, low + length, hidden_z, 0, unroll=length)
        low, length = LAST_CHUNKS[c]
        lax.fori_loop(low, low + length, second_outer, 0, unroll=length)

    table_copy.wait()

    def copy(k):
        device = partner(me, k)
        return pltpu.make_async_remote_copy(
            src_ref=send_ref.at[device],
            dst_ref=got_ref.at[me],
            send_sem=far_send.at[k],
            recv_sem=far_recv.at[k],
            device_id=place(device),
            device_id_type=MESH,
        )

    for k in range(AHEAD):
        moments_of(emb_ref, table_ref, partner(me, k), send_ref)
    own_copy = pltpu.make_async_copy(send_ref.at[me], got_ref.at[me], own_sem)
    own_copy.start()
    for k in range(1, AHEAD):
        copy(k).start()

    def send(i, carry):
        for t in range(AHEAD):
            moments_of(emb_ref, table_ref, partner(me, i * AHEAD + t), send_ref)
        for t in range(AHEAD):
            copy(i * AHEAD + t).start()
        return carry

    lax.fori_loop(1, DEVS // AHEAD, send, 0)
    for entry in first + then:
        leave(entry)

    def finish(k, carry):
        copy(k).wait()
        return carry

    lax.fori_loop(1, DEVS, finish, 0)
    own_copy.wait()


def main(features, first_weight, first_bias, second_weight, second_bias, labels, blocks, owner_map):
    own = features.transpose(1, 2, 0, 3)
    w1 = first_weight.reshape(27, 48, 48)
    w2 = second_weight.reshape(27, 64, 48)
    bf, f32, i32 = jnp.bfloat16, jnp.float32, jnp.int32
    count = blocks.shape[0]
    return pl.pallas_call(
        main_kernel,
        out_shape=jax.ShapeDtypeStruct((DEVS, ROWS, 128), bf),
        in_specs=[pl.BlockSpec(memory_space=pltpu.VMEM)] * 6
        + [pl.BlockSpec(memory_space=pl.ANY)] * 2,
        out_specs=pl.BlockSpec(memory_space=pl.ANY),
        scratch_shapes=[
            pltpu.VMEM((6, 22, 144, 256), bf),
            pltpu.VMEM((6, 22, 144, 256), bf),
            pltpu.VMEM((4, 20, 48, 256), bf),
            pltpu.VMEM((2, 20, 48, 256), bf),
            pltpu.VMEM((2, 6, 48, 256), bf),
            pltpu.VMEM((2, 20, 48, 256), bf),
            pltpu.VMEM((2, 6, 48, 256), bf),
            pltpu.VMEM((2, 20, 48, 256), f32),
            pltpu.VMEM((2, 20, 64, 256), f32),
            pltpu.VMEM((GROUPS, EMB, 128), bf),
            pltpu.VMEM((DEVS, ROWS, 128), bf),
            pltpu.SMEM(labels.shape, i32),
            pltpu.SMEM(owner_map.shape, i32),
            pltpu.VMEM((8, count), i32),
            pltpu.SMEM((8, count), i32),
            pltpu.SMEM((8, count), i32),
            pltpu.VMEM((8, count), i32),
            pltpu.VMEM((8, DEVS), i32),
            pltpu.SMEM((8, DEVS), i32),
            pltpu.SemaphoreType.DMA((2 * PER_EXCHANGE,)),
            pltpu.SemaphoreType.DMA((2 * PER_EXCHANGE,)),
            pltpu.SemaphoreType.DMA((DEVS,)),
            pltpu.SemaphoreType.DMA((DEVS,)),
            pltpu.SemaphoreType.DMA,
            pltpu.SemaphoreType.DMA((5,)),
            pltpu.SemaphoreType.REGULAR((ROUNDS,)),
            pltpu.VMEM((144, 432), bf),
            pltpu.VMEM((192, 432), bf),
        ],
        compiler_params=pltpu.CompilerParams(
            collective_id=0, has_side_effects=True, vmem_limit_bytes=52 << 20
        ),
    )(own, w1, first_bias[None], w2, second_bias[None], blocks, labels, owner_map)


def place(device):
    return (device // 32, lax.rem(device, 32))


def partner(me, k):
    core, x, y, z = lax.rem(me, 2), lax.rem(me // 2, 4), lax.rem(me // 8, 4), me // 32
    kc, kx, ky, kz = k // 64, lax.rem(k, 4), lax.rem(k // 4, 4), lax.rem(k // 16, 4)
    ky = lax.rem(ky + kx, 4)
    kz = lax.rem(kz + kx + ky, 4)
    there = (lax.rem(z + kz, 4) * 4 + lax.rem(y + ky, 4)) * 4 + lax.rem(x + kx, 4)
    return there * 2 + lax.rem(core + kc, 2)


def moments_of(emb_ref, table_ref, device, send_ref):
    lane = lax.broadcasted_iota(jnp.int32, (1, 128), 1)
    inner = lax.broadcasted_iota(jnp.int32, (HALF, 128), 1) & 63
    outer = lax.broadcasted_iota(jnp.int32, (HALF, 128), 0)
    upper = (inner >= HALF) | (inner >= outer)
    diagonal = inner == outer
    line = lax.broadcasted_iota(jnp.int32, (16, 128), 0)
    one = jnp.ones((EMB, 256), jnp.bfloat16)
    near = lax.broadcasted_iota(jnp.int32, (EMB, 128), 1) < EMB
    extras = jnp.zeros((16, 128), jnp.float32)
    for p in range(PAIRS):
        parts, sizes, rows = [], [], []
        for h in range(2):
            code = table_ref[2 * p + h, device]
            start = code >> 15
            size = (code >> 7) & 255
            rows.append((code & 127).astype(jnp.float32))
            sizes.append(size.astype(jnp.float32))
            group = jnp.clip(start >> 7, 0, GROUPS - 1)
            low = start & 127
            first = emb_ref[group]
            second = emb_ref[jnp.minimum(group + 1, GROUPS - 1)]
            in_first = jnp.where((lane >= low) & (lane < low + size), 1.0, 0.0).astype(jnp.bfloat16)
            in_second = jnp.where(lane + 128 < low + size, 1.0, 0.0).astype(jnp.bfloat16)
            mask_rows = jnp.broadcast_to(jnp.concatenate([in_first, in_second], axis=1), (16, 256))
            whole = jnp.concatenate([first, second], axis=1)
            left = jnp.concatenate([jnp.concatenate([first * in_first, second * in_second], axis=1), mask_rows], axis=0)
            right = jnp.concatenate([whole, one] if h == 0 else [one, whole], axis=0)
            parts.append(lax.dot_general(left, right, (((1,), (1,)), ((), ())), preferred_element_type=jnp.float32))
        size_row = jnp.where(lane < EMB, sizes[0], sizes[1])
        owner_row = jnp.where(lane < EMB, rows[0], rows[1])
        second_row = jnp.where(near[0:1], parts[0][EMB : EMB + 1], parts[1][EMB : EMB + 1])
        mean = second_row / jnp.maximum(size_row, 1.0)
        square = jnp.where(near, parts[0][0:EMB], parts[1][0:EMB])
        column = pltpu.roll(jnp.where(near, parts[1][0:EMB], parts[0][0:EMB]), EMB, 1)
        centred = square - column * mean
        rolled = pltpu.roll(centred[HALF:EMB], 96, 1)
        packed = jnp.where(upper, centred[0:HALF], rolled)
        send_ref[device, p * HALF : (p + 1) * HALF, :] = packed.astype(jnp.bfloat16)
        diag = jnp.sum(jnp.where(diagonal, rolled, 0.0), axis=0, keepdims=True)
        high = mean.astype(jnp.bfloat16).astype(jnp.float32)
        for place_of, value in (
            (p, diag),
            (3 + p, high),
            (6 + p, mean - high),
            (9 + p, size_row),
            (12 + p, owner_row),
        ):
            extras = jnp.where(line == place_of, value, extras)
    send_ref[device, BODY:ROWS, :] = extras.astype(jnp.bfloat16)


CHUNKS = 4
QUAD = 4


def total_kernel(
    got_ref, mean_ref, cov_ref, body, extra, lines, acc_a, acc_b, id_vec, ids, hits, spread,
    second, full, body_sem, extra_sem, id_sem,
):
    fast = lax.Precision.HIGHEST
    per = DEVS // CHUNKS
    extra_copy = pltpu.make_async_copy(got_ref.at[:, pl.ds(BODY, 16), :], extra, extra_sem)
    extra_copy.start()
    body_copies = [
        pltpu.make_async_copy(
            got_ref.at[pl.ds(c * per, per), pl.ds(0, BODY), :],
            body.at[pl.ds(c * per, per)],
            body_sem.at[c],
        )
        for c in range(CHUNKS)
    ]
    for one in body_copies:
        one.start()
    acc_a[...] = jnp.zeros_like(acc_a)
    acc_b[...] = jnp.zeros_like(acc_b)
    extra_copy.wait()
    lines[...] = extra[...].astype(jnp.float32).reshape(DEVS * 16, 128)

    def line(k):
        return lines[pl.ds(k, DEVS, stride=16), :]

    lane = lax.broadcasted_iota(jnp.int32, (DEVS, 128), 1)
    row = lax.broadcasted_iota(jnp.int32, (DEVS, 128), 0)
    inner = lane & 63
    owners = [line(12 + p) for p in range(PAIRS)]
    id_vec[...] = jnp.where(
        inner == 0, owners[0], jnp.where(inner == 1, owners[1], owners[2])
    ).astype(jnp.int32)
    id_copy = pltpu.make_async_copy(id_vec, ids, id_sem)
    id_copy.start()

    means, sizes = [], []
    sums = jnp.zeros((DEVS, 384), jnp.float32)
    for p in range(PAIRS):
        mean = line(3 + p) + line(6 + p)
        size = line(9 + p)
        means.append(mean)
        sizes.append(size)
        turned = owners[p].T
        for h in range(2):
            hit = jnp.where(row == turned[64 * h : 64 * h + 1, :].astype(jnp.int32), 1.0, 0.0)
            hits[:, (2 * p + h) * 128 : (2 * p + h + 1) * 128] = hit
            mine = (lane >= EMB) if h else (lane < EMB)
            values = jnp.concatenate(
                [
                    jnp.where(mine, size * mean, 0.0),
                    jnp.where(mine, size, 0.0),
                    jnp.where(mine, line(p), 0.0),
                ],
                axis=1,
            )
            sums = sums + jnp.dot(
                hit, values, preferred_element_type=jnp.float32, precision=fast
            )

    def folded(value):
        return value + pltpu.roll(value, EMB, 1)

    count = jnp.maximum(folded(sums[:, 128:256]), 1.0)
    total_mean = folded(sums[:, 0:128]) / count
    mean_ref[...] = total_mean[:, 0:EMB]
    diag_sum = folded(sums[:, 256:384])
    inverse = 1.0 / count
    lines[0:DEVS, :] = diag_sum
    lines[DEVS : 2 * DEVS, :] = inverse

    for p in range(PAIRS):
        for h in range(2):
            owner = owners[p]
            other = pltpu.roll(owner, EMB, 1)
            owner_all = (
                jnp.where(lane < EMB, other, owner) if h else jnp.where(lane < EMB, owner, other)
            )
            hit_t = jnp.where(owner_all.astype(jnp.int32) == lane, 1.0, 0.0)
            theirs = jnp.dot(
                hit_t, total_mean, preferred_element_type=jnp.float32, precision=fast
            )
            off = jnp.sqrt(sizes[p]) * (means[p] - theirs)
            if h:
                off = pltpu.roll(off, EMB, 1)
            off = jnp.where(lane < EMB, off, 0.0)
            k = 2 * p + h
            second[k * 128 : (k + 1) * 128, :] = off.astype(jnp.bfloat16)
            spread[:, k * 128 : (k + 1) * 128] = off.T[0:EMB, :].astype(jnp.bfloat16)

    id_copy.wait()
    for c in range(CHUNKS):
        body_copies[c].wait()

        def add(s, carry):
            for p in range(PAIRS):
                value = body[s, p * HALF : (p + 1) * HALF, :].astype(jnp.float32)
                a = ids[s, p]
                b = ids[s, 64 + p]
                acc_a[a] = acc_a[a] + value
                acc_b[b] = acc_b[b] + value
            return carry

        lax.fori_loop(c * per, (c + 1) * per, add, 0, unroll=2)

    lane32 = lax.broadcasted_iota(jnp.int32, (HALF, 128), 1)
    row32 = lax.broadcasted_iota(jnp.int32, (HALF, 128), 0)

    def quad(q, carry):
        base = q * QUAD
        left = []
        for t in range(QUAD):
            mask = hits[pl.ds(base + t, 1), :].astype(jnp.bfloat16)
            left.append(spread[...] * mask)
        between = jnp.dot(
            jnp.concatenate(left, axis=0), second[...], preferred_element_type=jnp.float32
        )
        packed = [
            acc_a[base + t] + pltpu.roll(acc_b[base + t], EMB, 1) for t in range(QUAD)
        ]
        turned = jnp.concatenate(packed, axis=0).T[0:EMB]
        for t in range(QUAD):
            diag = lines[pl.ds(base + t, 1), :]
            inv = lines[pl.ds(DEVS + base + t, 1), :]
            flip = pltpu.roll(turned, (128 - HALF * t) % 128, 1) if t else turned
            flip_up, flip_down = flip[0:HALF], flip[HALF:EMB]
            here = packed[t]
            top = jnp.where((lane32 >= HALF) | (lane32 >= row32), here, flip_up)
            low = jnp.where(
                lane32 < row32, here, jnp.where(lane32 == row32, diag, flip_up)
            )
            bottom = jnp.where(lane32 < HALF, flip_down, pltpu.roll(low, HALF, 1))
            both = jnp.concatenate([top, bottom], axis=0)
            both = (both + between[t * EMB : (t + 1) * EMB]) * inv
            full[pl.ds((base + t) * EMB, EMB), :] = both
        return carry

    lax.fori_loop(0, SV_DEV // QUAD, quad, 0, unroll=2)

    for t in range(EMB // 2):
        even = full[pl.ds(2 * t, SV_DEV, stride=EMB), :]
        odd = full[pl.ds(2 * t + 1, SV_DEV, stride=EMB), :]
        cov_ref[:, t * 128 : (t + 1) * 128] = jnp.where(
            lane < EMB, even, pltpu.roll(odd, EMB, 1)
        )


def totals(got):
    return pl.pallas_call(
        total_kernel,
        out_shape=(
            jax.ShapeDtypeStruct((SV_DEV, EMB), jnp.float32),
            jax.ShapeDtypeStruct((SV_DEV, EMB * EMB), jnp.float32),
        ),
        in_specs=[pl.BlockSpec(memory_space=pl.ANY)],
        out_specs=(
            pl.BlockSpec(memory_space=pltpu.VMEM),
            pl.BlockSpec(memory_space=pltpu.VMEM),
        ),
        scratch_shapes=[
            pltpu.VMEM((DEVS, BODY, 128), jnp.bfloat16),
            pltpu.VMEM((DEVS, 16, 128), jnp.bfloat16),
            pltpu.VMEM((DEVS * 16, 128), jnp.float32),
            pltpu.VMEM((SV_DEV, HALF, 128), jnp.float32),
            pltpu.VMEM((SV_DEV, HALF, 128), jnp.float32),
            pltpu.VMEM((DEVS, 128), jnp.int32),
            pltpu.SMEM((DEVS, 128), jnp.int32),
            pltpu.VMEM((SV_DEV, DEVS * SLOTS), jnp.float32),
            pltpu.VMEM((EMB, DEVS * SLOTS), jnp.bfloat16),
            pltpu.VMEM((DEVS * SLOTS, 128), jnp.bfloat16),
            pltpu.VMEM((SV_DEV * EMB, 128), jnp.float32),
            pltpu.SemaphoreType.DMA((CHUNKS,)),
            pltpu.SemaphoreType.DMA,
            pltpu.SemaphoreType.DMA,
        ],
        compiler_params=pltpu.CompilerParams(vmem_limit_bytes=60 << 20),
    )(got)


def local(
    features, first_weight, first_bias, second_weight, second_bias, labels, blocks, owner_map
):
    got = main(
        features,
        first_weight,
        first_bias,
        second_weight,
        second_bias,
        labels,
        blocks.reshape(blocks.shape[2], blocks.shape[3]),
        owner_map,
    )
    return totals(got)


def solution(mesh):
    return jax.shard_map(
        local,
        mesh=mesh,
        in_specs=(
            P(None, "gz", "xy", None),
            P(),
            P(),
            P(),
            P(),
            P("gz", "xy", None),
            P("gz", "xy", None, None),
            P(),
        ),
        out_specs=(P(("gz", "xy"), None), P(("gz", "xy"), None)),
        check_vma=False,
    )
```

```python
import functools

import jax
import jax.numpy as jnp
from jax import lax
from jax.experimental import pallas as pl
from jax.experimental.pallas import tpu as pltpu
from jax.sharding import PartitionSpec as P

SV_DEV = 128
EMB = 64
HALF = 32
SLOTS = 6
PAIRS = 3
BODY = PAIRS * HALF
ROWS = BODY + 16
DEVS = 128
GROUPS = 160
AHEAD = 4
ROUNDS = 7
MESH = pl.DeviceIdType.MESH


FEATURE_CHUNKS = ((0, 5), (5, 5), (10, 5), (15, 5))
HIDDEN_CHUNKS = ((0, 4), (4, 5), (9, 5), (14, 6))
LAST_CHUNKS = ((0, 3), (3, 5), (8, 5), (13, 7))
PER_EXCHANGE = 14


def halo_copies(own, side_z, side_y, chunks, base, send_sem, recv_sem):
    gz, xy = lax.axis_index("gz"), lax.axis_index("xy")
    depth, height = lax.axis_size("gz"), lax.axis_size("xy")
    plan = []
    for c, (first, length) in enumerate(chunks):
        rows = pl.ds(first, length)
        plan.append(((1, 0), own.at[3, rows], side_z.at[0, rows]))
        plan.append(((-1, 0), own.at[0, rows], side_z.at[1, rows]))
    plan.append(((0, 1), own.at[:, 19], side_y.at[0, pl.ds(1, 4)]))
    plan.append(((0, -1), own.at[:, 0], side_y.at[1, pl.ds(1, 4)]))
    plan.append(((1, 1), own.at[3, 19], side_y.at[0, 0]))
    plan.append(((1, -1), own.at[3, 0], side_y.at[1, 0]))
    plan.append(((-1, 1), own.at[0, 19], side_y.at[0, 5]))
    plan.append(((-1, -1), own.at[0, 0], side_y.at[1, 5]))
    copies = []
    for i, ((dz, dy), src, dst) in enumerate(plan):
        def inside(a, b):
            return (a >= 0) & (a < depth) & (b >= 0) & (b < height)

        copy = pltpu.make_async_remote_copy(
            src_ref=src,
            dst_ref=dst,
            send_sem=send_sem.at[base + i],
            recv_sem=recv_sem.at[base + i],
            device_id=(gz + dz, xy + dy),
            device_id_type=MESH,
        )
        copies.append((copy, inside(gz + dz, xy + dy), inside(gz - dz, xy - dy)))
    return copies


def start(entry):
    @pl.when(entry[1])
    def _():
        entry[0].start()


def arrive(entry):
    @pl.when(entry[2])
    def _():
        entry[0].wait_recv()


def leave(entry):
    @pl.when(entry[1])
    def _():
        entry[0].wait_send()


def main_kernel(
    own, raw1, b1, raw2, b2, lists_ref, labels_hbm, owner_hbm, got_ref, wide, hwide, hidden,
    fz, fy, hz, hy, part1, part2, emb_ref, send_ref, labels_ref, owner_ref, facts, scalars,
    rows_s, rows_v, table_v, table_ref, send_sem, recv_sem, far_send, far_recv, own_sem, here_sem,
    round_sem, w1, w2,
):
    gz, xy = lax.axis_index("gz"), lax.axis_index("xy")
    depth, height = lax.axis_size("gz"), lax.axis_size("xy")
    me = gz * 32 + xy
    barrier = pltpu.get_barrier_semaphore()
    labels_copy = pltpu.make_async_copy(labels_hbm, labels_ref, here_sem.at[0])
    owner_copy = pltpu.make_async_copy(owner_hbm, owner_ref, here_sem.at[1])
    labels_copy.start()
    owner_copy.start()

    for side, has in ((0, gz == 0), (1, gz == depth - 1)):
        @pl.when(has)
        def _():
            zeros = jnp.zeros(fz.shape[1:], fz.dtype)
            fz[side] = zeros
            hz[side] = zeros
            for s in range(2):
                fy[s, 5 * side] = jnp.zeros(fy.shape[2:], fy.dtype)
                hy[s, 5 * side] = jnp.zeros(fy.shape[2:], fy.dtype)

    for side, has in ((0, xy == 0), (1, xy == height - 1)):
        @pl.when(has)
        def _():
            fy[side] = jnp.zeros(fy.shape[1:], fy.dtype)
            hy[side] = jnp.zeros(fy.shape[1:], fy.dtype)

    lane = lax.broadcasted_iota(jnp.int32, (48, 256), 1)

    def put(ref, e, y, value):
        turned = value.astype(jnp.float32)
        left = jnp.where(lane == 0, 0.0, pltpu.roll(turned, 1, 1))
        right = jnp.where(lane == 255, 0.0, pltpu.roll(turned, 255, 1))
        ref[e, y, 0:48, :] = left.astype(jnp.bfloat16)
        ref[e, y, 48:96, :] = value
        ref[e, y, 96:144, :] = right.astype(jnp.bfloat16)

    near = [(a, b) for a in (-1, 0, 1) for b in (-1, 0, 1) if (a, b) != (0, 0)]
    for a, b in near:
        there = (gz + a >= 0) & (gz + a < depth) & (xy + b >= 0) & (xy + b < height)

        @pl.when(there)
        def _():
            pl.semaphore_signal(
                barrier, inc=1, device_id=(gz + a, xy + b), device_id_type=MESH
            )

    def across(r):
        bit = lax.rem(me // (1 << r), 2)
        return place(me + (1 - 2 * bit) * (1 << r))

    for r in range(ROUNDS):
        pl.semaphore_signal(barrier, inc=1, device_id=across(r), device_id_type=MESH)

    def tell(r):
        pl.semaphore_signal(
            round_sem.at[r], inc=1, device_id=across(r), device_id_type=MESH
        )

    def hear(r):
        pl.semaphore_wait(round_sem.at[r], 1)

    def fill(y, carry):
        for z in range(4):
            put(wide, z + 1, y + 1, own[z, y])
        return carry

    count = lists_ref.shape[0]
    lists = lists_ref[...]
    sizes = jnp.sum(jnp.where(lists >= 0, 1, 0), axis=1, keepdims=True)
    column = lax.broadcasted_iota(jnp.int32, lists.shape, 1)
    facts[...] = jnp.where(column == 0, lists, sizes).astype(jnp.float32).T[0:8, :].astype(jnp.int32)
    facts_copy = pltpu.make_async_copy(facts, scalars, here_sem.at[2])
    facts_copy.start()
    beside_z = jnp.where(gz > 0, 1, 0) + jnp.where(gz < depth - 1, 1, 0)
    beside_y = jnp.where(xy > 0, 1, 0) + jnp.where(xy < height - 1, 1, 0)
    pl.semaphore_wait(barrier, (1 + beside_z) * (1 + beside_y) - 1 + ROUNDS)

    first = halo_copies(own, fz, fy, FEATURE_CHUNKS, 0, send_sem, recv_sem)
    then = halo_copies(hidden, hz, hy, HIDDEN_CHUNKS, PER_EXCHANGE, send_sem, recv_sem)
    for entry in first[8:] + first[:8]:
        start(entry)
    tell(0)
    for raw, w, channels in ((raw1, w1, 48), (raw2, w2, 64)):
        for dz in range(3):
            w[dz * channels : (dz + 1) * channels, :] = jnp.concatenate(
                [raw[dz * 9 + t] for t in range(9)], axis=1
            )
    lax.fori_loop(0, 20, fill, 0)
    hear(0)
    tell(1)

    def slab(ref, e, y):
        return ref[e, pl.ds(y, 3)].reshape(432, 256)

    def product(w, ref, e, y, low, high, channels):
        r = jnp.dot(
            w[low * channels : (high + 1) * channels, :],
            slab(ref, e, y),
            preferred_element_type=jnp.float32,
        )
        return {
            e - dz: r[(dz - low) * channels : (dz - low + 1) * channels]
            for dz in range(low, high + 1)
        }

    def inner(w, ref, y, channels):
        total = {}
        for e, low, high in ((1, 0, 1), (2, 0, 2), (3, 0, 2), (4, 1, 2)):
            for z, v in product(w, ref, e, y, low, high, channels).items():
                total[z] = total[z] + v if z in total else v
        return total

    for entry in first[8:]:
        arrive(entry)
    hear(1)
    tell(2)

    def fill_side(e, carry):
        put(wide, e, 0, fy[0, e])
        put(wide, e, 21, fy[1, e])
        return carry

    lax.fori_loop(0, 6, fill_side, 0)

    def bias_of(ref, channels):
        line = jnp.concatenate([ref[...], jnp.zeros((1, 128 - channels), jnp.float32)], axis=1)
        tall = jnp.broadcast_to(line, (128, 128)).T[0:channels]
        return jnp.concatenate([tall, tall], axis=1)

    bias1 = bias_of(b1, 48)
    bias2 = bias_of(b2, 64)

    def keep_hidden(z, y, total):
        value = jnp.maximum(total + bias1, 0.0).astype(jnp.bfloat16)
        hidden[z, y] = value
        put(hwide, z + 1, y + 1, value)

    labels_copy.wait()
    owner_copy.wait()
    facts_copy.wait()

    def look(b):
        at = scalars[0, b]
        run = at >> 8
        z = jnp.clip((run * 3277) >> 16, 0, 3)
        label = labels_ref[jnp.clip(run - z * 20, 0, 19), z, at & 255]
        rows_s[0, b] = owner_ref[label & (owner_ref.shape[0] - 1)]

    each = -(-count // 20)

    def first_inner(y, carry):
        for t in range(each):
            look(jnp.minimum(y * each + t, count - 1))
        total = inner(w1, wide, y, 48)
        part1[0, y] = total[0]
        part1[1, y] = total[3]
        keep_hidden(1, y, total[1])
        keep_hidden(2, y, total[2])
        return carry

    lax.fori_loop(0, 20, first_inner, 0, unroll=4)

    def fill_z(y, carry):
        put(wide, 0, y + 1, fz[0, y])
        put(wide, 5, y + 1, fz[1, y])
        return carry

    def first_outer(y, carry):
        keep_hidden(0, y, part1[0, y] + product(w1, wide, 0, y, 0, 0, 48)[0])
        keep_hidden(3, y, part1[1, y] + product(w1, wide, 5, y, 2, 2, 48)[3])
        return carry

    for c in range(4):
        arrive(first[2 * c])
        arrive(first[2 * c + 1])
        low, length = FEATURE_CHUNKS[c]
        lax.fori_loop(low, low + length, fill_z, 0, unroll=length)
        low, length = HIDDEN_CHUNKS[c]
        lax.fori_loop(low, low + length, first_outer, 0, unroll=length)
        if c == 0:
            for i in (9, 11, 13):
                start(then[i])
        if c == 3:
            for i in (8, 10, 12):
                start(then[i])
        start(then[2 * c])
        start(then[2 * c + 1])
        hear(2 + c)
        tell(3 + c)

    rows_copy = pltpu.make_async_copy(rows_s, rows_v, here_sem.at[3])
    rows_copy.start()
    rows_copy.wait()
    line8 = lax.broadcasted_iota(jnp.int32, (8, count), 0)
    three = jnp.where(line8 == 2, jnp.broadcast_to(rows_v[0:1, :], (8, count)), facts[...])
    turned3 = jnp.concatenate(
        [three.astype(jnp.float32), jnp.zeros((120, count), jnp.float32)], axis=0
    ).T.astype(jnp.int32)
    row_of = turned3[:, 2:3]
    code = (turned3[:, 0:1] << 15) + (turned3[:, 1:2] << 7) + (row_of & 127)
    hit = (row_of >> 7) == lax.broadcasted_iota(jnp.int32, (count, DEVS), 1)
    before = lax.broadcasted_iota(jnp.int32, (count, count), 0) > lax.broadcasted_iota(
        jnp.int32, (count, count), 1
    )
    rank = jnp.dot(
        jnp.where(before, 1.0, 0.0).astype(jnp.bfloat16),
        jnp.where(hit, 1.0, 0.0).astype(jnp.bfloat16),
        preferred_element_type=jnp.float32,
    )
    rank = jnp.where(hit, rank, -1.0)
    slots = [
        jnp.sum(jnp.where(rank == float(k), code, 0), axis=0, keepdims=True)
        for k in range(SLOTS)
    ]
    table_v[...] = jnp.concatenate(slots + [slots[0], slots[0]], axis=0)
    table_copy = pltpu.make_async_copy(table_v, table_ref, here_sem.at[4])
    table_copy.start()

    arrive(then[8])
    arrive(then[9])
    hear(6)

    def hidden_side(e, carry):
        put(hwide, e, 0, hy[0, e])
        put(hwide, e, 21, hy[1, e])
        return carry

    lax.fori_loop(1, 5, hidden_side, 0)

    def keep(z, y, total):
        value = (total + bias2).astype(jnp.bfloat16)
        group = (z * 20 + y) * 2
        emb_ref[group] = value[:, 0:128]
        emb_ref[group + 1] = value[:, 128:256]

    def second_inner(y, carry):
        total = inner(w2, hwide, y, 64)
        part2[0, y] = total[0]
        part2[1, y] = total[3]
        keep(1, y, total[1])
        keep(2, y, total[2])
        return carry

    lax.fori_loop(0, 20, second_inner, 0, unroll=4)

    def hidden_z(y, carry):
        put(hwide, 0, y + 1, hz[0, y])
        put(hwide, 5, y + 1, hz[1, y])
        return carry

    def second_outer(y, carry):
        keep(0, y, part2[0, y] + product(w2, hwide, 0, y, 0, 0, 64)[0])
        keep(3, y, part2[1, y] + product(w2, hwide, 5, y, 2, 2, 64)[3])
        return carry

    for entry in then[10:]:
        arrive(entry)
    hidden_side(0, 0)
    hidden_side(5, 0)
    for c in range(4):
        arrive(then[2 * c])
        arrive(then[2 * c + 1])
        low, length = HIDDEN_CHUNKS[c]
        lax.fori_loop(low, low + length, hidden_z, 0, unroll=length)
        low, length = LAST_CHUNKS[c]
        lax.fori_loop(low, low + length, second_outer, 0, unroll=length)

    table_copy.wait()

    def copy(k):
        device = partner(me, k)
        return pltpu.make_async_remote_copy(
            src_ref=send_ref.at[device],
            dst_ref=got_ref.at[me],
            send_sem=far_send.at[k],
            recv_sem=far_recv.at[k],
            device_id=place(device),
            device_id_type=MESH,
        )

    for k in range(AHEAD):
        moments_of(emb_ref, table_ref, partner(me, k), send_ref)
    own_copy = pltpu.make_async_copy(send_ref.at[me], got_ref.at[me], own_sem)
    own_copy.start()
    for k in range(1, AHEAD):
        copy(k).start()

    def send(i, carry):
        for t in range(AHEAD):
            moments_of(emb_ref, table_ref, partner(me, i * AHEAD + t), send_ref)
        for t in range(AHEAD):
            copy(i * AHEAD + t).start()
        return carry

    lax.fori_loop(1, DEVS // AHEAD, send, 0)
    for entry in first + then:
        leave(entry)

    def finish(k, carry):
        copy(k).wait()
        return carry

    lax.fori_loop(1, DEVS, finish, 0)
    own_copy.wait()


def main(features, first_weight, first_bias, second_weight, second_bias, labels, blocks, owner_map):
    own = features.transpose(1, 2, 0, 3)
    w1 = first_weight.reshape(27, 48, 48)
    w2 = second_weight.reshape(27, 64, 48)
    bf, f32, i32 = jnp.bfloat16, jnp.float32, jnp.int32
    count = blocks.shape[0]
    return pl.pallas_call(
        main_kernel,
        out_shape=jax.ShapeDtypeStruct((DEVS, ROWS, 128), bf),
        in_specs=[pl.BlockSpec(memory_space=pltpu.VMEM)] * 6
        + [pl.BlockSpec(memory_space=pl.ANY)] * 2,
        out_specs=pl.BlockSpec(memory_space=pl.ANY),
        scratch_shapes=[
            pltpu.VMEM((6, 22, 144, 256), bf),
            pltpu.VMEM((6, 22, 144, 256), bf),
            pltpu.VMEM((4, 20, 48, 256), bf),
            pltpu.VMEM((2, 20, 48, 256), bf),
            pltpu.VMEM((2, 6, 48, 256), bf),
            pltpu.VMEM((2, 20, 48, 256), bf),
            pltpu.VMEM((2, 6, 48, 256), bf),
            pltpu.VMEM((2, 20, 48, 256), f32),
            pltpu.VMEM((2, 20, 64, 256), f32),
            pltpu.VMEM((GROUPS, EMB, 128), bf),
            pltpu.VMEM((DEVS, ROWS, 128), bf),
            pltpu.SMEM(labels.shape, i32),
            pltpu.SMEM(owner_map.shape, i32),
            pltpu.VMEM((8, count), i32),
            pltpu.SMEM((8, count), i32),
            pltpu.SMEM((8, count), i32),
            pltpu.VMEM((8, count), i32),
            pltpu.VMEM((8, DEVS), i32),
            pltpu.SMEM((8, DEVS), i32),
            pltpu.SemaphoreType.DMA((2 * PER_EXCHANGE,)),
            pltpu.SemaphoreType.DMA((2 * PER_EXCHANGE,)),
            pltpu.SemaphoreType.DMA((DEVS,)),
            pltpu.SemaphoreType.DMA((DEVS,)),
            pltpu.SemaphoreType.DMA,
            pltpu.SemaphoreType.DMA((5,)),
            pltpu.SemaphoreType.REGULAR((ROUNDS,)),
            pltpu.VMEM((144, 432), bf),
            pltpu.VMEM((192, 432), bf),
        ],
        compiler_params=pltpu.CompilerParams(
            collective_id=0, has_side_effects=True, vmem_limit_bytes=52 << 20
        ),
    )(own, w1, first_bias[None], w2, second_bias[None], blocks, labels, owner_map)


def place(device):
    return (device // 32, lax.rem(device, 32))


def partner(me, k):
    core, x, y, z = lax.rem(me, 2), lax.rem(me // 2, 4), lax.rem(me // 8, 4), me // 32
    kc, kx, ky, kz = k // 64, lax.rem(k, 4), lax.rem(k // 4, 4), lax.rem(k // 16, 4)
    ky = lax.rem(ky + kx, 4)
    kz = lax.rem(kz + kx + ky, 4)
    there = (lax.rem(z + kz, 4) * 4 + lax.rem(y + ky, 4)) * 4 + lax.rem(x + kx, 4)
    return there * 2 + lax.rem(core + kc, 2)


def moments_of(emb_ref, table_ref, device, send_ref):
    lane = lax.broadcasted_iota(jnp.int32, (1, 128), 1)
    inner = lax.broadcasted_iota(jnp.int32, (HALF, 128), 1) & 63
    outer = lax.broadcasted_iota(jnp.int32, (HALF, 128), 0)
    upper = (inner >= HALF) | (inner >= outer)
    diagonal = inner == outer
    line = lax.broadcasted_iota(jnp.int32, (16, 128), 0)
    one = jnp.ones((EMB, 256), jnp.bfloat16)
    near = lax.broadcasted_iota(jnp.int32, (EMB, 128), 1) < EMB
    extras = jnp.zeros((16, 128), jnp.float32)
    for p in range(PAIRS):
        parts, sizes, rows = [], [], []
        for h in range(2):
            code = table_ref[2 * p + h, device]
            start = code >> 15
            size = (code >> 7) & 255
            rows.append((code & 127).astype(jnp.float32))
            sizes.append(size.astype(jnp.float32))
            group = jnp.clip(start >> 7, 0, GROUPS - 1)
            low = start & 127
            first = emb_ref[group]
            second = emb_ref[jnp.minimum(group + 1, GROUPS - 1)]
            in_first = jnp.where((lane >= low) & (lane < low + size), 1.0, 0.0).astype(jnp.bfloat16)
            in_second = jnp.where(lane + 128 < low + size, 1.0, 0.0).astype(jnp.bfloat16)
            mask_rows = jnp.broadcast_to(jnp.concatenate([in_first, in_second], axis=1), (16, 256))
            whole = jnp.concatenate([first, second], axis=1)
            left = jnp.concatenate([jnp.concatenate([first * in_first, second * in_second], axis=1), mask_rows], axis=0)
            right = jnp.concatenate([whole, one] if h == 0 else [one, whole], axis=0)
            parts.append(lax.dot_general(left, right, (((1,), (1,)), ((), ())), preferred_element_type=jnp.float32))
        size_row = jnp.where(lane < EMB, sizes[0], sizes[1])
        owner_row = jnp.where(lane < EMB, rows[0], rows[1])
        second_row = jnp.where(near[0:1], parts[0][EMB : EMB + 1], parts[1][EMB : EMB + 1])
        mean = second_row / jnp.maximum(size_row, 1.0)
        square = jnp.where(near, parts[0][0:EMB], parts[1][0:EMB])
        column = pltpu.roll(jnp.where(near, parts[1][0:EMB], parts[0][0:EMB]), EMB, 1)
        centred = square - column * mean
        rolled = pltpu.roll(centred[HALF:EMB], 96, 1)
        packed = jnp.where(upper, centred[0:HALF], rolled)
        send_ref[device, p * HALF : (p + 1) * HALF, :] = packed.astype(jnp.bfloat16)
        diag = jnp.sum(jnp.where(diagonal, rolled, 0.0), axis=0, keepdims=True)
        high = mean.astype(jnp.bfloat16).astype(jnp.float32)
        for place_of, value in (
            (p, diag),
            (3 + p, high),
            (6 + p, mean - high),
            (9 + p, size_row),
            (12 + p, owner_row),
        ):
            extras = jnp.where(line == place_of, value, extras)
    send_ref[device, BODY:ROWS, :] = extras.astype(jnp.bfloat16)


CHUNKS = 4
QUAD = 4


def total_kernel(
    got_ref, mean_ref, cov_ref, body, extra, lines, acc_a, acc_b, id_vec, ids, hits, spread,
    second, full, body_sem, extra_sem, id_sem,
):
    fast = lax.Precision.HIGHEST
    per = DEVS // CHUNKS
    extra_copy = pltpu.make_async_copy(got_ref.at[:, pl.ds(BODY, 16), :], extra, extra_sem)
    extra_copy.start()
    body_copies = [
        pltpu.make_async_copy(
            got_ref.at[pl.ds(c * per, per), pl.ds(0, BODY), :],
            body.at[pl.ds(c * per, per)],
            body_sem.at[c],
        )
        for c in range(CHUNKS)
    ]
    for one in body_copies:
        one.start()
    acc_a[...] = jnp.zeros_like(acc_a)
    acc_b[...] = jnp.zeros_like(acc_b)
    extra_copy.wait()
    lines[...] = extra[...].astype(jnp.float32).reshape(DEVS * 16, 128)

    def line(k):
        return lines[pl.ds(k, DEVS, stride=16), :]

    lane = lax.broadcasted_iota(jnp.int32, (DEVS, 128), 1)
    row = lax.broadcasted_iota(jnp.int32, (DEVS, 128), 0)
    inner = lane & 63
    owners = [line(12 + p) for p in range(PAIRS)]
    id_vec[...] = jnp.where(
        inner == 0, owners[0], jnp.where(inner == 1, owners[1], owners[2])
    ).astype(jnp.int32)
    id_copy = pltpu.make_async_copy(id_vec, ids, id_sem)
    id_copy.start()

    means, sizes = [], []
    sums = jnp.zeros((DEVS, 384), jnp.float32)
    for p in range(PAIRS):
        mean = line(3 + p) + line(6 + p)
        size = line(9 + p)
        means.append(mean)
        sizes.append(size)
        turned = owners[p].T
        for h in range(2):
            hit = jnp.where(row == turned[64 * h : 64 * h + 1, :].astype(jnp.int32), 1.0, 0.0)
            hits[:, (2 * p + h) * 128 : (2 * p + h + 1) * 128] = hit
            mine = (lane >= EMB) if h else (lane < EMB)
            values = jnp.concatenate(
                [
                    jnp.where(mine, size * mean, 0.0),
                    jnp.where(mine, size, 0.0),
                    jnp.where(mine, line(p), 0.0),
                ],
                axis=1,
            )
            sums = sums + jnp.dot(
                hit, values, preferred_element_type=jnp.float32, precision=fast
            )

    def folded(value):
        return value + pltpu.roll(value, EMB, 1)

    count = jnp.maximum(folded(sums[:, 128:256]), 1.0)
    total_mean = folded(sums[:, 0:128]) / count
    mean_ref[...] = total_mean.T[0:EMB]
    diag_sum = folded(sums[:, 256:384])
    inverse = 1.0 / count
    lines[0:DEVS, :] = diag_sum
    lines[DEVS : 2 * DEVS, :] = inverse

    for p in range(PAIRS):
        for h in range(2):
            owner = owners[p]
            other = pltpu.roll(owner, EMB, 1)
            owner_all = (
                jnp.where(lane < EMB, other, owner) if h else jnp.where(lane < EMB, owner, other)
            )
            hit_t = jnp.where(owner_all.astype(jnp.int32) == lane, 1.0, 0.0)
            theirs = jnp.dot(
                hit_t, total_mean, preferred_element_type=jnp.float32, precision=fast
            )
            off = jnp.sqrt(sizes[p]) * (means[p] - theirs)
            if h:
                off = pltpu.roll(off, EMB, 1)
            off = jnp.where(lane < EMB, off, 0.0)
            k = 2 * p + h
            second[k * 128 : (k + 1) * 128, :] = off.astype(jnp.bfloat16)
            spread[:, k * 128 : (k + 1) * 128] = off.T[0:EMB, :].astype(jnp.bfloat16)

    id_copy.wait()
    for c in range(CHUNKS):
        body_copies[c].wait()

        def add(s, carry):
            for p in range(PAIRS):
                value = body[s, p * HALF : (p + 1) * HALF, :].astype(jnp.float32)
                a = ids[s, p]
                b = ids[s, 64 + p]
                acc_a[a] = acc_a[a] + value
                acc_b[b] = acc_b[b] + value
            return carry

        lax.fori_loop(c * per, (c + 1) * per, add, 0, unroll=4)

    lane32 = lax.broadcasted_iota(jnp.int32, (HALF, 128), 1)
    row32 = lax.broadcasted_iota(jnp.int32, (HALF, 128), 0)

    def quad(q, carry):
        base = q * QUAD
        left = []
        for t in range(QUAD):
            mask = hits[pl.ds(base + t, 1), :].astype(jnp.bfloat16)
            left.append(spread[...] * mask)
        between = jnp.dot(
            jnp.concatenate(left, axis=0), second[...], preferred_element_type=jnp.float32
        )
        packed = [
            acc_a[base + t] + pltpu.roll(acc_b[base + t], EMB, 1) for t in range(QUAD)
        ]
        turned = jnp.concatenate(packed, axis=0).T[0:EMB]
        for t in range(QUAD):
            diag = lines[pl.ds(base + t, 1), :]
            inv = lines[pl.ds(DEVS + base + t, 1), :]
            flip = pltpu.roll(turned, (128 - HALF * t) % 128, 1) if t else turned
            flip_up, flip_down = flip[0:HALF], flip[HALF:EMB]
            here = packed[t]
            top = jnp.where((lane32 >= HALF) | (lane32 >= row32), here, flip_up)
            low = jnp.where(
                lane32 < row32, here, jnp.where(lane32 == row32, diag, flip_up)
            )
            bottom = jnp.where(lane32 < HALF, flip_down, pltpu.roll(low, HALF, 1))
            both = jnp.concatenate([top, bottom], axis=0)
            both = (both + between[t * EMB : (t + 1) * EMB]) * inv
            full[pl.ds((base + t) * EMB, EMB), :] = both
        return carry

    lax.fori_loop(0, SV_DEV // QUAD, quad, 0, unroll=2)

    for t in range(EMB // 2):
        even = full[pl.ds(2 * t, SV_DEV, stride=EMB), :]
        odd = full[pl.ds(2 * t + 1, SV_DEV, stride=EMB), :]
        cov_ref[:, t * 128 : (t + 1) * 128] = jnp.where(
            lane < EMB, even, pltpu.roll(odd, EMB, 1)
        )


def totals(got):
    return pl.pallas_call(
        total_kernel,
        out_shape=(
            jax.ShapeDtypeStruct((EMB, SV_DEV), jnp.float32),
            jax.ShapeDtypeStruct((SV_DEV, EMB * EMB), jnp.float32),
        ),
        in_specs=[pl.BlockSpec(memory_space=pl.ANY)],
        out_specs=(
            pl.BlockSpec(memory_space=pltpu.VMEM),
            pl.BlockSpec(memory_space=pltpu.VMEM),
        ),
        scratch_shapes=[
            pltpu.VMEM((DEVS, BODY, 128), jnp.bfloat16),
            pltpu.VMEM((DEVS, 16, 128), jnp.bfloat16),
            pltpu.VMEM((DEVS * 16, 128), jnp.float32),
            pltpu.VMEM((SV_DEV, HALF, 128), jnp.float32),
            pltpu.VMEM((SV_DEV, HALF, 128), jnp.float32),
            pltpu.VMEM((DEVS, 128), jnp.int32),
            pltpu.SMEM((DEVS, 128), jnp.int32),
            pltpu.VMEM((SV_DEV, DEVS * SLOTS), jnp.float32),
            pltpu.VMEM((EMB, DEVS * SLOTS), jnp.bfloat16),
            pltpu.VMEM((DEVS * SLOTS, 128), jnp.bfloat16),
            pltpu.VMEM((SV_DEV * EMB, 128), jnp.float32),
            pltpu.SemaphoreType.DMA((CHUNKS,)),
            pltpu.SemaphoreType.DMA,
            pltpu.SemaphoreType.DMA,
        ],
        compiler_params=pltpu.CompilerParams(vmem_limit_bytes=60 << 20),
    )(got)


def local(
    features, first_weight, first_bias, second_weight, second_bias, labels, blocks, owner_map
):
    got = main(
        features,
        first_weight,
        first_bias,
        second_weight,
        second_bias,
        labels.transpose(1, 0, 2),
        blocks.reshape(blocks.shape[2], blocks.shape[3]),
        owner_map,
    )
    mean, covariance = totals(got)
    return mean.T, covariance


def solution(mesh):
    return jax.shard_map(
        local,
        mesh=mesh,
        in_specs=(
            P(None, "gz", "xy", None),
            P(),
            P(),
            P(),
            P(),
            P("gz", "xy", None),
            P("gz", "xy", None, None),
            P(),
        ),
        out_specs=(P(("gz", "xy"), None), P(("gz", "xy"), None)),
        check_vma=False,
    )
```

```python
import functools

import jax
import jax.numpy as jnp
from jax import lax
from jax.experimental import pallas as pl
from jax.experimental.pallas import tpu as pltpu
from jax.sharding import PartitionSpec as P

SV_DEV = 128
EMB = 64
HALF = 32
SLOTS = 6
PAIRS = 3
BODY = PAIRS * HALF
ROWS = BODY + 16
DEVS = 128
GROUPS = 160
AHEAD = 4
ROUNDS = 7
MESH = pl.DeviceIdType.MESH


FEATURE_CHUNKS = ((0, 5), (5, 5), (10, 5), (15, 5))
HIDDEN_CHUNKS = ((0, 4), (4, 5), (9, 5), (14, 6))
LAST_CHUNKS = ((0, 3), (3, 5), (8, 5), (13, 7))
PER_EXCHANGE = 14


def halo_copies(own, side_z, side_y, chunks, base, send_sem, recv_sem):
    gz, xy = lax.axis_index("gz"), lax.axis_index("xy")
    depth, height = lax.axis_size("gz"), lax.axis_size("xy")
    plan = []
    for c, (first, length) in enumerate(chunks):
        rows = pl.ds(first, length)
        plan.append(((1, 0), own.at[3, rows], side_z.at[0, rows]))
        plan.append(((-1, 0), own.at[0, rows], side_z.at[1, rows]))
    plan.append(((0, 1), own.at[:, 19], side_y.at[0, pl.ds(1, 4)]))
    plan.append(((0, -1), own.at[:, 0], side_y.at[1, pl.ds(1, 4)]))
    plan.append(((1, 1), own.at[3, 19], side_y.at[0, 0]))
    plan.append(((1, -1), own.at[3, 0], side_y.at[1, 0]))
    plan.append(((-1, 1), own.at[0, 19], side_y.at[0, 5]))
    plan.append(((-1, -1), own.at[0, 0], side_y.at[1, 5]))
    copies = []
    for i, ((dz, dy), src, dst) in enumerate(plan):
        def inside(a, b):
            return (a >= 0) & (a < depth) & (b >= 0) & (b < height)

        copy = pltpu.make_async_remote_copy(
            src_ref=src,
            dst_ref=dst,
            send_sem=send_sem.at[base + i],
            recv_sem=recv_sem.at[base + i],
            device_id=(gz + dz, xy + dy),
            device_id_type=MESH,
        )
        copies.append((copy, inside(gz + dz, xy + dy), inside(gz - dz, xy - dy)))
    return copies


def start(entry):
    @pl.when(entry[1])
    def _():
        entry[0].start()


def arrive(entry):
    @pl.when(entry[2])
    def _():
        entry[0].wait_recv()


def leave(entry):
    @pl.when(entry[1])
    def _():
        entry[0].wait_send()


def main_kernel(
    own, raw1, b1, raw2, b2, lists_ref, labels_hbm, owner_hbm, got_ref, wide, hwide, hidden,
    fz, fy, hz, hy, part1, part2, emb_ref, send_ref, labels_ref, owner_ref, facts, scalars,
    rows_s, rows_v, table_v, table_ref, send_sem, recv_sem, far_send, far_recv, own_sem, here_sem,
    round_sem, w1, w2,
):
    gz, xy = lax.axis_index("gz"), lax.axis_index("xy")
    depth, height = lax.axis_size("gz"), lax.axis_size("xy")
    me = gz * 32 + xy
    barrier = pltpu.get_barrier_semaphore()
    labels_copy = pltpu.make_async_copy(labels_hbm, labels_ref, here_sem.at[0])
    owner_copy = pltpu.make_async_copy(owner_hbm, owner_ref, here_sem.at[1])
    labels_copy.start()
    owner_copy.start()

    lane = lax.broadcasted_iota(jnp.int32, (48, 256), 1)

    def put(ref, e, y, value):
        turned = value.astype(jnp.float32)
        left = jnp.where(lane == 0, 0.0, pltpu.roll(turned, 1, 1))
        right = jnp.where(lane == 255, 0.0, pltpu.roll(turned, 255, 1))
        ref[e, y, 0:48, :] = left.astype(jnp.bfloat16)
        ref[e, y, 48:96, :] = value
        ref[e, y, 96:144, :] = right.astype(jnp.bfloat16)

    near = [(a, b) for a in (-1, 0, 1) for b in (-1, 0, 1) if (a, b) != (0, 0)]
    for a, b in near:
        there = (gz + a >= 0) & (gz + a < depth) & (xy + b >= 0) & (xy + b < height)

        @pl.when(there)
        def _():
            pl.semaphore_signal(
                barrier, inc=1, device_id=(gz + a, xy + b), device_id_type=MESH
            )

    def across(r):
        bit = lax.rem(me // (1 << r), 2)
        return place(me + (1 - 2 * bit) * (1 << r))

    for r in range(ROUNDS):
        pl.semaphore_signal(barrier, inc=1, device_id=across(r), device_id_type=MESH)

    def tell(r):
        pl.semaphore_signal(
            round_sem.at[r], inc=1, device_id=across(r), device_id_type=MESH
        )

    def hear(r):
        pl.semaphore_wait(round_sem.at[r], 1)

    def fill(y, carry):
        for z in range(4):
            put(wide, z + 1, y + 1, own[z, y])
        return carry

    for side, has in ((0, gz == 0), (1, gz == depth - 1)):
        @pl.when(has)
        def _():
            zeros = jnp.zeros(fz.shape[1:], fz.dtype)
            fz[side] = zeros
            hz[side] = zeros
            for s in range(2):
                fy[s, 5 * side] = jnp.zeros(fy.shape[2:], fy.dtype)
                hy[s, 5 * side] = jnp.zeros(fy.shape[2:], fy.dtype)

    for side, has in ((0, xy == 0), (1, xy == height - 1)):
        @pl.when(has)
        def _():
            fy[side] = jnp.zeros(fy.shape[1:], fy.dtype)
            hy[side] = jnp.zeros(fy.shape[1:], fy.dtype)

    beside_z = jnp.where(gz > 0, 1, 0) + jnp.where(gz < depth - 1, 1, 0)
    beside_y = jnp.where(xy > 0, 1, 0) + jnp.where(xy < height - 1, 1, 0)
    pl.semaphore_wait(barrier, (1 + beside_z) * (1 + beside_y) - 1 + ROUNDS)

    first = halo_copies(own, fz, fy, FEATURE_CHUNKS, 0, send_sem, recv_sem)
    then = halo_copies(hidden, hz, hy, HIDDEN_CHUNKS, PER_EXCHANGE, send_sem, recv_sem)
    for entry in first[8:] + first[:8]:
        start(entry)
    tell(0)
    count = lists_ref.shape[0]
    lists = lists_ref[...]
    sizes = jnp.sum(jnp.where(lists >= 0, 1, 0), axis=1, keepdims=True)
    column = lax.broadcasted_iota(jnp.int32, lists.shape, 1)
    facts[...] = jnp.where(column == 0, lists, sizes).astype(jnp.float32).T[0:8, :].astype(jnp.int32)
    facts_copy = pltpu.make_async_copy(facts, scalars, here_sem.at[2])
    facts_copy.start()
    for raw, w, channels in ((raw1, w1, 48), (raw2, w2, 64)):
        for dz in range(3):
            w[dz * channels : (dz + 1) * channels, :] = jnp.concatenate(
                [raw[dz * 9 + t] for t in range(9)], axis=1
            )
    lax.fori_loop(0, 20, fill, 0)
    hear(0)
    tell(1)

    def slab(ref, e, y):
        return ref[e, pl.ds(y, 3)].reshape(432, 256)

    def product(w, ref, e, y, low, high, channels):
        r = jnp.dot(
            w[low * channels : (high + 1) * channels, :],
            slab(ref, e, y),
            preferred_element_type=jnp.float32,
        )
        return {
            e - dz: r[(dz - low) * channels : (dz - low + 1) * channels]
            for dz in range(low, high + 1)
        }

    def inner(w, ref, y, channels):
        total = {}
        for e, low, high in ((1, 0, 1), (2, 0, 2), (3, 0, 2), (4, 1, 2)):
            for z, v in product(w, ref, e, y, low, high, channels).items():
                total[z] = total[z] + v if z in total else v
        return total

    for entry in first[8:]:
        arrive(entry)
    hear(1)
    tell(2)

    def fill_side(e, carry):
        put(wide, e, 0, fy[0, e])
        put(wide, e, 21, fy[1, e])
        return carry

    lax.fori_loop(0, 6, fill_side, 0)

    def bias_of(ref, channels):
        line = jnp.concatenate([ref[...], jnp.zeros((1, 128 - channels), jnp.float32)], axis=1)
        tall = jnp.broadcast_to(line, (128, 128)).T[0:channels]
        return jnp.concatenate([tall, tall], axis=1)

    bias1 = bias_of(b1, 48)
    bias2 = bias_of(b2, 64)

    def keep_hidden(z, y, total):
        value = jnp.maximum(total + bias1, 0.0).astype(jnp.bfloat16)
        hidden[z, y] = value
        put(hwide, z + 1, y + 1, value)

    labels_copy.wait()
    owner_copy.wait()
    facts_copy.wait()

    def look(b):
        at = scalars[0, b]
        run = at >> 8
        z = jnp.clip((run * 3277) >> 16, 0, 3)
        label = labels_ref[jnp.clip(run - z * 20, 0, 19), z, at & 255]
        rows_s[0, b] = owner_ref[label & (owner_ref.shape[0] - 1)]

    each = -(-count // 20)

    def first_inner(y, carry):
        for t in range(each):
            look(jnp.minimum(y * each + t, count - 1))
        total = inner(w1, wide, y, 48)
        part1[0, y] = total[0]
        part1[1, y] = total[3]
        keep_hidden(1, y, total[1])
        keep_hidden(2, y, total[2])
        return carry

    lax.fori_loop(0, 20, first_inner, 0, unroll=4)

    def fill_z(y, carry):
        put(wide, 0, y + 1, fz[0, y])
        put(wide, 5, y + 1, fz[1, y])
        return carry

    def first_outer(y, carry):
        keep_hidden(0, y, part1[0, y] + product(w1, wide, 0, y, 0, 0, 48)[0])
        keep_hidden(3, y, part1[1, y] + product(w1, wide, 5, y, 2, 2, 48)[3])
        return carry

    for c in range(4):
        arrive(first[2 * c])
        arrive(first[2 * c + 1])
        low, length = FEATURE_CHUNKS[c]
        lax.fori_loop(low, low + length, fill_z, 0, unroll=length)
        low, length = HIDDEN_CHUNKS[c]
        lax.fori_loop(low, low + length, first_outer, 0, unroll=length)
        if c == 0:
            for i in (9, 11, 13):
                start(then[i])
        if c == 3:
            for i in (8, 10, 12):
                start(then[i])
        start(then[2 * c])
        start(then[2 * c + 1])
        hear(2 + c)
        tell(3 + c)

    rows_copy = pltpu.make_async_copy(rows_s, rows_v, here_sem.at[3])
    rows_copy.start()
    rows_copy.wait()
    line8 = lax.broadcasted_iota(jnp.int32, (8, count), 0)
    three = jnp.where(line8 == 2, jnp.broadcast_to(rows_v[0:1, :], (8, count)), facts[...])
    turned3 = jnp.concatenate(
        [three.astype(jnp.float32), jnp.zeros((120, count), jnp.float32)], axis=0
    ).T.astype(jnp.int32)
    row_of = turned3[:, 2:3]
    code = (turned3[:, 0:1] << 15) + (turned3[:, 1:2] << 7) + (row_of & 127)
    hit = (row_of >> 7) == lax.broadcasted_iota(jnp.int32, (count, DEVS), 1)
    before = lax.broadcasted_iota(jnp.int32, (count, count), 0) > lax.broadcasted_iota(
        jnp.int32, (count, count), 1
    )
    rank = jnp.dot(
        jnp.where(before, 1.0, 0.0).astype(jnp.bfloat16),
        jnp.where(hit, 1.0, 0.0).astype(jnp.bfloat16),
        preferred_element_type=jnp.float32,
    )
    rank = jnp.where(hit, rank, -1.0)
    slots = [
        jnp.sum(jnp.where(rank == float(k), code, 0), axis=0, keepdims=True)
        for k in range(SLOTS)
    ]
    table_v[...] = jnp.concatenate(slots + [slots[0], slots[0]], axis=0)
    table_copy = pltpu.make_async_copy(table_v, table_ref, here_sem.at[4])
    table_copy.start()

    arrive(then[8])
    arrive(then[9])
    hear(6)

    def hidden_side(e, carry):
        put(hwide, e, 0, hy[0, e])
        put(hwide, e, 21, hy[1, e])
        return carry

    lax.fori_loop(1, 5, hidden_side, 0)

    def keep(z, y, total):
        value = (total + bias2).astype(jnp.bfloat16)
        group = (z * 20 + y) * 2
        emb_ref[group] = value[:, 0:128]
        emb_ref[group + 1] = value[:, 128:256]

    def second_inner(y, carry):
        total = inner(w2, hwide, y, 64)
        part2[0, y] = total[0]
        part2[1, y] = total[3]
        keep(1, y, total[1])
        keep(2, y, total[2])
        return carry

    lax.fori_loop(0, 20, second_inner, 0, unroll=4)

    def hidden_z(y, carry):
        put(hwide, 0, y + 1, hz[0, y])
        put(hwide, 5, y + 1, hz[1, y])
        return carry

    def second_outer(y, carry):
        keep(0, y, part2[0, y] + product(w2, hwide, 0, y, 0, 0, 64)[0])
        keep(3, y, part2[1, y] + product(w2, hwide, 5, y, 2, 2, 64)[3])
        return carry

    for entry in then[10:]:
        arrive(entry)
    hidden_side(0, 0)
    hidden_side(5, 0)
    for c in range(4):
        arrive(then[2 * c])
        arrive(then[2 * c + 1])
        low, length = HIDDEN_CHUNKS[c]
        lax.fori_loop(low, low + length, hidden_z, 0, unroll=length)
        low, length = LAST_CHUNKS[c]
        lax.fori_loop(low, low + length, second_outer, 0, unroll=length)

    table_copy.wait()

    def copy(k):
        device = partner(me, k)
        return pltpu.make_async_remote_copy(
            src_ref=send_ref.at[device],
            dst_ref=got_ref.at[me],
            send_sem=far_send.at[k],
            recv_sem=far_recv.at[k],
            device_id=place(device),
            device_id_type=MESH,
        )

    for k in range(AHEAD):
        moments_of(emb_ref, table_ref, partner(me, k), send_ref)
    own_copy = pltpu.make_async_copy(send_ref.at[me], got_ref.at[me], own_sem)
    own_copy.start()
    for k in range(1, AHEAD):
        copy(k).start()

    def send(i, carry):
        for t in range(AHEAD):
            moments_of(emb_ref, table_ref, partner(me, i * AHEAD + t), send_ref)
        for t in range(AHEAD):
            copy(i * AHEAD + t).start()
        return carry

    lax.fori_loop(1, DEVS // AHEAD, send, 0)
    for entry in first + then:
        leave(entry)

    def finish(k, carry):
        copy(k).wait()
        return carry

    lax.fori_loop(1, DEVS, finish, 0)
    own_copy.wait()


def main(features, first_weight, first_bias, second_weight, second_bias, labels, blocks, owner_map):
    own = features.transpose(1, 2, 0, 3)
    w1 = first_weight.reshape(27, 48, 48)
    w2 = second_weight.reshape(27, 64, 48)
    bf, f32, i32 = jnp.bfloat16, jnp.float32, jnp.int32
    count = blocks.shape[0]
    return pl.pallas_call(
        main_kernel,
        out_shape=jax.ShapeDtypeStruct((DEVS, ROWS, 128), bf),
        in_specs=[pl.BlockSpec(memory_space=pltpu.VMEM)] * 6
        + [pl.BlockSpec(memory_space=pl.ANY)] * 2,
        out_specs=pl.BlockSpec(memory_space=pl.ANY),
        scratch_shapes=[
            pltpu.VMEM((6, 22, 144, 256), bf),
            pltpu.VMEM((6, 22, 144, 256), bf),
            pltpu.VMEM((4, 20, 48, 256), bf),
            pltpu.VMEM((2, 20, 48, 256), bf),
            pltpu.VMEM((2, 6, 48, 256), bf),
            pltpu.VMEM((2, 20, 48, 256), bf),
            pltpu.VMEM((2, 6, 48, 256), bf),
            pltpu.VMEM((2, 20, 48, 256), f32),
            pltpu.VMEM((2, 20, 64, 256), f32),
            pltpu.VMEM((GROUPS, EMB, 128), bf),
            pltpu.VMEM((DEVS, ROWS, 128), bf),
            pltpu.SMEM(labels.shape, i32),
            pltpu.SMEM(owner_map.shape, i32),
            pltpu.VMEM((8, count), i32),
            pltpu.SMEM((8, count), i32),
            pltpu.SMEM((8, count), i32),
            pltpu.VMEM((8, count), i32),
            pltpu.VMEM((8, DEVS), i32),
            pltpu.SMEM((8, DEVS), i32),
            pltpu.SemaphoreType.DMA((2 * PER_EXCHANGE,)),
            pltpu.SemaphoreType.DMA((2 * PER_EXCHANGE,)),
            pltpu.SemaphoreType.DMA((DEVS,)),
            pltpu.SemaphoreType.DMA((DEVS,)),
            pltpu.SemaphoreType.DMA,
            pltpu.SemaphoreType.DMA((5,)),
            pltpu.SemaphoreType.REGULAR((ROUNDS,)),
            pltpu.VMEM((144, 432), bf),
            pltpu.VMEM((192, 432), bf),
        ],
        compiler_params=pltpu.CompilerParams(
            collective_id=0, has_side_effects=True, vmem_limit_bytes=52 << 20
        ),
    )(own, w1, first_bias[None], w2, second_bias[None], blocks, labels, owner_map)


def place(device):
    return (device // 32, lax.rem(device, 32))


def partner(me, k):
    core, x, y, z = lax.rem(me, 2), lax.rem(me // 2, 4), lax.rem(me // 8, 4), me // 32
    kc, kx, ky, kz = k // 64, lax.rem(k, 4), lax.rem(k // 4, 4), lax.rem(k // 16, 4)
    ky = lax.rem(ky + kx, 4)
    kz = lax.rem(kz + kx + ky, 4)
    there = (lax.rem(z + kz, 4) * 4 + lax.rem(y + ky, 4)) * 4 + lax.rem(x + kx, 4)
    return there * 2 + lax.rem(core + kc, 2)


def moments_of(emb_ref, table_ref, device, send_ref):
    lane = lax.broadcasted_iota(jnp.int32, (1, 128), 1)
    inner = lax.broadcasted_iota(jnp.int32, (HALF, 128), 1) & 63
    outer = lax.broadcasted_iota(jnp.int32, (HALF, 128), 0)
    upper = (inner >= HALF) | (inner >= outer)
    diagonal = inner == outer
    line = lax.broadcasted_iota(jnp.int32, (16, 128), 0)
    one = jnp.ones((EMB, 256), jnp.bfloat16)
    near = lax.broadcasted_iota(jnp.int32, (EMB, 128), 1) < EMB
    extras = jnp.zeros((16, 128), jnp.float32)
    for p in range(PAIRS):
        parts, sizes, rows = [], [], []
        for h in range(2):
            code = table_ref[2 * p + h, device]
            start = code >> 15
            size = (code >> 7) & 255
            rows.append((code & 127).astype(jnp.float32))
            sizes.append(size.astype(jnp.float32))
            group = jnp.clip(start >> 7, 0, GROUPS - 1)
            low = start & 127
            first = emb_ref[group]
            second = emb_ref[jnp.minimum(group + 1, GROUPS - 1)]
            in_first = jnp.where((lane >= low) & (lane < low + size), 1.0, 0.0).astype(jnp.bfloat16)
            in_second = jnp.where(lane + 128 < low + size, 1.0, 0.0).astype(jnp.bfloat16)
            mask_rows = jnp.broadcast_to(jnp.concatenate([in_first, in_second], axis=1), (16, 256))
            whole = jnp.concatenate([first, second], axis=1)
            left = jnp.concatenate([jnp.concatenate([first * in_first, second * in_second], axis=1), mask_rows], axis=0)
            right = jnp.concatenate([whole, one] if h == 0 else [one, whole], axis=0)
            parts.append(lax.dot_general(left, right, (((1,), (1,)), ((), ())), preferred_element_type=jnp.float32))
        size_row = jnp.where(lane < EMB, sizes[0], sizes[1])
        owner_row = jnp.where(lane < EMB, rows[0], rows[1])
        second_row = jnp.where(near[0:1], parts[0][EMB : EMB + 1], parts[1][EMB : EMB + 1])
        mean = second_row / jnp.maximum(size_row, 1.0)
        square = jnp.where(near, parts[0][0:EMB], parts[1][0:EMB])
        column = pltpu.roll(jnp.where(near, parts[1][0:EMB], parts[0][0:EMB]), EMB, 1)
        centred = square - column * mean
        rolled = pltpu.roll(centred[HALF:EMB], 96, 1)
        packed = jnp.where(upper, centred[0:HALF], rolled)
        send_ref[device, p * HALF : (p + 1) * HALF, :] = packed.astype(jnp.bfloat16)
        diag = jnp.sum(jnp.where(diagonal, rolled, 0.0), axis=0, keepdims=True)
        high = mean.astype(jnp.bfloat16).astype(jnp.float32)
        for place_of, value in (
            (p, diag),
            (3 + p, high),
            (6 + p, mean - high),
            (9 + p, size_row),
            (12 + p, owner_row),
        ):
            extras = jnp.where(line == place_of, value, extras)
    send_ref[device, BODY:ROWS, :] = extras.astype(jnp.bfloat16)


CHUNKS = 4
QUAD = 4


def total_kernel(
    got_ref, mean_ref, cov_ref, body, extra, lines, acc_a, acc_b, id_vec, ids, hits, spread,
    second, full, body_sem, extra_sem, id_sem,
):
    fast = lax.Precision.HIGHEST
    per = DEVS // CHUNKS
    extra_copy = pltpu.make_async_copy(got_ref.at[:, pl.ds(BODY, 16), :], extra, extra_sem)
    extra_copy.start()
    body_copies = [
        pltpu.make_async_copy(
            got_ref.at[pl.ds(c * per, per), pl.ds(0, BODY), :],
            body.at[pl.ds(c * per, per)],
            body_sem.at[c],
        )
        for c in range(CHUNKS)
    ]
    for one in body_copies:
        one.start()
    acc_a[...] = jnp.zeros_like(acc_a)
    acc_b[...] = jnp.zeros_like(acc_b)
    extra_copy.wait()
    lines[...] = extra[...].astype(jnp.float32).reshape(DEVS * 16, 128)

    def line(k):
        return lines[pl.ds(k, DEVS, stride=16), :]

    lane = lax.broadcasted_iota(jnp.int32, (DEVS, 128), 1)
    row = lax.broadcasted_iota(jnp.int32, (DEVS, 128), 0)
    inner = lane & 63
    owners = [line(12 + p) for p in range(PAIRS)]
    id_vec[...] = jnp.where(
        inner == 0, owners[0], jnp.where(inner == 1, owners[1], owners[2])
    ).astype(jnp.int32)
    id_copy = pltpu.make_async_copy(id_vec, ids, id_sem)
    id_copy.start()

    means, sizes = [], []
    sums = jnp.zeros((DEVS, 384), jnp.float32)
    for p in range(PAIRS):
        mean = line(3 + p) + line(6 + p)
        size = line(9 + p)
        means.append(mean)
        sizes.append(size)
        turned = owners[p].T
        for h in range(2):
            hit = jnp.where(row == turned[64 * h : 64 * h + 1, :].astype(jnp.int32), 1.0, 0.0)
            hits[:, (2 * p + h) * 128 : (2 * p + h + 1) * 128] = hit
            mine = (lane >= EMB) if h else (lane < EMB)
            values = jnp.concatenate(
                [
                    jnp.where(mine, size * mean, 0.0),
                    jnp.where(mine, size, 0.0),
                    jnp.where(mine, line(p), 0.0),
                ],
                axis=1,
            )
            sums = sums + jnp.dot(
                hit, values, preferred_element_type=jnp.float32, precision=fast
            )

    def folded(value):
        return value + pltpu.roll(value, EMB, 1)

    count = jnp.maximum(folded(sums[:, 128:256]), 1.0)
    total_mean = folded(sums[:, 0:128]) / count
    mean_ref[...] = total_mean.T[0:EMB]
    diag_sum = folded(sums[:, 256:384])
    inverse = 1.0 / count
    lines[0:DEVS, :] = diag_sum
    lines[DEVS : 2 * DEVS, :] = inverse

    for p in range(PAIRS):
        for h in range(2):
            owner = owners[p]
            other = pltpu.roll(owner, EMB, 1)
            owner_all = (
                jnp.where(lane < EMB, other, owner) if h else jnp.where(lane < EMB, owner, other)
            )
            hit_t = jnp.where(owner_all.astype(jnp.int32) == lane, 1.0, 0.0)
            theirs = jnp.dot(
                hit_t, total_mean, preferred_element_type=jnp.float32, precision=fast
            )
            off = jnp.sqrt(sizes[p]) * (means[p] - theirs)
            if h:
                off = pltpu.roll(off, EMB, 1)
            off = jnp.where(lane < EMB, off, 0.0)
            k = 2 * p + h
            second[k * 128 : (k + 1) * 128, :] = off.astype(jnp.bfloat16)
            spread[:, k * 128 : (k + 1) * 128] = off.T[0:EMB, :].astype(jnp.bfloat16)

    id_copy.wait()
    for c in range(CHUNKS):
        body_copies[c].wait()

        def add(s, carry):
            for p in range(PAIRS):
                value = body[s, p * HALF : (p + 1) * HALF, :].astype(jnp.float32)
                a = ids[s, p]
                b = ids[s, 64 + p]
                acc_a[a] = acc_a[a] + value
                acc_b[b] = acc_b[b] + value
            return carry

        lax.fori_loop(c * per, (c + 1) * per, add, 0, unroll=4)

    lane32 = lax.broadcasted_iota(jnp.int32, (HALF, 128), 1)
    row32 = lax.broadcasted_iota(jnp.int32, (HALF, 128), 0)

    def quad(q, carry):
        base = q * QUAD
        left = []
        for t in range(QUAD):
            mask = hits[pl.ds(base + t, 1), :].astype(jnp.bfloat16)
            left.append(spread[...] * mask)
        between = jnp.dot(
            jnp.concatenate(left, axis=0), second[...], preferred_element_type=jnp.float32
        )
        packed = [
            acc_a[base + t] + pltpu.roll(acc_b[base + t], EMB, 1) for t in range(QUAD)
        ]
        turned = jnp.concatenate(packed, axis=0).T[0:EMB]
        for t in range(QUAD):
            diag = lines[pl.ds(base + t, 1), :]
            inv = lines[pl.ds(DEVS + base + t, 1), :]
            flip = pltpu.roll(turned, (128 - HALF * t) % 128, 1) if t else turned
            flip_up, flip_down = flip[0:HALF], flip[HALF:EMB]
            here = packed[t]
            top = jnp.where((lane32 >= HALF) | (lane32 >= row32), here, flip_up)
            low = jnp.where(
                lane32 < row32, here, jnp.where(lane32 == row32, diag, flip_up)
            )
            bottom = jnp.where(lane32 < HALF, flip_down, pltpu.roll(low, HALF, 1))
            both = jnp.concatenate([top, bottom], axis=0)
            both = (both + between[t * EMB : (t + 1) * EMB]) * inv
            full[pl.ds((base + t) * EMB, EMB), :] = both
        return carry

    lax.fori_loop(0, SV_DEV // QUAD, quad, 0, unroll=2)

    for t in range(EMB // 2):
        even = full[pl.ds(2 * t, SV_DEV, stride=EMB), :]
        odd = full[pl.ds(2 * t + 1, SV_DEV, stride=EMB), :]
        cov_ref[:, t * 128 : (t + 1) * 128] = jnp.where(
            lane < EMB, even, pltpu.roll(odd, EMB, 1)
        )


def totals(got):
    return pl.pallas_call(
        total_kernel,
        out_shape=(
            jax.ShapeDtypeStruct((EMB, SV_DEV), jnp.float32),
            jax.ShapeDtypeStruct((SV_DEV, EMB * EMB), jnp.float32),
        ),
        in_specs=[pl.BlockSpec(memory_space=pl.ANY)],
        out_specs=(
            pl.BlockSpec(memory_space=pltpu.VMEM),
            pl.BlockSpec(memory_space=pltpu.VMEM),
        ),
        scratch_shapes=[
            pltpu.VMEM((DEVS, BODY, 128), jnp.bfloat16),
            pltpu.VMEM((DEVS, 16, 128), jnp.bfloat16),
            pltpu.VMEM((DEVS * 16, 128), jnp.float32),
            pltpu.VMEM((SV_DEV, HALF, 128), jnp.float32),
            pltpu.VMEM((SV_DEV, HALF, 128), jnp.float32),
            pltpu.VMEM((DEVS, 128), jnp.int32),
            pltpu.SMEM((DEVS, 128), jnp.int32),
            pltpu.VMEM((SV_DEV, DEVS * SLOTS), jnp.float32),
            pltpu.VMEM((EMB, DEVS * SLOTS), jnp.bfloat16),
            pltpu.VMEM((DEVS * SLOTS, 128), jnp.bfloat16),
            pltpu.VMEM((SV_DEV * EMB, 128), jnp.float32),
            pltpu.SemaphoreType.DMA((CHUNKS,)),
            pltpu.SemaphoreType.DMA,
            pltpu.SemaphoreType.DMA,
        ],
        compiler_params=pltpu.CompilerParams(vmem_limit_bytes=60 << 20),
    )(got)


def local(
    features, first_weight, first_bias, second_weight, second_bias, labels, blocks, owner_map
):
    got = main(
        features,
        first_weight,
        first_bias,
        second_weight,
        second_bias,
        labels.transpose(1, 0, 2),
        blocks.reshape(blocks.shape[2], blocks.shape[3]),
        owner_map,
    )
    mean, covariance = totals(got)
    return mean.T, covariance


def solution(mesh):
    return jax.shard_map(
        local,
        mesh=mesh,
        in_specs=(
            P(None, "gz", "xy", None),
            P(),
            P(),
            P(),
            P(),
            P("gz", "xy", None),
            P("gz", "xy", None, None),
            P(),
        ),
        out_specs=(P(("gz", "xy"), None), P(("gz", "xy"), None)),
        check_vma=False,
    )
```
